32 devices in a mesh: dp: 8 (over z, y), head: 4 (over x, core).
Axes of the slice: x: 2, y: 2, z: 4, core: 2. Of those that a mesh axis runs over, the one named last changes fastest.
Arguments:
- tokens: bfloat16 [2, 4096, 2048], P(None, ('dp', 'head')), may hold values from -6 to 6
- out_grad: bfloat16 [2, 4096, 2048], P(None, ('dp', 'head')), may hold values from -6 to 6
- seq_lengths: int32 [2, 4], replicated, may hold values from 1 to 3584, as said below
- attn_norm: float32 [2048], replicated, may hold values from 0.5 to 1.5
- query_proj: bfloat16 [2048, 2048], P('dp', 'head'), may hold values from -0.125 to 0.125
- key_proj: bfloat16 [2048, 2048], P('dp', 'head'), may hold values from -0.125 to 0.125
- value_proj: bfloat16 [2048, 4096], P('dp', 'head'), may hold values from -0.125 to 0.125
- gate_proj: bfloat16 [2048, 4096], P('dp', 'head'), may hold values from -0.125 to 0.125
- decay_proj: bfloat16 [2048, 16], P('dp', 'head'), may hold values from -0.125 to 0.125
- beta_proj: bfloat16 [2048, 16], P('dp', 'head'), may hold values from -0.125 to 0.125
- conv_query: float32 [4, 2048], replicated, may hold values from -3 to 3
- conv_key: float32 [4, 2048], replicated, may hold values from -3 to 3
- conv_value: float32 [4, 4096], replicated, may hold values from -3 to 3
- log_rate: float32 [16], replicated, may hold values from -0.7 to 0.7
- step_bias: float32 [16], replicated, may hold values from -15 to -2
- head_norm: float32 [256], replicated, may hold values from 0.5 to 1.5
- out_proj: bfloat16 [4096, 2048], P('head', 'dp'), may hold values from -0.1875 to 0.1875
- ffn_norm: float32 [2048], replicated, may hold values from 0.5 to 1.5
- ffn_gate: bfloat16 [2048, 5632], P('dp', 'head'), may hold values from -0.125 to 0.125
- ffn_up: bfloat16 [2048, 5632], P('dp', 'head'), may hold values from -0.125 to 0.125
- ffn_down: bfloat16 [5632, 2048], P('head', 'dp'), may hold values from -0.15625 to 0.15625
Outputs:
- block_out: bfloat16 [2, 4096, 2048], P(None, ('dp', 'head'))
- tokens_grad: float32 [2, 4096, 2048], P(None, ('dp', 'head'))
- attn_norm_grad: float32 [2048], replicated
- query_proj_grad: float32 [2048, 2048], P('dp', 'head')
- key_proj_grad: float32 [2048, 2048], P('dp', 'head')
- value_proj_grad: float32 [2048, 4096], P('dp', 'head')
- gate_proj_grad: float32 [2048, 4096], P('dp', 'head')
- decay_proj_grad: float32 [2048, 16], P('dp', 'head')
- beta_proj_grad: float32 [2048, 16], P('dp', 'head')
- conv_query_grad: float32 [4, 2048], replicated
- conv_key_grad: float32 [4, 2048], replicated
- conv_value_grad: float32 [4, 4096], replicated
- log_rate_grad: float32 [16], replicated
- step_bias_grad: float32 [16], replicated
- head_norm_grad: float32 [256], replicated
- out_proj_grad: float32 [4096, 2048], P('head', 'dp')
- ffn_norm_grad: float32 [2048], replicated
- ffn_gate_grad: float32 [2048, 5632], P('dp', 'head')
- ffn_up_grad: float32 [2048, 5632], P('dp', 'head')
- ffn_down_grad: float32 [5632, 2048], P('head', 'dp')
The draws below stay inside these ranges and needn't reach their ends.
Inputs may be any that keep to these rules, and one draw needn't show every extreme that they name: `seq_lengths`: each micro-batch packs 4 sequences end to end with lengths summing to 4096; the second sequence has exactly (7) * 512 tokens and starts within the first 512 tokens, the others are shorter than 512.
All inputs are finite; a program needn't handle non-finite values.
Results may differ from the reference program's by a relative error of at most 0.018.
Values may be sent and summed in bfloat16 or wider, within the bound.
No kernel may reach another device: no remote copies, remote signals or barrier semaphores. Data moves between devices by JAX's collectives and lax.ppermute only.
A program may use at most 384 MiB of HBM per device.

```python
import jax
import jax.numpy as jnp
from jax import lax

D = 2048
HEADS = 16
DV = 256
FF = 5632
GROUP = 64
KCONV = 4
MB = 2
ROWS = 512
TOKENS = 4096
QKD = 2048
VD = 4096
N_DP = 8


def draw_seq_lengths(key, part):
    key = jax.random.fold_in(key, 11)
    columns = []
    long_len = (N_DP - 1) * ROWS
    for micro_index in range(MB):
        subkeys = jax.random.split(jax.random.fold_in(key, micro_index), 2)
        head_len = jax.random.randint(subkeys[0], (), 1, ROWS - 1)
        remainder = ROWS - head_len
        middle_len = jax.random.randint(subkeys[1], (), 1, remainder)
        columns.append(jnp.stack([head_len, jnp.int32(long_len) + 0 * head_len, middle_len, remainder - middle_len]))
    return jnp.stack(columns).astype(jnp.int32)


def levels(own_key, shape, cuts, smallest, high):
    gain = 1.0
    for axis_at, shards_of in cuts:
        heights = jax.random.uniform(jax.random.fold_in(jax.random.fold_in(own_key, 6), axis_at), (shards_of,), jnp.float32, smallest / len(cuts), high / len(cuts))
        gain = gain * jnp.repeat(jnp.exp(heights), shape[axis_at] // shards_of).reshape((-1,) + (1,) * (len(shape) - 1 - axis_at))
    return gain


def gaussian(own_key, dims, scale, reach, cuts=(), kind=jnp.bfloat16):
    gain = levels(own_key, dims, cuts, -0.22, 0.18) if cuts else 1.0
    entries = jax.random.normal(own_key, dims, jnp.float32) * scale * gain
    return jnp.minimum(jnp.maximum(entries, -reach), reach).astype(kind)


def setup_inputs(seed: int = 0) -> dict:
    arg_keys = jax.random.split(jax.random.key(seed), 22)
    return {
        "tokens": gaussian(arg_keys[0], (MB, TOKENS, D), 1.0, 6.0, ((1, 32),)),
        "out_grad": gaussian(arg_keys[1], (MB, TOKENS, D), 1.0, 6.0, ((1, 32),)),
        "seq_lengths": draw_seq_lengths(jax.random.fold_in(arg_keys[21], 71), 0),
        "attn_norm": jnp.clip(1.0 + 0.1 * jax.random.normal(arg_keys[3], (D,), jnp.float32), 0.5, 1.5),
        "query_proj": gaussian(arg_keys[4], (D, QKD), D ** -0.5, 0.125, ((0, 8), (1, 4))),
        "key_proj": gaussian(arg_keys[5], (D, QKD), D ** -0.5, 0.125, ((0, 8), (1, 4))),
        "value_proj": gaussian(arg_keys[6], (D, VD), D ** -0.5, 0.125, ((0, 8), (1, 4))),
        "gate_proj": gaussian(arg_keys[7], (D, VD), D ** -0.5, 0.125, ((0, 8), (1, 4))),
        "decay_proj": gaussian(arg_keys[8], (D, HEADS), D ** -0.5, 0.125, ((0, 8), (1, 4))),
        "beta_proj": gaussian(arg_keys[9], (D, HEADS), D ** -0.5, 0.125, ((0, 8), (1, 4))),
        "conv_query": gaussian(arg_keys[10], (KCONV, QKD), 0.5, 3.0, (), jnp.float32),
        "conv_key": gaussian(arg_keys[11], (KCONV, QKD), 0.5, 3.0, (), jnp.float32),
        "conv_value": gaussian(arg_keys[12], (KCONV, VD), 0.5, 3.0, (), jnp.float32),
        "log_rate": jnp.clip(jax.random.uniform(arg_keys[13], (HEADS,), jnp.float32, -0.7, 0.7), -0.7, 0.7),
        "step_bias": jnp.clip(jax.random.uniform(arg_keys[14], (HEADS,), jnp.float32, -15.0, -2.0), -15.0, -2.0),
        "head_norm": jnp.clip(1.0 + 0.1 * jax.random.normal(arg_keys[15], (DV,), jnp.float32), 0.5, 1.5),
        "out_proj": gaussian(arg_keys[16], (VD, D), (VD // 4) ** -0.5, 0.1875, ((0, 4), (1, 8))),
        "ffn_norm": jnp.clip(1.0 + 0.1 * jax.random.normal(arg_keys[17], (D,), jnp.float32), 0.5, 1.5),
        "ffn_gate": gaussian(arg_keys[18], (D, FF), D ** -0.5, 0.125, ((0, 8), (1, 4))),
        "ffn_up": gaussian(arg_keys[19], (D, FF), D ** -0.5, 0.125, ((0, 8), (1, 4))),
        "ffn_down": gaussian(arg_keys[20], (FF, D), (FF // 4) ** -0.5, 0.15625, ((0, 4), (1, 8))),
    }


EPSILON = 1e-06
HEAD_FLOOR = 0.01
FULL_PRECISION = lax.Precision.HIGHEST

@jax.custom_vjp
def low(v):
    return lax.optimization_barrier(v.astype(jnp.bfloat16)).astype(jnp.float32)

@jax.custom_vjp
def low_back(v):
    return v

def low_keep(v):
    return (low(v), None)

def low_pass(kept, grad):
    return (grad,)

def back_keep(v):
    return (v, None)

def back_low(kept, grad):
    return (low(grad),)
low.defvjp(low_keep, low_pass)
low_back.defvjp(back_keep, back_low)

def matmul(left, right):
    return jnp.dot(left.astype(jnp.float32), right.astype(jnp.float32), precision=FULL_PRECISION, preferred_element_type=jnp.float32)

def seq_offsets(lengths, first_row, row_count):
    seq_ends = jnp.cumsum(lengths).astype(jnp.int32)
    starts = seq_ends - lengths
    places = first_row + lax.iota(jnp.int32, row_count)
    begun_at = jnp.where(starts[None, :] <= places[:, None], starts[None, :], 0)
    return places - lax.optimization_barrier(jnp.max(begun_at, axis=1))

def group_step(carried_state, block):
    query_rows, keys_now, values, beta_rows, decays, opening = block
    span_len = query_rows.shape[1]
    key_length = keys_now.shape[2]
    segment = jnp.cumsum(opening)
    untouched = (segment < 0.5).astype(jnp.float32)
    cumulative = jnp.cumsum(decays, axis=-1)
    row_ids = lax.broadcasted_iota(jnp.int32, (span_len, span_len), 0)
    col_ids = lax.broadcasted_iota(jnp.int32, (span_len, span_len), 1)
    same_seg = segment[:, None] == segment[None, :]
    inclusive = jnp.logical_and(row_ids >= col_ids, same_seg)
    strictly = jnp.logical_and(row_ids > col_ids, same_seg)
    spread = cumulative[:, :, None] - cumulative[:, None, :]
    pair_decay = jnp.where(inclusive, jnp.exp(jnp.where(inclusive, spread, 0.0)), 0.0)
    key_gram = jnp.einsum('hik,hjk->hij', keys_now, keys_now, precision=FULL_PRECISION)
    coupling = jnp.where(strictly, beta_rows[:, :, None] * pair_decay * key_gram, 0.0)
    system = coupling + jnp.eye(span_len, dtype=jnp.float32)
    incoming_carry = jnp.exp(cumulative) * untouched
    targets = jnp.concatenate([(beta_rows * incoming_carry)[:, :, None] * keys_now, beta_rows[:, :, None] * values], axis=2)
    solved_system = lax.linalg.triangular_solve(system, targets, left_side=True, lower=True, unit_diagonal=True)
    written_values = solved_system[:, :, key_length:] - jnp.einsum('dyj,djs->dys', solved_system[:, :, :key_length], carried_state, precision=FULL_PRECISION)
    attend = jnp.einsum('hik,hjk->hij', query_rows, keys_now, precision=FULL_PRECISION) * pair_decay
    output_rows = incoming_carry[:, :, None] * jnp.einsum('dyj,djs->dys', query_rows, carried_state, precision=FULL_PRECISION)
    output_rows = output_rows + jnp.einsum('hij,hjv->hiv', attend, written_values, precision=FULL_PRECISION)
    key_rows_weighted = pair_decay[:, -1, :, None] * keys_now
    updated_state = incoming_carry[:, -1, None, None] * carried_state + jnp.einsum('sdm,sdw->smw', key_rows_weighted, written_values, precision=FULL_PRECISION)
    return (updated_state, output_rows)

def run_chain(query_rows, keys_now, values, beta_rows, decays, opening, initial):
    block_count = query_rows.shape[0] // GROUP

    def blocked(source):
        shaped = source.reshape((block_count, GROUP) + source.shape[1:])
        return jnp.moveaxis(shaped, 1, 2)
    blocks = (blocked(query_rows), blocked(keys_now), blocked(values), blocked(beta_rows), blocked(decays), opening.reshape(block_count, GROUP))
    final_state, output_rows = lax.scan(jax.checkpoint(group_step), initial, blocks)
    output_rows = jnp.moveaxis(output_rows, 2, 1)
    output_rows = output_rows.reshape((block_count * GROUP, output_rows.shape[2], output_rows.shape[3]))
    return (output_rows, final_state)

def layer(params, residual, offsets):
    attn_norm, query_proj, key_proj, value_proj, gate_proj, decay_proj, beta_proj, conv_query, conv_key, conv_value, log_rate, step_bias, head_norm, out_proj, ffn_norm, ffn_gate, ffn_up, ffn_down = params
    row_count = residual.shape[0]
    head_count = log_rate.shape[0]
    key_length = query_proj.shape[1] // head_count
    value_size = value_proj.shape[1] // head_count
    qk_width = head_count * key_length
    scale_one = lax.rsqrt(lax.optimization_barrier(jnp.mean(residual * residual, axis=-1, keepdims=True)) + EPSILON)
    normed = low(residual * scale_one * attn_norm)
    pre_conv = jnp.concatenate([matmul(normed, query_proj), matmul(normed, key_proj), matmul(normed, value_proj)], axis=1)
    pre_conv = low_back(low(pre_conv))
    conv_all = jnp.concatenate([conv_query, conv_key, conv_value], axis=1)
    conv_sum = conv_all[KCONV - 1] * pre_conv
    for lag_size in range(1, KCONV):
        shifted = jnp.concatenate([jnp.zeros((lag_size, pre_conv.shape[1]), jnp.float32), pre_conv[:row_count - lag_size]], axis=0)
        keep_lag = (offsets >= lag_size).astype(jnp.float32)
        conv_sum = conv_sum + conv_all[KCONV - 1 - lag_size] * shifted * keep_lag[:, None]
    active = jax.nn.silu(conv_sum)
    query_rows = active[:, :qk_width].reshape(row_count, head_count, key_length)
    keys_now = active[:, qk_width:2 * qk_width].reshape(row_count, head_count, key_length)
    values = active[:, 2 * qk_width:].reshape(row_count, head_count, value_size)
    query_rows = query_rows * lax.rsqrt(lax.optimization_barrier(jnp.sum(query_rows * query_rows, axis=-1, keepdims=True)) + EPSILON) * key_length ** (-0.5)
    keys_now = keys_now * lax.rsqrt(lax.optimization_barrier(jnp.sum(keys_now * keys_now, axis=-1, keepdims=True)) + EPSILON)
    decay_lin = low_back(jnp.concatenate([matmul(normed, decay_proj), matmul(normed, beta_proj)], axis=1))
    beta_rows = jax.nn.sigmoid(decay_lin[:, head_count:])
    decays = -jnp.exp(log_rate) * jax.nn.softplus(decay_lin[:, :head_count] + step_bias)
    opening = (offsets == 0).astype(jnp.float32)
    initial = jnp.zeros((head_count, key_length, value_size), jnp.float32)
    mixer_output, final_state = run_chain(query_rows, keys_now, values, beta_rows, decays, opening, initial)
    gate_lin = low_back(matmul(normed, gate_proj)).reshape(row_count, head_count, value_size)
    out_scale = lax.rsqrt(lax.optimization_barrier(jnp.mean(mixer_output * mixer_output, axis=-1, keepdims=True)) + HEAD_FLOOR)
    gated_out = low((mixer_output * out_scale * head_norm * jax.nn.silu(gate_lin)).reshape(row_count, head_count * value_size))
    after_mix = residual + low_back(matmul(gated_out, out_proj))
    scale_two = lax.rsqrt(lax.optimization_barrier(jnp.mean(after_mix * after_mix, axis=-1, keepdims=True)) + EPSILON)
    ffn_in = low(after_mix * scale_two * ffn_norm)
    gate_ffn = low_back(matmul(ffn_in, ffn_gate))
    up_ffn = low_back(matmul(ffn_in, ffn_up))
    hidden = low(jax.nn.silu(gate_ffn) * up_ffn)
    return after_mix + matmul(hidden, ffn_down)

def reference(tokens, out_grad, seq_lengths, attn_norm, query_proj, key_proj, value_proj, gate_proj, decay_proj, beta_proj, conv_query, conv_key, conv_value, log_rate, step_bias, head_norm, out_proj, ffn_norm, ffn_gate, ffn_up, ffn_down):
    params = tuple((weight.astype(jnp.float32) for weight in (attn_norm, query_proj, key_proj, value_proj, gate_proj, decay_proj, beta_proj, conv_query, conv_key, conv_value, log_rate, step_bias, head_norm, out_proj, ffn_norm, ffn_gate, ffn_up, ffn_down)))
    totals = None
    results = []
    input_grads = []
    for micro_index in range(MB):
        residual = tokens[micro_index].astype(jnp.float32)
        offsets = seq_offsets(seq_lengths[micro_index], 0, TOKENS)
        result, pull_back = jax.vjp(lambda weights, rows_in: layer(weights, rows_in, offsets), params, residual)
        weight_grads, input_grad = pull_back(out_grad[micro_index].astype(jnp.float32))
        totals = weight_grads if totals is None else jax.tree.map(jnp.add, totals, weight_grads)
        results.append(result.astype(jnp.bfloat16))
        input_grads.append(input_grad)
    return (jnp.stack(results), jnp.stack(input_grads), totals[0], totals[1], totals[2], totals[3], totals[4], totals[5], totals[6], totals[7], totals[8], totals[9], totals[10], totals[11], totals[12], totals[13], totals[14], totals[15], totals[16], totals[17])
```

```python
from functools import partial

import jax
import jax.numpy as jnp
from jax import lax
from jax.experimental import pallas as pl
from jax.experimental.pallas import tpu as pltpu
from jax.sharding import PartitionSpec as P

CHUNK = 128
KCONV = 4
LANES = 128
HALO = 16

EPSILON = 1e-06
HEAD_FLOOR = 0.01
F32 = jnp.float32
BF16 = jnp.bfloat16
NN = (((1,), (0,)), ((), ()))
NT = (((1,), (1,)), ((), ()))
TN = (((0,), (0,)), ((), ()))


def mm(left, right, dims=NN):
    return lax.dot_general(
        left.astype(BF16), right.astype(BF16), dims, preferred_element_type=F32
    )


def split(value):
    high = value.astype(BF16)
    return high, (value - high.astype(F32)).astype(BF16)


def mm3(left, right, dims=NN):
    left_high, left_low = split(left)
    right_high, right_low = split(right)
    return mm(left_high, right_high, dims) + (
        mm(left_high, right_low, dims) + mm(left_low, right_high, dims)
    )


def chunk_places(info_ref, micro, chunk, seq_count):
    first = info_ref[micro, seq_count] + chunk * CHUNK
    starts = [info_ref[micro, at] for at in range(seq_count)]
    rows = first + lax.broadcasted_iota(jnp.int32, (CHUNK, 1), 0)
    lanes = first + lax.broadcasted_iota(jnp.int32, (1, CHUNK), 1)
    seg_col = jnp.zeros((CHUNK, 1), jnp.int32)
    seg_row = jnp.zeros((1, CHUNK), jnp.int32)
    begun = jnp.zeros((CHUNK, 1), jnp.int32)
    seg_before = jnp.int32(0)
    seg_last = jnp.int32(0)
    for start in starts:
        seg_col = seg_col + jnp.where(rows >= start, 1, 0)
        seg_row = seg_row + jnp.where(lanes >= start, 1, 0)
        begun = jnp.maximum(begun, jnp.where(rows >= start, start, 0))
        seg_before = seg_before + jnp.where(first - 1 >= start, 1, 0)
        seg_last = seg_last + jnp.where(first + CHUNK - 1 >= start, 1, 0)
    offset = rows - begun
    row_ids = lax.broadcasted_iota(jnp.int32, (CHUNK, CHUNK), 0)
    col_ids = lax.broadcasted_iota(jnp.int32, (CHUNK, CHUNK), 1)
    same = seg_col == seg_row
    return dict(
        row_ids=row_ids,
        col_ids=col_ids,
        inclusive=jnp.logical_and(row_ids >= col_ids, same),
        strictly=jnp.logical_and(row_ids > col_ids, same),
        untouched=jnp.where(seg_col == seg_before, 1.0, 0.0).astype(F32),
        with_last=jnp.where(seg_col == seg_last, 1.0, 0.0).astype(F32),
        lags=[jnp.where(offset >= lag, 1.0, 0.0).astype(F32) for lag in range(1, KCONV)],
    )


def decay_parts(g_col, places):
    row_ids, col_ids = places["row_ids"], places["col_ids"]
    cum_row = jnp.sum(jnp.where(row_ids <= col_ids, g_col, 0.0), axis=0, keepdims=True)
    cum_col = jnp.sum(jnp.where(row_ids == col_ids, cum_row, 0.0), axis=1, keepdims=True)
    spread = jnp.where(places["inclusive"], cum_col - cum_row, 0.0)
    pair = jnp.where(places["inclusive"], jnp.exp(spread), 0.0)
    carry = jnp.exp(cum_col) * places["untouched"]
    cum_last = cum_col[CHUNK - 1 :, :]
    to_last = jnp.exp(jnp.minimum(cum_last - cum_col, 0.0)) * places["with_last"]
    return pair, carry, to_last, carry[CHUNK - 1 :, :]


def conv_rows(extended, taps, lags):
    total = taps[KCONV - 1 :, :] * extended[HALO:]
    for lag in range(1, KCONV):
        shifted = extended[HALO - lag : HALO - lag + CHUNK]
        total = total + taps[KCONV - 1 - lag : KCONV - lag, :] * shifted * lags[lag - 1]
    return total


def head_columns(head, heads, key_size, value_size):
    return (
        (head * key_size, key_size),
        ((heads + head) * key_size, key_size),
        (2 * heads * key_size + head * value_size, value_size),
    )


def unit_rows(active):
    return active * lax.rsqrt(jnp.sum(active * active, axis=1, keepdims=True) + EPSILON)


def softplus(value):
    return jnp.maximum(value, 0.0) + jnp.log1p(jnp.exp(-jnp.abs(value)))


def unit_lower_inverses(systems, places):
    row_ids, col_ids = places["row_ids"], places["col_ids"]
    eye = jnp.where(row_ids == col_ids, 1.0, 0.0).astype(F32)
    pairs = jnp.right_shift(row_ids, 1) == jnp.right_shift(col_ids, 1)
    found = [eye - jnp.where(pairs, system, 0.0) for system in systems]
    level = 1
    while (1 << level) < CHUNK:
        row_block = jnp.right_shift(row_ids, level)
        col_block = jnp.right_shift(col_ids, level)
        lower = jnp.logical_and(
            jnp.right_shift(row_block, 1) == jnp.right_shift(col_block, 1), row_block > col_block
        )
        inner = [
            INVERSE_MM(jnp.where(lower, system, 0.0), inverse)
            for system, inverse in zip(systems, found)
        ]
        found = [
            inverse - INVERSE_MM(inverse, middle) for inverse, middle in zip(found, inner)
        ]
        level += 1
    return found


INVERSE_MM = mm3


def mix_forward_kernel(
    info_ref,
    x_ref,
    rim_ref,
    dec_ref,
    taps_ref,
    par_ref,
    out_ref,
    cmap_ref,
    inv_ref,
    start_ref,
    final_ref,
    halo,
    state,
    *,
    heads,
    key_size,
    value_size,
    seq_count,
):
    micro, chunk = pl.program_id(0), pl.program_id(1)
    span = range(heads)

    @pl.when(chunk == 0)
    def _():
        halo[...] = rim_ref[0]
        row_ids = lax.broadcasted_iota(jnp.int32, (key_size, key_size), 0)
        col_ids = lax.broadcasted_iota(jnp.int32, (key_size, key_size), 1)
        eye = jnp.where(row_ids == col_ids, 1.0, 0.0).astype(F32)
        for head in span:
            state[head] = jnp.concatenate([jnp.zeros((key_size, value_size), F32), eye], axis=1)

    places = chunk_places(info_ref, micro, chunk, seq_count)
    dec = dec_ref[...]
    beta_all = jax.nn.sigmoid(dec)
    g_all = par_ref[0:1, :] * softplus(dec + par_ref[1:2, :])
    scale = key_size**-0.5

    queries, keys, values = [], [], []
    for head in span:
        rows = []
        for begin, width in head_columns(head, heads, key_size, value_size):
            cut = slice(begin, begin + width)
            extended = jnp.concatenate(
                [halo[:, cut].astype(F32), x_ref[:, cut].astype(F32)], axis=0
            )
            summed = conv_rows(extended, taps_ref[0:KCONV, cut], places["lags"])
            rows.append(summed * jax.nn.sigmoid(summed))
        queries.append(unit_rows(rows[0]) * scale)
        keys.append(unit_rows(rows[1]))
        values.append(rows[2])
    halo[...] = x_ref[CHUNK - HALO :, :]

    betas = [beta_all[:, heads + head : heads + head + 1] for head in span]
    decays = [decay_parts(g_all[:, head : head + 1], places) for head in span]
    grams = [mm(keys[head], keys[head], NT) for head in span]
    systems = [
        jnp.where(places["strictly"], betas[head] * decays[head][0] * grams[head], 0.0)
        for head in span
    ]
    inverses = unit_lower_inverses(systems, places)
    attends = [mm(queries[head], keys[head], NT) * decays[head][0] for head in span]
    solved = [
        mm(
            inverses[head],
            jnp.concatenate(
                [betas[head] * values[head], betas[head] * decays[head][1] * keys[head]], axis=1
            ),
        )
        for head in span
    ]
    starts = [state[head] for head in span]
    written = [
        jnp.concatenate(
            [solved[head][:, :value_size], jnp.zeros((CHUNK, key_size), F32)], axis=1
        )
        - mm(solved[head][:, value_size:], starts[head])
        for head in span
    ]
    outs = [
        decays[head][1] * mm(queries[head], starts[head]) + mm(attends[head], written[head])
        for head in span
    ]
    for head in span:
        _, _, to_last, carry_last = decays[head]
        inv_ref[0, head] = inverses[head].astype(BF16)
        start_ref[0, head] = starts[head].astype(BF16)
        out_ref[:, head * value_size : (head + 1) * value_size] = outs[head][:, :value_size]
        cmap_ref[:, head * key_size : (head + 1) * key_size] = outs[head][:, value_size:].astype(
            BF16
        )
        state[head] = carry_last * starts[head] + mm(to_last * keys[head], written[head], TN)

    @pl.when(chunk == pl.num_programs(1) - 1)
    def _():
        final_ref[0] = state[...]


def mix_backward_kernel(
    info_ref,
    x_ref,
    before_ref,
    rim_ref,
    dec_ref,
    taps_ref,
    par_ref,
    grad_ref,
    inv_ref,
    start_ref,
    incoming_ref,
    leaving_ref,
    dx_ref,
    rim_grad_ref,
    tail_ref,
    ddec_ref,
    dtaps_ref,
    dpar_ref,
    carry,
    dstate,
    *,
    heads,
    key_size,
    value_size,
    seq_count,
):
    micro, step = pl.program_id(0), pl.program_id(1)
    chunk = pl.num_programs(1) - 1 - step
    span = range(heads)

    @pl.when(step == 0)
    def _():
        carry[...] = jnp.zeros_like(carry)
        dstate[...] = leaving_ref[0].astype(F32)

    @pl.when(jnp.logical_and(micro == 0, step == 0))
    def _():
        dtaps_ref[...] = jnp.zeros_like(dtaps_ref)
        dpar_ref[...] = jnp.zeros_like(dpar_ref)

    places = chunk_places(info_ref, micro, chunk, seq_count)
    row_ids, col_ids = places["row_ids"], places["col_ids"]
    lags = places["lags"]
    dec = dec_ref[...]
    beta_all = jax.nn.sigmoid(dec)
    shifted_dec = dec + par_ref[1:2, :]
    g_all = par_ref[0:1, :] * softplus(shifted_dec)
    scale = key_size**-0.5
    opening = jnp.where(chunk == 0, rim_ref[0].astype(F32), before_ref[...].astype(F32))

    def extended_rows(cut):
        return jnp.concatenate([opening[:, cut], x_ref[:, cut].astype(F32)], axis=0)

    sums, norms, unit = [], [], []
    for head in span:
        mine = [
            conv_rows(extended_rows(slice(begin, begin + width)), taps_ref[0:KCONV, begin : begin + width], lags)
            for begin, width in head_columns(head, heads, key_size, value_size)
        ]
        active = [value * jax.nn.sigmoid(value) for value in mine]
        inverse_norms = [
            lax.rsqrt(jnp.sum(value * value, axis=1, keepdims=True) + EPSILON)
            for value in active[:2]
        ]
        sums.append(mine)
        norms.append(inverse_norms)
        unit.append([active[0] * inverse_norms[0], active[1] * inverse_norms[1], active[2]])
    keys = [unit[head][1] for head in span]
    key_low = [keys[head].astype(BF16) for head in span]
    query_low = [(unit[head][0] * scale).astype(BF16) for head in span]
    betas = [beta_all[:, heads + head : heads + head + 1] for head in span]
    decays = [decay_parts(g_all[:, head : head + 1], places) for head in span]
    grams = [mm(key_low[head], key_low[head], NT) for head in span]
    products = [mm(query_low[head], key_low[head], NT) for head in span]
    attends = [(products[head] * decays[head][0]).astype(BF16) for head in span]
    starts = []
    for head in span:
        saved = start_ref[0, head]
        starts.append(
            saved[:, :value_size].astype(F32)
            + mm(saved[:, value_size:], incoming_ref[0, head])
        )
    start_low = [starts[head].astype(BF16) for head in span]
    key_state = [mm(key_low[head], start_low[head]) for head in span]
    query_state = [mm(query_low[head], start_low[head]) for head in span]
    grads = [grad_ref[:, head * value_size : (head + 1) * value_size] for head in span]
    grad_low = [grads[head].astype(BF16) for head in span]
    residues = [unit[head][2] - decays[head][1] * key_state[head] for head in span]
    inverses = [inv_ref[0, head] for head in span]
    written = [mm(inverses[head], betas[head] * residues[head]).astype(BF16) for head in span]
    ahead = [dstate[head] for head in span]
    ahead_low = [ahead[head].astype(BF16) for head in span]
    key_last = [(decays[head][2] * keys[head]).astype(BF16) for head in span]
    dwritten = [
        mm(attends[head], grad_low[head], TN) + mm(key_last[head], ahead_low[head])
        for head in span
    ]
    dresidue = [mm(inverses[head], dwritten[head], TN) for head in span]
    dresidue_low = [dresidue[head].astype(BF16) for head in span]
    dattend = [
        jnp.where(places["inclusive"], mm(grad_low[head], written[head], NT), 0.0)
        for head in span
    ]
    dsystem = [
        jnp.where(places["strictly"], -mm(dresidue_low[head], written[head], NT), 0.0)
        for head in span
    ]
    dproducts = [(dattend[head] * decays[head][0]).astype(BF16) for head in span]
    dcarried = [decays[head][1] * grads[head] for head in span]
    dcarried_low = [dcarried[head].astype(BF16) for head in span]
    dkey_state = [-(betas[head] * decays[head][1]) * dresidue[head] for head in span]
    dkey_state_low = [dkey_state[head].astype(BF16) for head in span]
    dkey_last = [mm(written[head], ahead_low[head], NT) for head in span]
    dgram = [dsystem[head] * betas[head] * decays[head][0] for head in span]
    dgram_low = [dgram[head].astype(BF16) for head in span]
    dquery = [
        mm(dcarried_low[head], start_low[head], NT) + mm(dproducts[head], key_low[head])
        for head in span
    ]
    dkey = [
        mm(dproducts[head], query_low[head], TN)
        + decays[head][2] * dkey_last[head]
        + mm(dkey_state_low[head], start_low[head], NT)
        + mm(dgram_low[head], key_low[head])
        + mm(dgram_low[head], key_low[head], TN)
        for head in span
    ]
    lane_ids = lax.broadcasted_iota(jnp.int32, (CHUNK, LANES), 1)
    ddec = jnp.zeros((CHUNK, LANES), F32)
    dg_all = jnp.zeros((CHUNK, LANES), F32)
    for head in span:
        pair, carried, to_last, carry_last = decays[head]
        coupled = dsystem[head] * grams[head]
        dpair = (dattend[head] * products[head] + coupled * betas[head]) * pair
        dbeta = jnp.sum(coupled * pair, axis=1, keepdims=True) + jnp.sum(
            dresidue[head] * residues[head], axis=1, keepdims=True
        )
        dcarry = jnp.sum(
            grads[head] * query_state[head] - betas[head] * dresidue[head] * key_state[head],
            axis=1,
            keepdims=True,
        )
        dcarry_last = jnp.sum(
            jnp.sum(ahead[head] * starts[head], axis=1, keepdims=True), axis=0, keepdims=True
        )
        dto_last = jnp.sum(dkey_last[head] * keys[head], axis=1, keepdims=True) * to_last
        is_last = lax.broadcasted_iota(jnp.int32, (CHUNK, 1), 0) == CHUNK - 1
        dcum_col = (
            jnp.sum(dpair, axis=1, keepdims=True)
            + dcarry * carried
            - dto_last
            + jnp.where(
                is_last,
                dcarry_last * carry_last + jnp.sum(dto_last, axis=0, keepdims=True),
                0.0,
            )
        )
        dcum_row = jnp.sum(
            jnp.where(row_ids == col_ids, dcum_col, 0.0) - dpair, axis=0, keepdims=True
        )
        dg = jnp.sum(jnp.where(col_ids >= row_ids, dcum_row, 0.0), axis=1, keepdims=True)
        beta = betas[head]
        dg_all = jnp.where(lane_ids == head, dg, dg_all)
        ddec = jnp.where(lane_ids == heads + head, dbeta * beta * (1.0 - beta), ddec)
        dstate[head] = (
            carry_last * ahead[head]
            + mm(query_low[head], dcarried_low[head], TN)
            + mm(key_low[head], dkey_state_low[head], TN)
        )
    dstep = dg_all * par_ref[0:1, :] * jax.nn.sigmoid(shifted_dec)
    ddec = ddec + dstep
    ddec_ref[...] = ddec.astype(BF16)
    dpar_ref[0:1, :] += jnp.sum(dg_all * g_all, axis=0, keepdims=True)
    dpar_ref[1:2, :] += jnp.sum(dstep, axis=0, keepdims=True)

    edge = jnp.zeros((8, 1), F32)
    for head in span:
        dunit = [dquery[head] * scale, dkey[head]]
        dactive = [
            norms[head][at]
            * (
                dunit[at]
                - unit[head][at] * jnp.sum(dunit[at] * unit[head][at], axis=1, keepdims=True)
            )
            for at in range(2)
        ]
        dactive.append(betas[head] * dresidue[head])
        for at, (begin, width) in enumerate(head_columns(head, heads, key_size, value_size)):
            cut = slice(begin, begin + width)
            sig = jax.nn.sigmoid(sums[head][at])
            dsum = dactive[at] * sig * (1.0 + sums[head][at] * (1.0 - sig))
            extended = extended_rows(cut)
            taps = taps_ref[0:KCONV, cut]
            zeros = jnp.zeros((8, width), F32)
            dtaps_ref[KCONV - 1 : KCONV, cut] += jnp.sum(
                dsum * extended[HALO:], axis=0, keepdims=True
            )
            total = jnp.concatenate([zeros, taps[KCONV - 1 :, :] * dsum], axis=0)
            for lag in range(1, KCONV):
                masked = dsum * lags[lag - 1]
                at_tap = KCONV - 1 - lag
                dtaps_ref[at_tap : at_tap + 1, cut] += jnp.sum(
                    masked * extended[HALO - lag : HALO - lag + CHUNK], axis=0, keepdims=True
                )
                padded = jnp.concatenate(
                    [zeros, taps[at_tap : at_tap + 1, :] * masked, zeros], axis=0
                )
                total = total + padded[lag : lag + 8 + CHUNK]
            body_rows = jnp.concatenate(
                [total[8:CHUNK], total[CHUNK:] + carry[:, cut]], axis=0
            )
            dx_ref[:, cut] = body_rows.astype(BF16)
            carry[:, cut] = total[:8]

            @pl.when(step == 0)
            def _():
                tail_ref[0, :, cut] = body_rows[CHUNK - HALO :]

    @pl.when(chunk == 0)
    def _():
        rim_grad_ref[0] = carry[...]


def mix_sizes(pre_conv, micros, heads, key_size):
    rows = pre_conv.shape[0] // micros
    value_size = pre_conv.shape[1] // heads - 2 * key_size
    return rows, rows // CHUNK, value_size


def mix_forward(info, pre_conv, rim, dec, taps, par, micros, heads, key_size):
    rows, chunks, value_size = mix_sizes(pre_conv, micros, heads, key_size)
    width = pre_conv.shape[1]
    wide = value_size + key_size

    def by_rows(columns):
        return pl.BlockSpec((CHUNK, columns), lambda m, c: (m * chunks + c, 0))

    kernel = partial(
        mix_forward_kernel,
        heads=heads,
        key_size=key_size,
        value_size=value_size,
        seq_count=info.shape[1] - 1,
    )
    return pl.pallas_call(
        kernel,
        grid=(micros, chunks),
        in_specs=[
            pl.BlockSpec(memory_space=pltpu.SMEM),
            by_rows(width),
            pl.BlockSpec((1, HALO, width), lambda m, c: (m, 0, 0)),
            by_rows(LANES),
            pl.BlockSpec((8, width), lambda m, c: (0, 0)),
            pl.BlockSpec((8, LANES), lambda m, c: (0, 0)),
        ],
        out_specs=[
            by_rows(heads * value_size),
            by_rows(heads * key_size),
            pl.BlockSpec((1, heads, CHUNK, CHUNK), lambda m, c: (m * chunks + c, 0, 0, 0)),
            pl.BlockSpec((1, heads, key_size, wide), lambda m, c: (m * chunks + c, 0, 0, 0)),
            pl.BlockSpec((1, heads, key_size, wide), lambda m, c: (m, 0, 0, 0)),
        ],
        out_shape=[
            jax.ShapeDtypeStruct((micros * rows, heads * value_size), F32),
            jax.ShapeDtypeStruct((micros * rows, heads * key_size), BF16),
            jax.ShapeDtypeStruct((micros * chunks, heads, CHUNK, CHUNK), BF16),
            jax.ShapeDtypeStruct((micros * chunks, heads, key_size, wide), BF16),
            jax.ShapeDtypeStruct((micros, heads, key_size, wide), F32),
        ],
        scratch_shapes=[
            pltpu.VMEM((HALO, width), BF16),
            pltpu.VMEM((heads, key_size, wide), F32),
        ],
        compiler_params=pltpu.CompilerParams(
            dimension_semantics=("arbitrary", "arbitrary"), vmem_limit_bytes=VMEM_BYTES
        ),
        name="mix_forward",
    )(info, pre_conv, rim, dec, taps, par)


def mix_backward(
    info, pre_conv, rim, dec, taps, par, grad, inverses, starts, incoming, leaving, micros, heads, key_size
):
    rows, chunks, value_size = mix_sizes(pre_conv, micros, heads, key_size)
    width = pre_conv.shape[1]
    wide = value_size + key_size
    halo_blocks = CHUNK // HALO

    def at(m, s):
        return m * chunks + chunks - 1 - s

    def by_rows(columns):
        return pl.BlockSpec((CHUNK, columns), lambda m, s: (at(m, s), 0))

    kernel = partial(
        mix_backward_kernel,
        heads=heads,
        key_size=key_size,
        value_size=value_size,
        seq_count=info.shape[1] - 1,
    )
    return pl.pallas_call(
        kernel,
        grid=(micros, chunks),
        in_specs=[
            pl.BlockSpec(memory_space=pltpu.SMEM),
            by_rows(width),
            pl.BlockSpec(
                (HALO, width), lambda m, s: (jnp.maximum(at(m, s) * halo_blocks - 1, 0), 0)
            ),
            pl.BlockSpec((1, HALO, width), lambda m, s: (m, 0, 0)),
            by_rows(LANES),
            pl.BlockSpec((8, width), lambda m, s: (0, 0)),
            pl.BlockSpec((8, LANES), lambda m, s: (0, 0)),
            by_rows(heads * value_size),
            pl.BlockSpec((1, heads, CHUNK, CHUNK), lambda m, s: (at(m, s), 0, 0, 0)),
            pl.BlockSpec((1, heads, key_size, wide), lambda m, s: (at(m, s), 0, 0, 0)),
            pl.BlockSpec((1, heads, key_size, value_size), lambda m, s: (m, 0, 0, 0)),
            pl.BlockSpec((1, heads, key_size, value_size), lambda m, s: (m, 0, 0, 0)),
        ],
        out_specs=[
            by_rows(width),
            pl.BlockSpec((1, 8, width), lambda m, s: (m, 0, 0)),
            pl.BlockSpec((1, HALO, width), lambda m, s: (m, 0, 0)),
            by_rows(LANES),
            pl.BlockSpec((8, width), lambda m, s: (0, 0)),
            pl.BlockSpec((8, LANES), lambda m, s: (0, 0)),
        ],
        out_shape=[
            jax.ShapeDtypeStruct((micros * rows, width), BF16),
            jax.ShapeDtypeStruct((micros, 8, width), F32),
            jax.ShapeDtypeStruct((micros, HALO, width), F32),
            jax.ShapeDtypeStruct((micros * rows, LANES), BF16),
            jax.ShapeDtypeStruct((8, width), F32),
            jax.ShapeDtypeStruct((8, LANES), F32),
        ],
        scratch_shapes=[
            pltpu.VMEM((8, width), F32),
            pltpu.VMEM((heads, key_size, value_size), F32),
        ],
        compiler_params=pltpu.CompilerParams(
            dimension_semantics=("arbitrary", "arbitrary"), vmem_limit_bytes=VMEM_BYTES
        ),
        name="mix_backward",
    )(info, pre_conv, pre_conv, rim, dec, taps, par, grad, inverses, starts, incoming, leaving)


VMEM_BYTES = 48 * 1024 * 1024


def from_behind(value, axis, steps):
    count = lax.axis_size(axis)
    leading, last = (max(0, -steps), min(count, count - steps))
    return lax.ppermute(value, axis, [(source, source + steps) for source in range(leading, last)])


def head_gather(value):
    return lax.all_gather(value, "head", axis=1, tiled=True)


def head_scatter(value):
    return lax.psum_scatter(value, "head", scatter_dimension=1, tiled=True)


def scan_states(maps, sums, backward):
    count, mine = lax.axis_size("dp"), lax.axis_index("dp")
    packed = lax.all_gather(jnp.concatenate([maps, sums], axis=-1).astype(BF16), "dp")
    if backward:
        packed = packed[::-1]
        mine = count - 1 - mine
    key_size = maps.shape[-1]
    state = jnp.zeros(sums.shape, F32)
    for position in range(count - 1):
        block = packed[position]
        moved = jnp.einsum(
            "mhji,mhjv->mhiv" if backward else "mhij,mhjv->mhiv",
            block[..., :key_size],
            state.astype(BF16),
            preferred_element_type=F32,
        )
        state = jnp.where(position < mine, moved + block[..., key_size:].astype(F32), state)
    return state


def contract_rows(left, right):
    return lax.dot_general(left, right, TN, preferred_element_type=F32)


def contract_cols(left, right):
    return lax.dot_general(left, right, NT, preferred_element_type=F32)


def norm_backward(grad_in, normed_rows, scale):
    return scale * (grad_in - normed_rows * jnp.mean(grad_in * normed_rows, axis=-1, keepdims=True))


def dp_gather(value, axis):
    return lax.all_gather(value, "dp", axis=axis, tiled=True)


def dp_scatter(value, axis):
    return lax.psum_scatter(value.astype(BF16), "dp", scatter_dimension=axis, tiled=True).astype(F32)


def body(
    tokens,
    out_grad,
    seq_lengths,
    attn_norm,
    query_proj,
    key_proj,
    value_proj,
    gate_proj,
    decay_proj,
    beta_proj,
    conv_query,
    conv_key,
    conv_value,
    log_rate,
    step_bias,
    head_norm,
    out_proj,
    ffn_norm,
    ffn_gate,
    ffn_up,
    ffn_down,
):
    head_rank = lax.axis_index("head")
    heads = decay_proj.shape[1]
    qk_width = query_proj.shape[1]
    v_width = value_proj.shape[1]
    key_size = qk_width // heads
    value_size = v_width // heads
    ffn_width = ffn_gate.shape[1]
    conv_width = 2 * qk_width + v_width
    main_width = conv_width + v_width
    micros = tokens.shape[0]
    model = tokens.shape[2]

    decay_pad = jnp.zeros((decay_proj.shape[0], LANES - 2 * heads), decay_proj.dtype)
    w_in = dp_gather(
        jnp.concatenate(
            [query_proj, key_proj, value_proj, gate_proj, decay_proj, beta_proj, decay_pad], axis=1
        ),
        0,
    )
    w_out = dp_gather(out_proj, 1)
    w_ffn = dp_gather(jnp.concatenate([ffn_gate, ffn_up], axis=1), 0)
    w_down = dp_gather(ffn_down, 1)

    def of_mine(whole, width):
        return lax.dynamic_slice_in_dim(whole, head_rank * width, width, whole.ndim - 1)

    taps = jnp.concatenate(
        [of_mine(conv_query, qk_width), of_mine(conv_key, qk_width), of_mine(conv_value, v_width)],
        axis=1,
    )
    taps = jnp.pad(taps, ((0, 8 - KCONV), (0, 0)))
    par = jnp.pad(
        jnp.stack([-jnp.exp(of_mine(log_rate, heads)), of_mine(step_bias, heads)]),
        ((0, 6), (0, LANES - heads)),
    )

    residual = tokens.astype(F32)
    scale_one = lax.rsqrt(jnp.mean(residual * residual, axis=-1, keepdims=True) + EPSILON)
    normed_one = residual * scale_one
    normed_all = head_gather((normed_one * attn_norm).astype(BF16))
    cotangent_all = head_gather(out_grad)
    block_rows = normed_all.shape[1]
    normed_all = normed_all.reshape(micros * block_rows, model)
    cotangent_all = cotangent_all.reshape(micros * block_rows, model)
    first_row = lax.axis_index("dp") * block_rows
    ends = jnp.cumsum(seq_lengths, axis=1)
    info = jnp.concatenate(
        [ends - seq_lengths, jnp.full((micros, 1), first_row, jnp.int32)], axis=1
    ).astype(jnp.int32)
    pre_conv = jnp.dot(normed_all, w_in[:, :conv_width], preferred_element_type=F32).astype(BF16)
    gate_lin = jnp.dot(normed_all, w_in[:, conv_width:main_width], preferred_element_type=F32)
    dec = jnp.dot(normed_all, w_in[:, main_width:], preferred_element_type=F32)
    last_rows = pre_conv.reshape(micros, block_rows, conv_width)[:, block_rows - HALO :]
    rim = from_behind(last_rows, "dp", 1)

    plain, carried_map, inverses, starts, final = mix_forward(
        info, pre_conv, rim, dec, taps, par, micros, heads, key_size
    )
    block_map = final[..., value_size:]
    incoming = scan_states(block_map, final[..., :value_size], False)
    head_rows = (micros, block_rows, heads)
    carried_map = carried_map.reshape(head_rows + (key_size,))
    mixed = plain.reshape(head_rows + (value_size,)) + jnp.einsum(
        "mthd,mhdv->mthv", carried_map, incoming.astype(BF16), preferred_element_type=F32
    )
    out_scale = lax.rsqrt(jnp.mean(mixed * mixed, axis=-1, keepdims=True) + HEAD_FLOOR)
    normed_mix = mixed * out_scale
    gate_lin = gate_lin.reshape(head_rows + (value_size,))
    gate_sigmoid = jax.nn.sigmoid(gate_lin)
    gate_active = gate_lin * gate_sigmoid
    gated = (normed_mix * head_norm * gate_active).astype(BF16).reshape(-1, v_width)

    mix_part = jnp.dot(gated, w_out, preferred_element_type=F32)
    after_mix = residual + head_scatter(mix_part.reshape(micros, block_rows, model))
    scale_two = lax.rsqrt(jnp.mean(after_mix * after_mix, axis=-1, keepdims=True) + EPSILON)
    normed_two = after_mix * scale_two
    ffn_all = head_gather((normed_two * ffn_norm).astype(BF16)).reshape(-1, model)
    gate_ffn = jnp.dot(ffn_all, w_ffn[:, :ffn_width], preferred_element_type=F32)
    up_ffn = jnp.dot(ffn_all, w_ffn[:, ffn_width:], preferred_element_type=F32)
    ffn_sigmoid = jax.nn.sigmoid(gate_ffn)
    ffn_active = gate_ffn * ffn_sigmoid
    hidden = (ffn_active * up_ffn).astype(BF16)
    ffn_part = jnp.dot(hidden, w_down, preferred_element_type=F32).astype(BF16)
    ffn_sum = head_scatter(ffn_part.reshape(micros, block_rows, model)).astype(F32)
    block_out = (after_mix + ffn_sum).astype(BF16)

    hidden_grad = contract_cols(cotangent_all, w_down)
    shard_down = dp_scatter(contract_rows(hidden, cotangent_all), 1)
    gate_ffn_grad = hidden_grad * up_ffn * ffn_sigmoid * (1.0 + gate_ffn * (1.0 - ffn_sigmoid))
    up_ffn_grad = hidden_grad * ffn_active
    gate_up_grad = jnp.concatenate([gate_ffn_grad, up_ffn_grad], axis=1).astype(BF16)
    shard_ffn = dp_scatter(contract_rows(ffn_all, gate_up_grad), 0)
    ffn_in_part = contract_cols(gate_up_grad, w_ffn)
    ffn_in_grad = head_scatter(ffn_in_part.reshape(micros, block_rows, model))
    grad_norm_two = jnp.sum(ffn_in_grad * normed_two, axis=(0, 1))
    after_mix_grad = out_grad.astype(F32) + norm_backward(
        ffn_in_grad * ffn_norm, normed_two, scale_two
    )

    branch_grad = head_gather(after_mix_grad.astype(BF16)).reshape(-1, model)
    gated_grad = contract_cols(branch_grad, w_out).reshape(head_rows + (value_size,))
    shard_out = dp_scatter(contract_rows(gated, branch_grad), 1)
    grad_head_norm = jnp.sum(gated_grad * normed_mix * gate_active, axis=(0, 1, 2))
    gate_lin_grad = (
        gated_grad * normed_mix * head_norm * gate_sigmoid * (1.0 + gate_lin * (1.0 - gate_sigmoid))
    )
    mixed_grad = norm_backward(gated_grad * head_norm * gate_active, normed_mix, out_scale)

    local_grad = jnp.einsum(
        "mthd,mthv->mhdv", carried_map, mixed_grad.astype(BF16), preferred_element_type=F32
    )
    leaving = scan_states(block_map, local_grad, True)
    pre_grad, rim_grad, tail, dec_grad, taps_grad, par_grad = mix_backward(
        info,
        pre_conv,
        rim,
        dec,
        taps,
        par,
        mixed_grad.reshape(-1, v_width),
        inverses,
        starts,
        incoming,
        leaving,
        micros,
        heads,
        key_size,
    )
    back_rim = from_behind(rim_grad, "dp", -1)
    tail = jnp.concatenate([tail[:, :8], tail[:, 8:] + back_rim], axis=1).astype(BF16)
    pre_grad = lax.dynamic_update_slice(
        pre_grad.reshape(micros, block_rows, conv_width), tail, (0, block_rows - HALO, 0)
    ).reshape(-1, conv_width)

    proj_grad = jnp.concatenate(
        [pre_grad, gate_lin_grad.reshape(-1, v_width).astype(BF16), dec_grad], axis=1
    )
    shard_in = dp_scatter(contract_rows(normed_all, proj_grad), 0)
    normed_part = contract_cols(proj_grad, w_in).astype(BF16)
    normed_grad = head_scatter(normed_part.reshape(micros, block_rows, model)).astype(F32)
    grad_norm_one = jnp.sum(normed_grad * normed_one, axis=(0, 1))
    input_grad = after_mix_grad + norm_backward(normed_grad * attn_norm, normed_one, scale_one)

    small = jnp.concatenate(
        [
            taps_grad[:KCONV].reshape(-1),
            jnp.pad(par_grad[0, :heads], (0, LANES - heads)),
            jnp.pad(par_grad[1, :heads], (0, LANES - heads)),
            grad_head_norm,
            grad_norm_one,
            grad_norm_two,
        ]
    ).reshape(-1, LANES)
    small = jnp.sum(lax.all_gather(small, "dp"), axis=0)
    small = lax.all_gather(small, "head")
    head_count = small.shape[0]
    tap_rows = KCONV * conv_width // LANES
    taps_all = small[:, :tap_rows].reshape(head_count, KCONV, conv_width).transpose(1, 0, 2)

    def joined(low, high):
        return taps_all[:, :, low:high].reshape(KCONV, -1)

    rest = jnp.sum(small[:, tap_rows + 2 :], axis=0).reshape(-1)
    return (
        block_out,
        input_grad,
        rest[value_size : value_size + model],
        shard_in[:, :qk_width],
        shard_in[:, qk_width : 2 * qk_width],
        shard_in[:, 2 * qk_width : conv_width],
        shard_in[:, conv_width:main_width],
        shard_in[:, main_width : main_width + heads],
        shard_in[:, main_width + heads : main_width + 2 * heads],
        joined(0, qk_width),
        joined(qk_width, 2 * qk_width),
        joined(2 * qk_width, conv_width),
        small[:, tap_rows, :heads].reshape(-1),
        small[:, tap_rows + 1, :heads].reshape(-1),
        rest[:value_size],
        shard_out,
        rest[value_size + model :],
        shard_ffn[:, :ffn_width],
        shard_ffn[:, ffn_width:],
        shard_down,
    )


def solution(mesh):
    rows, plane, turned, whole = P(None, ("dp", "head"), None), P("dp", "head"), P("head", "dp"), P()
    in_specs = (rows, rows, whole, whole) + (plane,) * 6 + (whole,) * 6
    in_specs += (turned, whole, plane, plane, turned)
    out_specs = (rows, rows, whole) + (plane,) * 6 + (whole,) * 6
    out_specs += (turned, whole, plane, plane, turned)
    return jax.shard_map(body, mesh=mesh, in_specs=in_specs, out_specs=out_specs, check_vma=False)
```

```python
from functools import partial

import jax
import jax.numpy as jnp
from jax import lax
from jax.experimental import pallas as pl
from jax.experimental.pallas import tpu as pltpu
from jax.sharding import PartitionSpec as P

CHUNK = 128
KCONV = 4
LANES = 128
HALO = 16

EPSILON = 1e-06
HEAD_FLOOR = 0.01
F32 = jnp.float32
BF16 = jnp.bfloat16
NN = (((1,), (0,)), ((), ()))
NT = (((1,), (1,)), ((), ()))
TN = (((0,), (0,)), ((), ()))


def mm(left, right, dims=NN):
    return lax.dot_general(
        left.astype(BF16), right.astype(BF16), dims, preferred_element_type=F32
    )


def split(value):
    high = value.astype(BF16)
    return high, (value - high.astype(F32)).astype(BF16)


def mm3(left, right, dims=NN):
    left_high, left_low = split(left)
    right_high, right_low = split(right)
    return mm(left_high, right_high, dims) + (
        mm(left_high, right_low, dims) + mm(left_low, right_high, dims)
    )


def chunk_places(info_ref, micro, chunk, seq_count):
    first = info_ref[micro, seq_count] + chunk * CHUNK
    starts = [info_ref[micro, at] for at in range(seq_count)]
    rows = first + lax.broadcasted_iota(jnp.int32, (CHUNK, 1), 0)
    lanes = first + lax.broadcasted_iota(jnp.int32, (1, CHUNK), 1)
    seg_col = jnp.zeros((CHUNK, 1), jnp.int32)
    seg_row = jnp.zeros((1, CHUNK), jnp.int32)
    begun = jnp.zeros((CHUNK, 1), jnp.int32)
    seg_before = jnp.int32(0)
    seg_last = jnp.int32(0)
    for start in starts:
        seg_col = seg_col + jnp.where(rows >= start, 1, 0)
        seg_row = seg_row + jnp.where(lanes >= start, 1, 0)
        begun = jnp.maximum(begun, jnp.where(rows >= start, start, 0))
        seg_before = seg_before + jnp.where(first - 1 >= start, 1, 0)
        seg_last = seg_last + jnp.where(first + CHUNK - 1 >= start, 1, 0)
    offset = rows - begun
    row_ids = lax.broadcasted_iota(jnp.int32, (CHUNK, CHUNK), 0)
    col_ids = lax.broadcasted_iota(jnp.int32, (CHUNK, CHUNK), 1)
    same = seg_col == seg_row
    return dict(
        row_ids=row_ids,
        col_ids=col_ids,
        inclusive=jnp.logical_and(row_ids >= col_ids, same),
        strictly=jnp.logical_and(row_ids > col_ids, same),
        untouched=jnp.where(seg_col == seg_before, 1.0, 0.0).astype(F32),
        with_last=jnp.where(seg_col == seg_last, 1.0, 0.0).astype(F32),
        lags=[jnp.where(offset >= lag, 1.0, 0.0).astype(F32) for lag in range(1, KCONV)],
    )


def decay_parts(g_col, places):
    row_ids, col_ids = places["row_ids"], places["col_ids"]
    cum_row = jnp.sum(jnp.where(row_ids <= col_ids, g_col, 0.0), axis=0, keepdims=True)
    cum_col = jnp.sum(jnp.where(row_ids == col_ids, cum_row, 0.0), axis=1, keepdims=True)
    spread = jnp.where(places["inclusive"], cum_col - cum_row, 0.0)
    pair = jnp.where(places["inclusive"], jnp.exp(spread), 0.0)
    carry = jnp.exp(cum_col) * places["untouched"]
    cum_last = cum_col[CHUNK - 1 :, :]
    to_last = jnp.exp(jnp.minimum(cum_last - cum_col, 0.0)) * places["with_last"]
    return pair, carry, to_last, carry[CHUNK - 1 :, :]


def conv_rows(extended, taps, lags):
    total = taps[KCONV - 1 :, :] * extended[HALO:]
    for lag in range(1, KCONV):
        shifted = extended[HALO - lag : HALO - lag + CHUNK]
        total = total + taps[KCONV - 1 - lag : KCONV - lag, :] * shifted * lags[lag - 1]
    return total


def head_columns(head, heads, key_size, value_size):
    return (
        (head * key_size, key_size),
        ((heads + head) * key_size, key_size),
        (2 * heads * key_size + head * value_size, value_size),
    )


def unit_rows(active):
    return active * lax.rsqrt(jnp.sum(active * active, axis=1, keepdims=True) + EPSILON)


def softplus(value):
    return jnp.maximum(value, 0.0) + jnp.log1p(jnp.exp(-jnp.abs(value)))


def unit_lower_inverses(systems, places):
    row_ids, col_ids = places["row_ids"], places["col_ids"]
    eye = jnp.where(row_ids == col_ids, 1.0, 0.0).astype(F32)
    pairs = jnp.right_shift(row_ids, 1) == jnp.right_shift(col_ids, 1)
    found = [eye - jnp.where(pairs, system, 0.0) for system in systems]
    level = 1
    while (1 << level) < CHUNK:
        row_block = jnp.right_shift(row_ids, level)
        col_block = jnp.right_shift(col_ids, level)
        lower = jnp.logical_and(
            jnp.right_shift(row_block, 1) == jnp.right_shift(col_block, 1), row_block > col_block
        )
        inner = [
            INVERSE_MM(jnp.where(lower, system, 0.0), inverse)
            for system, inverse in zip(systems, found)
        ]
        found = [
            inverse - INVERSE_MM(inverse, middle) for inverse, middle in zip(found, inner)
        ]
        level += 1
    return found


INVERSE_MM = mm3


def mix_forward_kernel(
    info_ref,
    x_ref,
    rim_ref,
    dec_ref,
    taps_ref,
    par_ref,
    out_ref,
    cmap_ref,
    inv_ref,
    start_ref,
    final_ref,
    halo,
    state,
    *,
    heads,
    key_size,
    value_size,
    seq_count,
):
    micro, chunk = pl.program_id(0), pl.program_id(1)
    span = range(heads)

    @pl.when(chunk == 0)
    def _():
        halo[...] = rim_ref[0]
        row_ids = lax.broadcasted_iota(jnp.int32, (key_size, key_size), 0)
        col_ids = lax.broadcasted_iota(jnp.int32, (key_size, key_size), 1)
        eye = jnp.where(row_ids == col_ids, 1.0, 0.0).astype(F32)
        for head in span:
            state[head] = jnp.concatenate([jnp.zeros((key_size, value_size), F32), eye], axis=1)

    places = chunk_places(info_ref, micro, chunk, seq_count)
    dec = dec_ref[...]
    beta_all = jax.nn.sigmoid(dec)
    g_all = par_ref[0:1, :] * softplus(dec + par_ref[1:2, :])
    scale = key_size**-0.5

    queries, keys, values = [], [], []
    for head in span:
        rows = []
        for begin, width in head_columns(head, heads, key_size, value_size):
            cut = slice(begin, begin + width)
            extended = jnp.concatenate(
                [halo[:, cut].astype(F32), x_ref[:, cut].astype(F32)], axis=0
            )
            summed = conv_rows(extended, taps_ref[0:KCONV, cut], places["lags"])
            rows.append(summed * jax.nn.sigmoid(summed))
        queries.append(unit_rows(rows[0]) * scale)
        keys.append(unit_rows(rows[1]))
        values.append(rows[2])
    halo[...] = x_ref[CHUNK - HALO :, :]

    betas = [beta_all[:, heads + head : heads + head + 1] for head in span]
    decays = [decay_parts(g_all[:, head : head + 1], places) for head in span]
    grams = [mm(keys[head], keys[head], NT) for head in span]
    systems = [
        jnp.where(places["strictly"], betas[head] * decays[head][0] * grams[head], 0.0)
        for head in span
    ]
    inverses = unit_lower_inverses(systems, places)
    attends = [mm(queries[head], keys[head], NT) * decays[head][0] for head in span]
    solved = [
        mm(
            inverses[head],
            jnp.concatenate(
                [betas[head] * values[head], betas[head] * decays[head][1] * keys[head]], axis=1
            ),
        )
        for head in span
    ]
    starts = [state[head] for head in span]
    written = [
        jnp.concatenate(
            [solved[head][:, :value_size], jnp.zeros((CHUNK, key_size), F32)], axis=1
        )
        - mm(solved[head][:, value_size:], starts[head])
        for head in span
    ]
    outs = [
        decays[head][1] * mm(queries[head], starts[head]) + mm(attends[head], written[head])
        for head in span
    ]
    for head in span:
        _, _, to_last, carry_last = decays[head]
        inv_ref[0, head] = inverses[head].astype(BF16)
        start_ref[0, head] = starts[head].astype(BF16)
        out_ref[:, head * value_size : (head + 1) * value_size] = outs[head][:, :value_size]
        cmap_ref[:, head * key_size : (head + 1) * key_size] = outs[head][:, value_size:].astype(
            BF16
        )
        state[head] = carry_last * starts[head] + mm(to_last * keys[head], written[head], TN)

    @pl.when(chunk == pl.num_programs(1) - 1)
    def _():
        final_ref[0] = state[...]


def mix_backward_kernel(
    info_ref,
    x_ref,
    before_ref,
    rim_ref,
    dec_ref,
    taps_ref,
    par_ref,
    grad_ref,
    inv_ref,
    start_ref,
    incoming_ref,
    leaving_ref,
    dx_ref,
    rim_grad_ref,
    tail_ref,
    ddec_ref,
    dtaps_ref,
    dpar_ref,
    carry,
    dstate,
    *,
    heads,
    key_size,
    value_size,
    seq_count,
):
    micro, step = pl.program_id(0), pl.program_id(1)
    chunk = pl.num_programs(1) - 1 - step
    span = range(heads)

    @pl.when(step == 0)
    def _():
        carry[...] = jnp.zeros_like(carry)
        dstate[...] = leaving_ref[0].astype(F32)

    @pl.when(jnp.logical_and(micro == 0, step == 0))
    def _():
        dtaps_ref[...] = jnp.zeros_like(dtaps_ref)
        dpar_ref[...] = jnp.zeros_like(dpar_ref)

    places = chunk_places(info_ref, micro, chunk, seq_count)
    row_ids, col_ids = places["row_ids"], places["col_ids"]
    lags = places["lags"]
    dec = dec_ref[...]
    beta_all = jax.nn.sigmoid(dec)
    shifted_dec = dec + par_ref[1:2, :]
    g_all = par_ref[0:1, :] * softplus(shifted_dec)
    scale = key_size**-0.5
    opening = jnp.where(chunk == 0, rim_ref[0].astype(F32), before_ref[...].astype(F32))

    def extended_rows(cut):
        return jnp.concatenate([opening[:, cut], x_ref[:, cut].astype(F32)], axis=0)

    sums, norms, unit = [], [], []
    for head in span:
        mine = [
            conv_rows(extended_rows(slice(begin, begin + width)), taps_ref[0:KCONV, begin : begin + width], lags)
            for begin, width in head_columns(head, heads, key_size, value_size)
        ]
        active = [value * jax.nn.sigmoid(value) for value in mine]
        inverse_norms = [
            lax.rsqrt(jnp.sum(value * value, axis=1, keepdims=True) + EPSILON)
            for value in active[:2]
        ]
        sums.append(mine)
        norms.append(inverse_norms)
        unit.append([active[0] * inverse_norms[0], active[1] * inverse_norms[1], active[2]])
    keys = [unit[head][1] for head in span]
    key_low = [keys[head].astype(BF16) for head in span]
    query_low = [(unit[head][0] * scale).astype(BF16) for head in span]
    betas = [beta_all[:, heads + head : heads + head + 1] for head in span]
    decays = [decay_parts(g_all[:, head : head + 1], places) for head in span]
    grams = [mm(key_low[head], key_low[head], NT) for head in span]
    products = [mm(query_low[head], key_low[head], NT) for head in span]
    attends = [(products[head] * decays[head][0]).astype(BF16) for head in span]
    starts = []
    for head in span:
        saved = start_ref[0, head]
        starts.append(
            saved[:, :value_size].astype(F32)
            + mm(saved[:, value_size:], incoming_ref[0, head])
        )
    start_low = [starts[head].astype(BF16) for head in span]
    key_state = [mm(key_low[head], start_low[head]) for head in span]
    query_state = [mm(query_low[head], start_low[head]) for head in span]
    grads = [grad_ref[:, head * value_size : (head + 1) * value_size] for head in span]
    grad_low = [grads[head].astype(BF16) for head in span]
    residues = [unit[head][2] - decays[head][1] * key_state[head] for head in span]
    inverses = [inv_ref[0, head] for head in span]
    written = [mm(inverses[head], betas[head] * residues[head]).astype(BF16) for head in span]
    ahead = [dstate[head] for head in span]
    ahead_low = [ahead[head].astype(BF16) for head in span]
    key_last = [(decays[head][2] * keys[head]).astype(BF16) for head in span]
    dwritten = [
        mm(attends[head], grad_low[head], TN) + mm(key_last[head], ahead_low[head])
        for head in span
    ]
    dresidue = [mm(inverses[head], dwritten[head], TN) for head in span]
    dresidue_low = [dresidue[head].astype(BF16) for head in span]
    dattend = [
        jnp.where(places["inclusive"], mm(grad_low[head], written[head], NT), 0.0)
        for head in span
    ]
    dsystem = [
        jnp.where(places["strictly"], -mm(dresidue_low[head], written[head], NT), 0.0)
        for head in span
    ]
    dproducts = [(dattend[head] * decays[head][0]).astype(BF16) for head in span]
    dcarried = [decays[head][1] * grads[head] for head in span]
    dcarried_low = [dcarried[head].astype(BF16) for head in span]
    dkey_state = [-(betas[head] * decays[head][1]) * dresidue[head] for head in span]
    dkey_state_low = [dkey_state[head].astype(BF16) for head in span]
    dkey_last = [mm(written[head], ahead_low[head], NT) for head in span]
    dgram = [dsystem[head] * betas[head] * decays[head][0] for head in span]
    dgram_low = [dgram[head].astype(BF16) for head in span]
    dquery = [
        mm(dcarried_low[head], start_low[head], NT) + mm(dproducts[head], key_low[head])
        for head in span
    ]
    dkey = [
        mm(dproducts[head], query_low[head], TN)
        + decays[head][2] * dkey_last[head]
        + mm(dkey_state_low[head], start_low[head], NT)
        + mm(dgram_low[head], key_low[head])
        + mm(dgram_low[head], key_low[head], TN)
        for head in span
    ]
    lane_ids = lax.broadcasted_iota(jnp.int32, (CHUNK, LANES), 1)
    ddec = jnp.zeros((CHUNK, LANES), F32)
    dg_all = jnp.zeros((CHUNK, LANES), F32)
    for head in span:
        pair, carried, to_last, carry_last = decays[head]
        coupled = dsystem[head] * grams[head]
        dpair = (dattend[head] * products[head] + coupled * betas[head]) * pair
        dbeta = jnp.sum(coupled * pair, axis=1, keepdims=True) + jnp.sum(
            dresidue[head] * residues[head], axis=1, keepdims=True
        )
        dcarry = jnp.sum(
            grads[head] * query_state[head] - betas[head] * dresidue[head] * key_state[head],
            axis=1,
            keepdims=True,
        )
        dcarry_last = jnp.sum(
            jnp.sum(ahead[head] * starts[head], axis=1, keepdims=True), axis=0, keepdims=True
        )
        dto_last = jnp.sum(dkey_last[head] * keys[head], axis=1, keepdims=True) * to_last
        is_last = lax.broadcasted_iota(jnp.int32, (CHUNK, 1), 0) == CHUNK - 1
        dcum_col = (
            jnp.sum(dpair, axis=1, keepdims=True)
            + dcarry * carried
            - dto_last
            + jnp.where(
                is_last,
                dcarry_last * carry_last + jnp.sum(dto_last, axis=0, keepdims=True),
                0.0,
            )
        )
        dcum_row = jnp.sum(
            jnp.where(row_ids == col_ids, dcum_col, 0.0) - dpair, axis=0, keepdims=True
        )
        dg = jnp.sum(jnp.where(col_ids >= row_ids, dcum_row, 0.0), axis=1, keepdims=True)
        beta = betas[head]
        dg_all = jnp.where(lane_ids == head, dg, dg_all)
        ddec = jnp.where(lane_ids == heads + head, dbeta * beta * (1.0 - beta), ddec)
        dstate[head] = (
            carry_last * ahead[head]
            + mm(query_low[head], dcarried_low[head], TN)
            + mm(key_low[head], dkey_state_low[head], TN)
        )
    dstep = dg_all * par_ref[0:1, :] * jax.nn.sigmoid(shifted_dec)
    ddec = ddec + dstep
    ddec_ref[...] = ddec.astype(BF16)
    dpar_ref[0:1, :] += jnp.sum(dg_all * g_all, axis=0, keepdims=True)
    dpar_ref[1:2, :] += jnp.sum(dstep, axis=0, keepdims=True)

    edge = jnp.zeros((8, 1), F32)
    for head in span:
        dunit = [dquery[head] * scale, dkey[head]]
        dactive = [
            norms[head][at]
            * (
                dunit[at]
                - unit[head][at] * jnp.sum(dunit[at] * unit[head][at], axis=1, keepdims=True)
            )
            for at in range(2)
        ]
        dactive.append(betas[head] * dresidue[head])
        for at, (begin, width) in enumerate(head_columns(head, heads, key_size, value_size)):
            cut = slice(begin, begin + width)
            sig = jax.nn.sigmoid(sums[head][at])
            dsum = dactive[at] * sig * (1.0 + sums[head][at] * (1.0 - sig))
            extended = extended_rows(cut)
            taps = taps_ref[0:KCONV, cut]
            zeros = jnp.zeros((8, width), F32)
            dtaps_ref[KCONV - 1 : KCONV, cut] += jnp.sum(
                dsum * extended[HALO:], axis=0, keepdims=True
            )
            total = jnp.concatenate([zeros, taps[KCONV - 1 :, :] * dsum], axis=0)
            for lag in range(1, KCONV):
                masked = dsum * lags[lag - 1]
                at_tap = KCONV - 1 - lag
                dtaps_ref[at_tap : at_tap + 1, cut] += jnp.sum(
                    masked * extended[HALO - lag : HALO - lag + CHUNK], axis=0, keepdims=True
                )
                padded = jnp.concatenate(
                    [zeros, taps[at_tap : at_tap + 1, :] * masked, zeros], axis=0
                )
                total = total + padded[lag : lag + 8 + CHUNK]
            body_rows = jnp.concatenate(
                [total[8:CHUNK], total[CHUNK:] + carry[:, cut]], axis=0
            )
            dx_ref[:, cut] = body_rows.astype(BF16)
            carry[:, cut] = total[:8]

            @pl.when(step == 0)
            def _():
                tail_ref[0, :, cut] = body_rows[CHUNK - HALO :]

    @pl.when(chunk == 0)
    def _():
        rim_grad_ref[0] = carry[...]


def gate_forward_kernel(
    info_ref, plain_ref, cmap_ref, incoming_ref, gate_ref, gain_ref, mixed_ref, gated_ref, *, heads, key_size, value_size
):
    for head in range(heads):
        cut = slice(head * value_size, (head + 1) * value_size)
        mixed = plain_ref[:, cut] + mm(
            cmap_ref[:, head * key_size : (head + 1) * key_size], incoming_ref[0, head]
        )
        mixed_ref[:, cut] = mixed
        normed = mixed * lax.rsqrt(
            jnp.mean(mixed * mixed, axis=1, keepdims=True) + HEAD_FLOOR
        )
        gate = gate_ref[:, cut]
        gated_ref[:, cut] = (normed * gain_ref[0:1, :] * gate * jax.nn.sigmoid(gate)).astype(BF16)


def gate_backward_kernel(
    info_ref,
    grad_ref,
    mixed_ref,
    cmap_ref,
    gate_ref,
    gain_ref,
    dgate_ref,
    dmixed_ref,
    dlocal_ref,
    dgain_ref,
    *,
    heads,
    key_size,
    value_size,
):
    micro, step = pl.program_id(0), pl.program_id(1)

    @pl.when(step == 0)
    def _():
        dlocal_ref[...] = jnp.zeros_like(dlocal_ref)

    @pl.when(jnp.logical_and(micro == 0, step == 0))
    def _():
        dgain_ref[...] = jnp.zeros_like(dgain_ref)

    gain = gain_ref[0:1, :]
    for head in range(heads):
        cut = slice(head * value_size, (head + 1) * value_size)
        mixed = mixed_ref[:, cut]
        scale = lax.rsqrt(jnp.mean(mixed * mixed, axis=1, keepdims=True) + HEAD_FLOOR)
        normed = mixed * scale
        gate = gate_ref[:, cut]
        sig = jax.nn.sigmoid(gate)
        active = gate * sig
        grad = grad_ref[:, cut]
        by_norm = grad * normed
        dgain_ref[0:1, :] += jnp.sum(by_norm * active, axis=0, keepdims=True)
        dgate_ref[:, cut] = (by_norm * gain * sig * (1.0 + gate * (1.0 - sig))).astype(BF16)
        dnormed = grad * gain * active
        dmixed = scale * (dnormed - normed * jnp.mean(dnormed * normed, axis=1, keepdims=True))
        dmixed_ref[:, cut] = dmixed
        dlocal_ref[0, head] += mm(
            cmap_ref[:, head * key_size : (head + 1) * key_size], dmixed, TN
        )


VMEM_BYTES = 48 * 1024 * 1024


def kernel_call(kernel, info, arrays, grid, in_specs, out_specs, out_shape, scratch, name, **sizes):
    return pl.pallas_call(
        partial(kernel, **sizes),
        grid_spec=pltpu.PrefetchScalarGridSpec(
            num_scalar_prefetch=1,
            grid=grid,
            in_specs=in_specs,
            out_specs=out_specs,
            scratch_shapes=scratch,
        ),
        out_shape=out_shape,
        compiler_params=pltpu.CompilerParams(
            dimension_semantics=("arbitrary",) * len(grid), vmem_limit_bytes=VMEM_BYTES
        ),
        name=name,
    )(info, *arrays)


class Mix:
    def __init__(self, info, micros, chunks, heads, key_size, value_size):
        self.info, self.micros, self.chunks = info, micros, chunks
        self.heads, self.key_size, self.value_size = heads, key_size, value_size
        self.width = heads * (2 * key_size + value_size)
        self.wide = key_size + value_size
        self.rows = micros * chunks * CHUNK
        self.sizes = dict(heads=heads, key_size=key_size, value_size=value_size)

    def block(self, m, c, info):
        return m * self.chunks + jnp.bitwise_xor(c, info[0, info.shape[1] - 1])

    def by_rows(self, columns, turned=False):
        def place(m, c, info):
            return self.block(m, self.chunks - 1 - c if turned else c, info), 0

        return pl.BlockSpec((CHUNK, columns), place)

    def by_chunk(self, rows, columns, turned=False):
        def place(m, c, info):
            return m * self.chunks + (self.chunks - 1 - c if turned else c), 0, 0, 0

        return pl.BlockSpec((1, self.heads, rows, columns), place)

    def by_micro(self, *dims):
        return pl.BlockSpec((1,) + dims, lambda m, c, info: (m,) + (0,) * len(dims))

    def whole(self, *dims):
        return pl.BlockSpec(dims, lambda m, c, info: (0,) * len(dims))

    def like(self, dtype, *dims):
        return jax.ShapeDtypeStruct(dims, dtype)

    def call(self, kernel, arrays, in_specs, outs, scratch, name, **more):
        return kernel_call(
            kernel,
            self.info,
            arrays,
            (self.micros, self.chunks),
            in_specs,
            [spec for spec, _ in outs],
            [shape for _, shape in outs],
            scratch,
            name,
            **self.sizes,
            **more,
        )

    def forward(self, pre_conv, rim, dec, taps, par):
        h, dk, dv, wide, width = self.heads, self.key_size, self.value_size, self.wide, self.width
        steps = self.micros * self.chunks
        return self.call(
            mix_forward_kernel,
            (pre_conv, rim, dec, taps, par),
            [
                self.by_rows(width),
                self.by_micro(HALO, width),
                self.by_rows(LANES),
                self.whole(8, width),
                self.whole(8, LANES),
            ],
            [
                (self.by_rows(h * dv), self.like(F32, self.rows, h * dv)),
                (self.by_rows(h * dk), self.like(BF16, self.rows, h * dk)),
                (self.by_chunk(CHUNK, CHUNK), self.like(BF16, steps, h, CHUNK, CHUNK)),
                (self.by_chunk(dk, wide), self.like(BF16, steps, h, dk, wide)),
                (self.by_micro(h, dk, wide), self.like(F32, self.micros, h, dk, wide)),
            ],
            [pltpu.VMEM((HALO, width), BF16), pltpu.VMEM((h, dk, wide), F32)],
            "mix_forward",
            seq_count=self.info.shape[1] - 2,
        )

    def backward(self, pre_conv, rim, dec, taps, par, grad, inverses, starts, incoming, leaving):
        h, dk, dv, wide, width = self.heads, self.key_size, self.value_size, self.wide, self.width
        halo_blocks = CHUNK // HALO

        def before(m, c, info):
            earlier = jnp.maximum(self.chunks - 2 - c, 0)
            return (self.block(m, earlier, info) + 1) * halo_blocks - 1, 0

        return self.call(
            mix_backward_kernel,
            (pre_conv, pre_conv, rim, dec, taps, par, grad, inverses, starts, incoming, leaving),
            [
                self.by_rows(width, True),
                pl.BlockSpec((HALO, width), before),
                self.by_micro(HALO, width),
                self.by_rows(LANES, True),
                self.whole(8, width),
                self.whole(8, LANES),
                self.by_rows(h * dv, True),
                self.by_chunk(CHUNK, CHUNK, True),
                self.by_chunk(dk, wide, True),
                self.by_micro(h, dk, dv),
                self.by_micro(h, dk, dv),
            ],
            [
                (self.by_rows(width, True), self.like(BF16, self.rows, width)),
                (self.by_micro(8, width), self.like(F32, self.micros, 8, width)),
                (self.by_micro(HALO, width), self.like(F32, self.micros, HALO, width)),
                (self.by_rows(LANES, True), self.like(BF16, self.rows, LANES)),
                (self.whole(8, width), self.like(F32, 8, width)),
                (self.whole(8, LANES), self.like(F32, 8, LANES)),
            ],
            [pltpu.VMEM((8, width), F32), pltpu.VMEM((h, dk, dv), F32)],
            "mix_backward",
            seq_count=self.info.shape[1] - 2,
        )

    def gate_forward(self, plain, cmap, incoming, gate, gain):
        h, dk, dv = self.heads, self.key_size, self.value_size
        return self.call(
            gate_forward_kernel,
            (plain, cmap, incoming, gate, gain),
            [
                self.by_rows(h * dv),
                self.by_rows(h * dk),
                self.by_micro(h, dk, dv),
                self.by_rows(h * dv),
                self.whole(8, dv),
            ],
            [
                (self.by_rows(h * dv), self.like(F32, self.rows, h * dv)),
                (self.by_rows(h * dv), self.like(BF16, self.rows, h * dv)),
            ],
            [],
            "gate_forward",
        )

    def gate_backward(self, grad, mixed, cmap, gate, gain):
        h, dk, dv = self.heads, self.key_size, self.value_size
        return self.call(
            gate_backward_kernel,
            (grad, mixed, cmap, gate, gain),
            [
                self.by_rows(h * dv),
                self.by_rows(h * dv),
                self.by_rows(h * dk),
                self.by_rows(h * dv),
                self.whole(8, dv),
            ],
            [
                (self.by_rows(h * dv), self.like(BF16, self.rows, h * dv)),
                (self.by_rows(h * dv), self.like(F32, self.rows, h * dv)),
                (self.by_micro(h, dk, dv), self.like(F32, self.micros, h, dk, dv)),
                (self.whole(8, dv), self.like(F32, 8, dv)),
            ],
            [],
            "gate_backward",
        )


def from_behind(value, axis, steps):
    count = lax.axis_size(axis)
    leading, last = (max(0, -steps), min(count, count - steps))
    return lax.ppermute(value, axis, [(source, source + steps) for source in range(leading, last)])


def swap(value, axis, bit):
    return lax.ppermute(value, axis, [(at, at ^ bit) for at in range(lax.axis_size(axis))])


def head_gather(value):
    across = swap(value, "head", 2)
    both = swap(jnp.stack([value, across], axis=1), "head", 1)
    return jnp.stack([value, both[:, 0], across, both[:, 1]], axis=1)


def head_scatter(parts):
    near = swap(jnp.stack([parts[:, 1], parts[:, 3]], axis=1).astype(BF16), "head", 1)
    mine = parts[:, 0].astype(F32) + near[:, 0].astype(F32)
    theirs = parts[:, 2].astype(F32) + near[:, 1].astype(F32)
    return mine + swap(theirs.astype(BF16), "head", 2).astype(F32)


def ring_order():
    count = lax.axis_size("dp")
    return list(range(0, count, 2)) + list(range(count - 1, 0, -2))


def ring_place():
    count, mine = lax.axis_size("dp"), lax.axis_index("dp")
    return jnp.where(mine % 2 == 0, mine // 2, count - 1 - mine // 2)


def ring_steps():
    ring = ring_order()
    ahead = [(ring[at], ring[(at + 1) % len(ring)]) for at in range(len(ring))]
    return ahead, [(after, before) for before, after in ahead]


def to_ring(value):
    ring = ring_order()
    size = value.shape[-1] // len(ring)
    parts = [value[..., rank * size : (rank + 1) * size] for rank in ring]
    twice = jnp.concatenate(parts + parts[:-1], axis=-1)
    return lax.dynamic_slice_in_dim(twice, ring_place() * size, value.shape[-1], value.ndim - 1)


def from_ring(value):
    ring = ring_order()
    count = len(ring)
    size = value.shape[-1] // count
    start = jnp.where(ring_place() == 0, 0, count - ring_place())
    turned = lax.dynamic_slice_in_dim(
        jnp.concatenate([value, value[..., : (count - 1) * size]], axis=-1),
        start * size,
        value.shape[-1],
        value.ndim - 1,
    )
    parts = [None] * count
    for at, rank in enumerate(ring):
        parts[rank] = turned[..., at * size : (at + 1) * size]
    return jnp.concatenate(parts, axis=-1)


def ring_gather(shard, axis):
    ahead, back = ring_steps()
    count = len(ahead)
    from_left, from_right = [shard], [shard]
    for _ in range(1, count // 2):
        from_left.append(lax.ppermute(from_left[-1], "dp", ahead))
        from_right.append(lax.ppermute(from_right[-1], "dp", back))
    half = shard.shape[0] // 2
    far = jnp.concatenate(
        [
            lax.ppermute(from_left[-1][:half], "dp", ahead),
            lax.ppermute(from_right[-1][half:], "dp", back),
        ],
        axis=0,
    )
    return jnp.concatenate(from_right + [far] + from_left[:0:-1], axis=axis), far


def ring_scatter(blocks):
    ahead, back = ring_steps()
    count = len(ahead)
    half = blocks[0].shape[0] // 2
    middle = count // 2

    def add(one, other):
        return one.astype(F32) + other.astype(F32)

    left = lax.ppermute(blocks[middle][:half], "dp", ahead)
    right = lax.ppermute(blocks[middle][half:], "dp", back)
    for at in range(middle - 1, 0, -1):
        up, down = blocks[at], blocks[count - at]
        if at == middle - 1:
            up = jnp.concatenate([add(up[:half], left).astype(BF16), up[half:]], axis=0)
            down = jnp.concatenate([down[:half], add(down[half:], right).astype(BF16)], axis=0)
        else:
            up, down = add(up, left).astype(BF16), add(down, right).astype(BF16)
        left = lax.ppermute(up, "dp", ahead)
        right = lax.ppermute(down, "dp", back)
    return add(blocks[0], left) + right.astype(F32)


def scatter_rows(grad):
    size = grad.shape[0] // lax.axis_size("dp")
    return ring_scatter([grad[at : at + size] for at in range(0, grad.shape[0], size)])


def scatter_columns(grad):
    size = grad.shape[1] // lax.axis_size("dp")
    return ring_scatter([grad[:, at : at + size] for at in range(0, grad.shape[1], size)])


def apply_map(moves, state, turned=False):
    return jnp.einsum(
        "hji,hjv->hiv" if turned else "hij,hjv->hiv",
        moves.astype(BF16),
        state.astype(BF16),
        preferred_element_type=F32,
    )


def own_and_swapped(value, bit):
    theirs = swap(jnp.where(bit == 0, value[1], value[0]).astype(BF16), "dp", 1)
    mine = jnp.where(bit == 0, value[0], value[1]).astype(F32)
    theirs = theirs.astype(F32)
    return jnp.where(bit == 0, mine, theirs), jnp.where(bit == 0, theirs, mine)


def hand_back(first, second, bit):
    mine = jnp.where(bit == 0, first, second).astype(BF16)
    theirs = swap(jnp.where(bit == 0, second, first).astype(BF16), "dp", 1)
    return jnp.stack([jnp.where(bit == 0, mine, theirs), jnp.where(bit == 0, theirs, mine)])


def scan_forward(final, value_size):
    bit, pairs = lax.axis_index("dp") % 2, lax.axis_size("dp") // 2
    first, second = own_and_swapped(final, bit)
    first_map, second_map = first[..., value_size:], second[..., value_size:]
    pair_map = apply_map(second_map, first_map)
    pair_sum = apply_map(second_map, first[..., :value_size]) + second[..., :value_size]
    state = jnp.zeros(pair_sum.shape, F32)
    for _ in range(pairs - 1):
        state = from_behind((apply_map(pair_map, state) + pair_sum).astype(BF16), "dp", 2).astype(F32)
    after_first = apply_map(first_map, state) + first[..., :value_size]
    return hand_back(state, after_first, bit), (first_map, second_map, pair_map)


def scan_backward(local, maps):
    bit, pairs = lax.axis_index("dp") % 2, lax.axis_size("dp") // 2
    first_map, second_map, pair_map = maps
    first, second = own_and_swapped(local, bit)
    pair_sum = apply_map(first_map, second, True) + first
    state = jnp.zeros(pair_sum.shape, F32)
    for _ in range(pairs - 1):
        state = from_behind(
            (apply_map(pair_map, state, True) + pair_sum).astype(BF16), "dp", -2
        ).astype(F32)
    before_second = apply_map(second_map, state, True) + second
    return hand_back(before_second, state, bit)


def contract_rows(left, right):
    return lax.dot_general(left, right, TN, preferred_element_type=F32)


def contract_cols(left, right):
    return lax.dot_general(left, right, NT, preferred_element_type=F32)


def norm_backward(grad_in, normed_rows, scale):
    return scale * (grad_in - normed_rows * jnp.mean(grad_in * normed_rows, axis=-1, keepdims=True))


def body(
    tokens,
    out_grad,
    seq_lengths,
    attn_norm,
    query_proj,
    key_proj,
    value_proj,
    gate_proj,
    decay_proj,
    beta_proj,
    conv_query,
    conv_key,
    conv_value,
    log_rate,
    step_bias,
    head_norm,
    out_proj,
    ffn_norm,
    ffn_gate,
    ffn_up,
    ffn_down,
):
    head_rank, ranks = lax.axis_index("head"), lax.axis_size("head")
    heads = decay_proj.shape[1]
    qk_width = query_proj.shape[1]
    v_width = value_proj.shape[1]
    key_size = qk_width // heads
    value_size = v_width // heads
    ffn_width = ffn_gate.shape[1]
    conv_width = 2 * qk_width + v_width
    micros, part_rows, model = tokens.shape
    assert part_rows == CHUNK and micros == 2 and ranks == 4

    decay_pad = jnp.zeros((decay_proj.shape[0], LANES - 2 * heads), decay_proj.dtype)
    w_conv, sent = ring_gather(
        jnp.concatenate(
            [query_proj, key_proj, value_proj, decay_proj, beta_proj, decay_pad], axis=1
        ),
        0,
    )
    gate_shard, out_shard, _ = lax.optimization_barrier((gate_proj, out_proj, sent[:8, :LANES]))
    w_gate, sent = ring_gather(gate_shard, 0)
    w_out, also_sent = ring_gather(out_shard, 1)
    ffn_shard, down_shard, _, _ = lax.optimization_barrier(
        (
            jnp.concatenate([ffn_gate, ffn_up], axis=1),
            ffn_down,
            sent[:8, :LANES],
            also_sent[:8, :LANES],
        )
    )
    w_ffn, _ = ring_gather(ffn_shard, 0)
    w_down, _ = ring_gather(down_shard, 1)

    def of_mine(whole, width):
        return lax.dynamic_slice_in_dim(whole, head_rank * width, width, whole.ndim - 1)

    taps = jnp.concatenate(
        [of_mine(conv_query, qk_width), of_mine(conv_key, qk_width), of_mine(conv_value, v_width)],
        axis=1,
    )
    taps = jnp.pad(taps, ((0, 8 - KCONV), (0, 0)))
    par = jnp.pad(
        jnp.stack([-jnp.exp(of_mine(log_rate, heads)), of_mine(step_bias, heads)]),
        ((0, 6), (0, LANES - heads)),
    )
    gain = jnp.broadcast_to(head_norm, (8, value_size))
    attn_gain, ffn_gain = to_ring(attn_norm), to_ring(ffn_norm)

    def flat(value):
        return value.reshape(-1, value.shape[-1])

    def ranked(value):
        return value.reshape(micros, ranks, part_rows, model)

    residual = to_ring(tokens).astype(F32)
    scale_one = lax.rsqrt(jnp.mean(residual * residual, axis=-1, keepdims=True) + EPSILON)
    normed_one = residual * scale_one
    normed_all = flat(head_gather((normed_one * attn_gain).astype(BF16)))
    cotangent = to_ring(out_grad)
    cotangent_all = flat(head_gather(cotangent))
    first_row = lax.axis_index("dp") * ranks * part_rows
    ends = jnp.cumsum(seq_lengths, axis=1)
    info = jnp.concatenate(
        [
            ends - seq_lengths,
            jnp.full((micros, 1), first_row, jnp.int32),
            jnp.full((micros, 1), head_rank, jnp.int32),
        ],
        axis=1,
    ).astype(jnp.int32)
    mix = Mix(info, micros, ranks, heads, key_size, value_size)
    projected = jnp.dot(normed_all, w_conv, preferred_element_type=F32)
    pre_conv = projected[:, :conv_width].astype(BF16)
    dec = projected[:, conv_width:]
    last_chunk = jnp.bitwise_xor(ranks - 1, head_rank)
    last_rows = lax.dynamic_slice(
        pre_conv.reshape(micros, ranks, part_rows, conv_width),
        (0, last_chunk, part_rows - HALO, 0),
        (micros, 1, HALO, conv_width),
    )[:, 0]
    rim = from_behind(last_rows, "dp", 1)

    plain, carried_map, inverses, starts, final = mix.forward(pre_conv, rim, dec, taps, par)
    incoming, maps = scan_forward(final, value_size)
    gate_lin = jnp.dot(normed_all, w_gate, preferred_element_type=F32)
    mixed, gated = mix.gate_forward(plain, carried_map, incoming, gate_lin, gain)

    mix_part = jnp.dot(gated, w_out, preferred_element_type=F32)
    after_mix = residual + head_scatter(ranked(mix_part))
    scale_two = lax.rsqrt(jnp.mean(after_mix * after_mix, axis=-1, keepdims=True) + EPSILON)
    normed_two = after_mix * scale_two
    ffn_all = flat(head_gather((normed_two * ffn_gain).astype(BF16)))
    gate_ffn = jnp.dot(ffn_all, w_ffn[:, :ffn_width], preferred_element_type=F32)
    up_ffn = jnp.dot(ffn_all, w_ffn[:, ffn_width:], preferred_element_type=F32)
    ffn_sigmoid = jax.nn.sigmoid(gate_ffn)
    ffn_active = gate_ffn * ffn_sigmoid
    hidden = (ffn_active * up_ffn).astype(BF16)

    hidden_grad = contract_cols(cotangent_all, w_down)
    gate_ffn_grad = hidden_grad * up_ffn * ffn_sigmoid * (1.0 + gate_ffn * (1.0 - ffn_sigmoid))
    up_ffn_grad = hidden_grad * ffn_active
    gate_up_grad = jnp.concatenate([gate_ffn_grad, up_ffn_grad], axis=1).astype(BF16)
    ffn_in_part = contract_cols(gate_up_grad, w_ffn)
    ffn_in_grad = head_scatter(ranked(ffn_in_part))
    shard_ffn = scatter_rows(contract_rows(ffn_all, gate_up_grad).astype(BF16))
    shard_down = scatter_columns(contract_rows(hidden, cotangent_all).astype(BF16))
    grad_norm_two = jnp.sum(ffn_in_grad * normed_two, axis=(0, 1))
    after_mix_grad = cotangent.astype(F32) + norm_backward(
        ffn_in_grad * ffn_gain, normed_two, scale_two
    )

    ffn_part = jnp.dot(hidden, w_down, preferred_element_type=F32)
    block_out = (after_mix + head_scatter(ranked(ffn_part))).astype(BF16)

    branch_grad = flat(head_gather(after_mix_grad.astype(BF16)))
    gated_grad = contract_cols(branch_grad, w_out)
    gate_grad, mixed_grad, local_grad, grad_head_norm = mix.gate_backward(
        gated_grad, mixed, carried_map, gate_lin, gain
    )
    shard_out = scatter_columns(contract_rows(gated, branch_grad).astype(BF16))

    leaving = scan_backward(local_grad, maps)
    shard_gate = scatter_rows(contract_rows(normed_all, gate_grad).astype(BF16))
    pre_grad, rim_grad, tail, dec_grad, taps_grad, par_grad = mix.backward(
        pre_conv, rim, dec, taps, par, mixed_grad, inverses, starts, incoming, leaving
    )
    back_rim = from_behind(rim_grad, "dp", -1)
    tail = jnp.concatenate([tail[:, :8], tail[:, 8:] + back_rim], axis=1).astype(BF16)
    pre_grad = lax.dynamic_update_slice(
        pre_grad.reshape(micros, ranks, part_rows, conv_width),
        tail[:, None],
        (0, last_chunk, part_rows - HALO, 0),
    ).reshape(-1, conv_width)

    conv_grad = jnp.concatenate([pre_grad, dec_grad], axis=1)
    shard_conv = scatter_rows(contract_rows(normed_all, conv_grad).astype(BF16))
    normed_part = contract_cols(conv_grad, w_conv) + contract_cols(gate_grad, w_gate)
    normed_grad = head_scatter(ranked(normed_part))
    grad_norm_one = jnp.sum(normed_grad * normed_one, axis=(0, 1))
    input_grad = after_mix_grad + norm_backward(normed_grad * attn_gain, normed_one, scale_one)

    small = jnp.concatenate(
        [
            taps_grad[:KCONV].reshape(-1),
            jnp.pad(par_grad[0, :heads], (0, LANES - heads)),
            jnp.pad(par_grad[1, :heads], (0, LANES - heads)),
            grad_head_norm[0],
            from_ring(grad_norm_one),
            from_ring(grad_norm_two),
        ]
    ).reshape(-1, LANES)
    small = jnp.sum(lax.all_gather(small, "dp"), axis=0)
    small = lax.all_gather(small, "head")
    tap_rows = KCONV * conv_width // LANES
    taps_all = small[:, :tap_rows].reshape(ranks, KCONV, conv_width).transpose(1, 0, 2)

    def joined(low, high):
        return taps_all[:, :, low:high].reshape(KCONV, -1)

    rest = jnp.sum(small[:, tap_rows + 2 :], axis=0).reshape(-1)
    return (
        from_ring(block_out),
        from_ring(input_grad),
        rest[value_size : value_size + model],
        shard_conv[:, :qk_width],
        shard_conv[:, qk_width : 2 * qk_width],
        shard_conv[:, 2 * qk_width : conv_width],
        shard_gate,
        shard_conv[:, conv_width : conv_width + heads],
        shard_conv[:, conv_width + heads : conv_width + 2 * heads],
        joined(0, qk_width),
        joined(qk_width, 2 * qk_width),
        joined(2 * qk_width, conv_width),
        small[:, tap_rows, :heads].reshape(-1),
        small[:, tap_rows + 1, :heads].reshape(-1),
        rest[:value_size],
        shard_out,
        rest[value_size + model :],
        shard_ffn[:, :ffn_width],
        shard_ffn[:, ffn_width:],
        shard_down,
    )


def solution(mesh):
    rows, plane, turned, whole = P(None, ("dp", "head"), None), P("dp", "head"), P("head", "dp"), P()
    in_specs = (rows, rows, whole, whole) + (plane,) * 6 + (whole,) * 6
    in_specs += (turned, whole, plane, plane, turned)
    out_specs = (rows, rows, whole) + (plane,) * 6 + (whole,) * 6
    out_specs += (turned, whole, plane, plane, turned)
    return jax.shard_map(body, mesh=mesh, in_specs=in_specs, out_specs=out_specs, check_vma=False)
```

```python
from functools import partial

import jax
import jax.numpy as jnp
from jax import lax
from jax.experimental import pallas as pl
from jax.experimental.pallas import tpu as pltpu
from jax.sharding import PartitionSpec as P

CHUNK = 128
KCONV = 4
LANES = 128
HALO = 16

EPSILON = 1e-06
HEAD_FLOOR = 0.01
F32 = jnp.float32
BF16 = jnp.bfloat16
NN = (((1,), (0,)), ((), ()))
NT = (((1,), (1,)), ((), ()))
TN = (((0,), (0,)), ((), ()))


def mm(left, right, dims=NN):
    return lax.dot_general(
        left.astype(BF16), right.astype(BF16), dims, preferred_element_type=F32
    )


def split(value):
    high = value.astype(BF16)
    return high, (value - high.astype(F32)).astype(BF16)


def mm3(left, right, dims=NN):
    left_high, left_low = split(left)
    right_high, right_low = split(right)
    return mm(left_high, right_high, dims) + (
        mm(left_high, right_low, dims) + mm(left_low, right_high, dims)
    )


def chunk_places(info_ref, micro, chunk, seq_count):
    first = info_ref[micro, seq_count] + chunk * CHUNK
    starts = [info_ref[micro, at] for at in range(seq_count)]
    rows = first + lax.broadcasted_iota(jnp.int32, (CHUNK, 1), 0)
    lanes = first + lax.broadcasted_iota(jnp.int32, (1, CHUNK), 1)
    seg_col = jnp.zeros((CHUNK, 1), jnp.int32)
    seg_row = jnp.zeros((1, CHUNK), jnp.int32)
    begun = jnp.zeros((CHUNK, 1), jnp.int32)
    seg_before = jnp.int32(0)
    seg_last = jnp.int32(0)
    for start in starts:
        seg_col = seg_col + jnp.where(rows >= start, 1, 0)
        seg_row = seg_row + jnp.where(lanes >= start, 1, 0)
        begun = jnp.maximum(begun, jnp.where(rows >= start, start, 0))
        seg_before = seg_before + jnp.where(first - 1 >= start, 1, 0)
        seg_last = seg_last + jnp.where(first + CHUNK - 1 >= start, 1, 0)
    offset = rows - begun
    row_ids = lax.broadcasted_iota(jnp.int32, (CHUNK, CHUNK), 0)
    col_ids = lax.broadcasted_iota(jnp.int32, (CHUNK, CHUNK), 1)
    same = seg_col == seg_row
    return dict(
        row_ids=row_ids,
        col_ids=col_ids,
        inclusive=jnp.logical_and(row_ids >= col_ids, same),
        strictly=jnp.logical_and(row_ids > col_ids, same),
        untouched=jnp.where(seg_col == seg_before, 1.0, 0.0).astype(F32),
        with_last=jnp.where(seg_col == seg_last, 1.0, 0.0).astype(F32),
        lags=[jnp.where(offset >= lag, 1.0, 0.0).astype(F32) for lag in range(1, KCONV)],
    )


def decay_parts(g_col, places):
    row_ids, col_ids = places["row_ids"], places["col_ids"]
    cum_row = jnp.sum(jnp.where(row_ids <= col_ids, g_col, 0.0), axis=0, keepdims=True)
    cum_col = jnp.sum(jnp.where(row_ids == col_ids, cum_row, 0.0), axis=1, keepdims=True)
    spread = jnp.where(places["inclusive"], cum_col - cum_row, 0.0)
    pair = jnp.where(places["inclusive"], jnp.exp(spread), 0.0)
    carry = jnp.exp(cum_col) * places["untouched"]
    cum_last = cum_col[CHUNK - 1 :, :]
    to_last = jnp.exp(jnp.minimum(cum_last - cum_col, 0.0)) * places["with_last"]
    return pair, carry, to_last, carry[CHUNK - 1 :, :]


def conv_rows(extended, taps, lags):
    total = taps[KCONV - 1 :, :] * extended[HALO:]
    for lag in range(1, KCONV):
        shifted = extended[HALO - lag : HALO - lag + CHUNK]
        total = total + taps[KCONV - 1 - lag : KCONV - lag, :] * shifted * lags[lag - 1]
    return total


def head_columns(head, heads, key_size, value_size):
    return (
        (head * key_size, key_size),
        ((heads + head) * key_size, key_size),
        (2 * heads * key_size + head * value_size, value_size),
    )


def unit_rows(active):
    return active * lax.rsqrt(jnp.sum(active * active, axis=1, keepdims=True) + EPSILON)


def softplus(value):
    return jnp.maximum(value, 0.0) + jnp.log1p(jnp.exp(-jnp.abs(value)))


def unit_lower_inverses(systems, places):
    row_ids, col_ids = places["row_ids"], places["col_ids"]
    eye = jnp.where(row_ids == col_ids, 1.0, 0.0).astype(F32)
    pairs = jnp.right_shift(row_ids, 1) == jnp.right_shift(col_ids, 1)
    found = [eye - jnp.where(pairs, system, 0.0) for system in systems]
    level = 1
    while (1 << level) < CHUNK:
        row_block = jnp.right_shift(row_ids, level)
        col_block = jnp.right_shift(col_ids, level)
        lower = jnp.logical_and(
            jnp.right_shift(row_block, 1) == jnp.right_shift(col_block, 1), row_block > col_block
        )
        inner = [
            INVERSE_MM(jnp.where(lower, system, 0.0), inverse)
            for system, inverse in zip(systems, found)
        ]
        found = [
            inverse - INVERSE_MM(inverse, middle) for inverse, middle in zip(found, inner)
        ]
        level += 1
    return found


INVERSE_MM = mm3


def mix_forward_kernel(
    info_ref,
    x_ref,
    rim_ref,
    taps_ref,
    par_ref,
    out_ref,
    cmap_ref,
    inv_ref,
    start_ref,
    final_ref,
    halo,
    state,
    *,
    heads,
    key_size,
    value_size,
    seq_count,
):
    micro, chunk = pl.program_id(0), pl.program_id(1)
    span = range(heads)

    width = halo.shape[1]

    @pl.when(chunk == 0)
    def _():
        halo[...] = rim_ref[:, :width].astype(BF16)
        row_ids = lax.broadcasted_iota(jnp.int32, (key_size, key_size), 0)
        col_ids = lax.broadcasted_iota(jnp.int32, (key_size, key_size), 1)
        eye = jnp.where(row_ids == col_ids, 1.0, 0.0).astype(F32)
        for head in span:
            state[head] = jnp.concatenate([jnp.zeros((key_size, value_size), F32), eye], axis=1)

    places = chunk_places(info_ref, micro, chunk, seq_count)
    dec = x_ref[:, width:]
    beta_all = jax.nn.sigmoid(dec)
    g_all = par_ref[0:1, :] * softplus(dec + par_ref[1:2, :])
    scale = key_size**-0.5

    queries, keys, values = [], [], []
    for head in span:
        rows = []
        for begin, size in head_columns(head, heads, key_size, value_size):
            cut = slice(begin, begin + size)
            extended = jnp.concatenate(
                [halo[:, cut].astype(F32), x_ref[:, cut].astype(BF16).astype(F32)], axis=0
            )
            summed = conv_rows(extended, taps_ref[0:KCONV, cut], places["lags"])
            rows.append(summed * jax.nn.sigmoid(summed))
        queries.append(unit_rows(rows[0]) * scale)
        keys.append(unit_rows(rows[1]))
        values.append(rows[2])
    halo[...] = x_ref[CHUNK - HALO :, :width].astype(BF16)

    betas = [beta_all[:, heads + head : heads + head + 1] for head in span]
    decays = [decay_parts(g_all[:, head : head + 1], places) for head in span]
    grams = [mm(keys[head], keys[head], NT) for head in span]
    systems = [
        jnp.where(places["strictly"], betas[head] * decays[head][0] * grams[head], 0.0)
        for head in span
    ]
    inverses = unit_lower_inverses(systems, places)
    attends = [mm(queries[head], keys[head], NT) * decays[head][0] for head in span]
    solved = [
        mm(
            inverses[head],
            jnp.concatenate(
                [betas[head] * values[head], betas[head] * decays[head][1] * keys[head]], axis=1
            ),
        )
        for head in span
    ]
    starts = [state[head] for head in span]
    written = [
        jnp.concatenate(
            [solved[head][:, :value_size], jnp.zeros((CHUNK, key_size), F32)], axis=1
        )
        - mm(solved[head][:, value_size:], starts[head])
        for head in span
    ]
    outs = [
        decays[head][1] * mm(queries[head], starts[head]) + mm(attends[head], written[head])
        for head in span
    ]
    for head in span:
        _, _, to_last, carry_last = decays[head]
        inv_ref[0, head] = inverses[head].astype(BF16)
        start_ref[0, head] = starts[head].astype(BF16)
        out_ref[:, head * value_size : (head + 1) * value_size] = outs[head][:, :value_size]
        cmap_ref[:, head * key_size : (head + 1) * key_size] = outs[head][:, value_size:].astype(
            BF16
        )
        state[head] = carry_last * starts[head] + mm(to_last * keys[head], written[head], TN)

    @pl.when(chunk == pl.num_programs(1) - 1)
    def _():
        final_ref[0] = state[...]


def mix_backward_kernel(
    info_ref,
    x_ref,
    before_ref,
    rim_ref,
    taps_ref,
    par_ref,
    grad_ref,
    inv_ref,
    start_ref,
    incoming_ref,
    leaving_ref,
    dx_ref,
    rim_grad_ref,
    tail_ref,
    dtaps_ref,
    dpar_ref,
    carry,
    dstate,
    *,
    heads,
    key_size,
    value_size,
    seq_count,
):
    micro, step = pl.program_id(0), pl.program_id(1)
    chunk = pl.num_programs(1) - 1 - step
    span = range(heads)
    width = carry.shape[1]

    @pl.when(step == 0)
    def _():
        carry[...] = jnp.zeros_like(carry)
        dstate[...] = leaving_ref[0].astype(F32)

    @pl.when(jnp.logical_and(micro == 0, step == 0))
    def _():
        dtaps_ref[...] = jnp.zeros_like(dtaps_ref)
        dpar_ref[...] = jnp.zeros_like(dpar_ref)

    places = chunk_places(info_ref, micro, chunk, seq_count)
    row_ids, col_ids = places["row_ids"], places["col_ids"]
    lags = places["lags"]
    dec = x_ref[:, width:]
    beta_all = jax.nn.sigmoid(dec)
    shifted_dec = dec + par_ref[1:2, :]
    g_all = par_ref[0:1, :] * softplus(shifted_dec)
    scale = key_size**-0.5
    opening = jnp.where(chunk == 0, rim_ref[:, :width], before_ref[:, :width])
    opening = opening.astype(BF16).astype(F32)

    def extended_rows(cut):
        return jnp.concatenate(
            [opening[:, cut], x_ref[:, cut].astype(BF16).astype(F32)], axis=0
        )

    sums, norms, unit = [], [], []
    for head in span:
        mine = [
            conv_rows(
                extended_rows(slice(begin, begin + size)),
                taps_ref[0:KCONV, begin : begin + size],
                lags,
            )
            for begin, size in head_columns(head, heads, key_size, value_size)
        ]
        active = [value * jax.nn.sigmoid(value) for value in mine]
        inverse_norms = [
            lax.rsqrt(jnp.sum(value * value, axis=1, keepdims=True) + EPSILON)
            for value in active[:2]
        ]
        sums.append(mine)
        norms.append(inverse_norms)
        unit.append([active[0] * inverse_norms[0], active[1] * inverse_norms[1], active[2]])
    keys = [unit[head][1] for head in span]
    key_low = [keys[head].astype(BF16) for head in span]
    query_low = [(unit[head][0] * scale).astype(BF16) for head in span]
    betas = [beta_all[:, heads + head : heads + head + 1] for head in span]
    decays = [decay_parts(g_all[:, head : head + 1], places) for head in span]
    grams = [mm(key_low[head], key_low[head], NT) for head in span]
    products = [mm(query_low[head], key_low[head], NT) for head in span]
    attends = [(products[head] * decays[head][0]).astype(BF16) for head in span]
    starts = []
    for head in span:
        saved = start_ref[0, head]
        starts.append(
            saved[:, :value_size].astype(F32)
            + mm(saved[:, value_size:], incoming_ref[0, head])
        )
    start_low = [starts[head].astype(BF16) for head in span]
    key_state = [mm(key_low[head], start_low[head]) for head in span]
    query_state = [mm(query_low[head], start_low[head]) for head in span]
    grads = [grad_ref[:, head * value_size : (head + 1) * value_size] for head in span]
    grad_low = [grads[head].astype(BF16) for head in span]
    residues = [unit[head][2] - decays[head][1] * key_state[head] for head in span]
    inverses = [inv_ref[0, head] for head in span]
    written = [mm(inverses[head], betas[head] * residues[head]).astype(BF16) for head in span]
    ahead = [dstate[head] for head in span]
    ahead_low = [ahead[head].astype(BF16) for head in span]
    key_last = [(decays[head][2] * keys[head]).astype(BF16) for head in span]
    dwritten = [
        mm(attends[head], grad_low[head], TN) + mm(key_last[head], ahead_low[head])
        for head in span
    ]
    dresidue = [mm(inverses[head], dwritten[head], TN) for head in span]
    dresidue_low = [dresidue[head].astype(BF16) for head in span]
    dattend = [
        jnp.where(places["inclusive"], mm(grad_low[head], written[head], NT), 0.0)
        for head in span
    ]
    dsystem = [
        jnp.where(places["strictly"], -mm(dresidue_low[head], written[head], NT), 0.0)
        for head in span
    ]
    dproducts = [(dattend[head] * decays[head][0]).astype(BF16) for head in span]
    dcarried = [decays[head][1] * grads[head] for head in span]
    dcarried_low = [dcarried[head].astype(BF16) for head in span]
    dkey_state = [-(betas[head] * decays[head][1]) * dresidue[head] for head in span]
    dkey_state_low = [dkey_state[head].astype(BF16) for head in span]
    dkey_last = [mm(written[head], ahead_low[head], NT) for head in span]
    dgram = [dsystem[head] * betas[head] * decays[head][0] for head in span]
    dgram_low = [dgram[head].astype(BF16) for head in span]
    dquery = [
        mm(dcarried_low[head], start_low[head], NT) + mm(dproducts[head], key_low[head])
        for head in span
    ]
    dkey = [
        mm(dproducts[head], query_low[head], TN)
        + decays[head][2] * dkey_last[head]
        + mm(dkey_state_low[head], start_low[head], NT)
        + mm(dgram_low[head], key_low[head])
        + mm(dgram_low[head], key_low[head], TN)
        for head in span
    ]
    lane_ids = lax.broadcasted_iota(jnp.int32, (CHUNK, LANES), 1)
    ddec = jnp.zeros((CHUNK, LANES), F32)
    dg_all = jnp.zeros((CHUNK, LANES), F32)
    for head in span:
        pair, carried, to_last, carry_last = decays[head]
        coupled = dsystem[head] * grams[head]
        dpair = (dattend[head] * products[head] + coupled * betas[head]) * pair
        dbeta = jnp.sum(coupled * pair, axis=1, keepdims=True) + jnp.sum(
            dresidue[head] * residues[head], axis=1, keepdims=True
        )
        dcarry = jnp.sum(
            grads[head] * query_state[head] - betas[head] * dresidue[head] * key_state[head],
            axis=1,
            keepdims=True,
        )
        dcarry_last = jnp.sum(
            jnp.sum(ahead[head] * starts[head], axis=1, keepdims=True), axis=0, keepdims=True
        )
        dto_last = jnp.sum(dkey_last[head] * keys[head], axis=1, keepdims=True) * to_last
        is_last = lax.broadcasted_iota(jnp.int32, (CHUNK, 1), 0) == CHUNK - 1
        dcum_col = (
            jnp.sum(dpair, axis=1, keepdims=True)
            + dcarry * carried
            - dto_last
            + jnp.where(
                is_last,
                dcarry_last * carry_last + jnp.sum(dto_last, axis=0, keepdims=True),
                0.0,
            )
        )
        dcum_row = jnp.sum(
            jnp.where(row_ids == col_ids, dcum_col, 0.0) - dpair, axis=0, keepdims=True
        )
        dg = jnp.sum(jnp.where(col_ids >= row_ids, dcum_row, 0.0), axis=1, keepdims=True)
        beta = betas[head]
        dg_all = jnp.where(lane_ids == head, dg, dg_all)
        ddec = jnp.where(lane_ids == heads + head, dbeta * beta * (1.0 - beta), ddec)
        dstate[head] = (
            carry_last * ahead[head]
            + mm(query_low[head], dcarried_low[head], TN)
            + mm(key_low[head], dkey_state_low[head], TN)
        )
    dstep = dg_all * par_ref[0:1, :] * jax.nn.sigmoid(shifted_dec)
    ddec = ddec + dstep
    dx_ref[:, width:] = ddec.astype(BF16)
    dpar_ref[0:1, :] += jnp.sum(dg_all * g_all, axis=0, keepdims=True)
    dpar_ref[1:2, :] += jnp.sum(dstep, axis=0, keepdims=True)

    for head in span:
        dunit = [dquery[head] * scale, dkey[head]]
        dactive = [
            norms[head][at]
            * (
                dunit[at]
                - unit[head][at] * jnp.sum(dunit[at] * unit[head][at], axis=1, keepdims=True)
            )
            for at in range(2)
        ]
        dactive.append(betas[head] * dresidue[head])
        for at, (begin, size) in enumerate(head_columns(head, heads, key_size, value_size)):
            cut = slice(begin, begin + size)
            sig = jax.nn.sigmoid(sums[head][at])
            dsum = dactive[at] * sig * (1.0 + sums[head][at] * (1.0 - sig))
            extended = extended_rows(cut)
            taps = taps_ref[0:KCONV, cut]
            zeros = jnp.zeros((8, size), F32)
            dtaps_ref[KCONV - 1 : KCONV, cut] += jnp.sum(
                dsum * extended[HALO:], axis=0, keepdims=True
            )
            total = jnp.concatenate([zeros, taps[KCONV - 1 :, :] * dsum], axis=0)
            for lag in range(1, KCONV):
                masked = dsum * lags[lag - 1]
                at_tap = KCONV - 1 - lag
                dtaps_ref[at_tap : at_tap + 1, cut] += jnp.sum(
                    masked * extended[HALO - lag : HALO - lag + CHUNK], axis=0, keepdims=True
                )
                padded = jnp.concatenate(
                    [zeros, taps[at_tap : at_tap + 1, :] * masked, zeros], axis=0
                )
                total = total + padded[lag : lag + 8 + CHUNK]
            body_rows = jnp.concatenate(
                [total[8:CHUNK], total[CHUNK:] + carry[:, cut]], axis=0
            )
            dx_ref[:, cut] = body_rows.astype(BF16)
            carry[:, cut] = total[:8]

            @pl.when(step == 0)
            def _():
                tail_ref[0, :, cut] = body_rows[CHUNK - HALO :]

    @pl.when(chunk == 0)
    def _():
        rim_grad_ref[0] = carry[...]


def gate_forward_kernel(
    info_ref, plain_ref, cmap_ref, incoming_ref, gate_ref, gain_ref, mixed_ref, gated_ref, *, heads, key_size, value_size
):
    for head in range(heads):
        cut = slice(head * value_size, (head + 1) * value_size)
        mixed = plain_ref[:, cut] + mm(
            cmap_ref[:, head * key_size : (head + 1) * key_size], incoming_ref[0, head]
        )
        mixed_ref[:, cut] = mixed
        normed = mixed * lax.rsqrt(
            jnp.mean(mixed * mixed, axis=1, keepdims=True) + HEAD_FLOOR
        )
        gate = gate_ref[:, cut]
        gated_ref[:, cut] = (normed * gain_ref[0:1, :] * gate * jax.nn.sigmoid(gate)).astype(BF16)


def gate_backward_kernel(
    info_ref,
    grad_ref,
    mixed_ref,
    cmap_ref,
    gate_ref,
    gain_ref,
    dgate_ref,
    dmixed_ref,
    dlocal_ref,
    dgain_ref,
    *,
    heads,
    key_size,
    value_size,
):
    micro, step = pl.program_id(0), pl.program_id(1)

    @pl.when(step == 0)
    def _():
        dlocal_ref[...] = jnp.zeros_like(dlocal_ref)

    @pl.when(jnp.logical_and(micro == 0, step == 0))
    def _():
        dgain_ref[...] = jnp.zeros_like(dgain_ref)

    gain = gain_ref[0:1, :]
    for head in range(heads):
        cut = slice(head * value_size, (head + 1) * value_size)
        mixed = mixed_ref[:, cut]
        scale = lax.rsqrt(jnp.mean(mixed * mixed, axis=1, keepdims=True) + HEAD_FLOOR)
        normed = mixed * scale
        gate = gate_ref[:, cut]
        sig = jax.nn.sigmoid(gate)
        active = gate * sig
        grad = grad_ref[:, cut]
        by_norm = grad * normed
        dgain_ref[0:1, :] += jnp.sum(by_norm * active, axis=0, keepdims=True)
        dgate_ref[:, cut] = (by_norm * gain * sig * (1.0 + gate * (1.0 - sig))).astype(BF16)
        dnormed = grad * gain * active
        dmixed = scale * (dnormed - normed * jnp.mean(dnormed * normed, axis=1, keepdims=True))
        dmixed_ref[:, cut] = dmixed
        dlocal_ref[0, head] += mm(
            cmap_ref[:, head * key_size : (head + 1) * key_size], dmixed, TN
        )


VMEM_BYTES = 48 * 1024 * 1024
PIECES = 4


def kernel_call(
    kernel, info, arrays, grid, in_specs, out_specs, out_shape, scratch, name, after=(), **sizes
):
    count = 1 + len(arrays)

    def body(*refs):
        kernel(*refs[:count], *refs[count + len(after) :], **sizes)

    return pl.pallas_call(
        body,
        grid_spec=pltpu.PrefetchScalarGridSpec(
            num_scalar_prefetch=1,
            grid=grid,
            in_specs=list(in_specs) + [pl.BlockSpec(memory_space=pl.ANY)] * len(after),
            out_specs=out_specs,
            scratch_shapes=scratch,
        ),
        out_shape=out_shape,
        compiler_params=pltpu.CompilerParams(
            dimension_semantics=("arbitrary",) * len(grid), vmem_limit_bytes=VMEM_BYTES
        ),
        name=name,
    )(info, *arrays, *after)


def tie(value, *earlier):
    if not earlier:
        return value
    return pl.pallas_call(
        lambda *refs: None,
        out_shape=jax.ShapeDtypeStruct(value.shape, value.dtype),
        in_specs=[pl.BlockSpec(memory_space=pl.ANY)] * (1 + len(earlier)),
        out_specs=pl.BlockSpec(memory_space=pl.ANY),
        input_output_aliases={0: 0},
        name="tie",
    )(value, *earlier)


ANYWHERE = pl.BlockSpec(memory_space=pl.ANY)


def assemble(plan, arrays, after=()):
    count = len(arrays)
    steps = [(out, *part) for out, (_, parts) in enumerate(plan) for part in parts]

    def kernel(*refs):
        targets = refs[count + len(after) :][: len(plan)]
        held = refs[count + len(after) + len(plan) : -2]
        into, back = refs[-2:]

        def place(buffers, out, rows, columns, row, column):
            return buffers[out].at[
                row : row + rows[1] - rows[0], column : column + columns[1] - columns[0]
            ]

        loads, stores = [], []
        for at, (out, which, rows, columns, row, column) in enumerate(steps):
            source = refs[which].at[rows[0] : rows[1], columns[0] : columns[1]]
            target = place(held, out, rows, columns, row, column)
            loads.append(pltpu.make_async_copy(source, target, into.at[at]))
            loads[-1].start()
        for at, (out, _, rows, columns, row, column) in enumerate(steps):
            loads[at].wait()
            source = place(held, out, rows, columns, row, column)
            target = place(targets, out, rows, columns, row, column)
            stores.append(pltpu.make_async_copy(source, target, back.at[at]))
            stores[-1].start()
        for store in stores:
            store.wait()

    return pl.pallas_call(
        kernel,
        out_shape=[jax.ShapeDtypeStruct(shape, arrays[0].dtype) for shape, _ in plan],
        in_specs=[ANYWHERE] * (count + len(after)),
        out_specs=[ANYWHERE] * len(plan),
        scratch_shapes=[pltpu.VMEM(shape, arrays[0].dtype) for shape, _ in plan]
        + [pltpu.SemaphoreType.DMA((len(steps),))] * 2,
        compiler_params=pltpu.CompilerParams(vmem_limit_bytes=VMEM_BYTES),
        name="assemble",
    )(*arrays, *after)


def stacked(arrays, after=()):
    rows, parts = 0, []
    for at, array in enumerate(arrays):
        parts.append((at, (0, array.shape[0]), (0, array.shape[1]), rows, 0))
        rows += array.shape[0]
    return assemble([((rows, arrays[0].shape[1]), parts)], arrays, after)[0]


def ring_add(ups, downs, left, right, partly, after=()):
    count = len(ups)
    total = sum(grad.shape[1] for grad, _ in ups)
    tile = left.shape[0] if partly else left.shape[0] // 2

    def kernel(*refs):
        mine_up, mine_down = refs[:count], refs[count : 2 * count]
        came_up, came_down = refs[2 * count : 2 * count + 2]
        out_up, out_down = refs[-2:]
        step = pl.program_id(0)
        column = 0
        for up, down in zip(mine_up, mine_down):
            cut = slice(column, column + up.shape[1])
            column += up.shape[1]
            for mine, came, out, when in ((up, came_up, out_up, 0), (down, came_down, out_down, 1)):

                def add(mine=mine, came=came, out=out, cut=cut):
                    out[:, cut] = (mine[...].astype(F32) + came[:, cut].astype(F32)).astype(BF16)

                def keep(mine=mine, out=out, cut=cut):
                    out[:, cut] = mine[...]

                if partly:
                    pl.when(step == when)(add)
                    pl.when(step != when)(keep)
                else:
                    add()

    def of_block(grad, at):
        return pl.BlockSpec((tile, grad.shape[1]), lambda i: (2 * at + i, 0))

    came = pl.BlockSpec((tile, total), lambda i: (0 if partly else i, 0))
    out = pl.BlockSpec((tile, total), lambda i: (i, 0))
    shape = jax.ShapeDtypeStruct((2 * tile, total), BF16)
    return pl.pallas_call(
        kernel,
        grid=(2,),
        out_shape=[shape, shape],
        in_specs=[of_block(*block) for block in ups]
        + [of_block(*block) for block in downs]
        + [came, came]
        + [ANYWHERE] * len(after),
        out_specs=[out, out],
        compiler_params=pltpu.CompilerParams(
            dimension_semantics=("arbitrary",), vmem_limit_bytes=VMEM_BYTES
        ),
        name="ring_add",
    )(*[grad for grad, _ in ups], *[grad for grad, _ in downs], left, right, *after)


def row_blocks(left, right, blocks, count, after=()):
    size = left.shape[1] // count

    def kernel(left_ref, right_ref, *refs):
        refs[-1][...] = lax.dot_general(
            left_ref[...], right_ref[...], TN, preferred_element_type=F32
        ).astype(BF16)

    def block(i):
        found = blocks[0]
        for at, wanted in enumerate(blocks[1:], 1):
            found = jnp.where(i >= at, wanted, found)
        return 0, found

    return pl.pallas_call(
        kernel,
        grid=(len(blocks),),
        in_specs=[
            pl.BlockSpec((left.shape[0], size), block),
            pl.BlockSpec(right.shape, lambda i: (0, 0)),
        ]
        + [ANYWHERE] * len(after),
        out_specs=pl.BlockSpec((size, right.shape[1]), lambda i: (i, 0)),
        out_shape=jax.ShapeDtypeStruct((len(blocks) * size, right.shape[1]), BF16),
        compiler_params=pltpu.CompilerParams(
            dimension_semantics=("arbitrary",), vmem_limit_bytes=VMEM_BYTES
        ),
        name="row_blocks",
    )(left, right, *after)


def matmul(pairs, dims, dtype, after=(), pieces=0):
    if dims == NT:
        rows, columns = pairs[0][0].shape[0], pairs[0][1].shape[0]
        tile = 512 if columns % 512 == 0 else columns
        grid, pick = columns // tile, lambda i: (0, i)
        specs = [
            (pl.BlockSpec(left.shape, lambda i: (0, 0)),
             pl.BlockSpec((tile, right.shape[1]), lambda i: (i, 0)))
            for left, right in pairs
        ]
        shape = (rows, tile)
    else:
        over = 1 if dims == TN else 0
        rows, columns = pairs[0][0].shape[over], pairs[0][1].shape[1]
        tile = 256
        grid, pick = rows // tile, lambda i: (i, 0)
        specs = [
            (pl.BlockSpec((left.shape[0], tile), lambda i: (0, i)) if dims == TN
             else pl.BlockSpec((tile, left.shape[1]), lambda i: (i, 0)),
             pl.BlockSpec(right.shape, lambda i: (0, 0)))
            for left, right in pairs
        ]
        shape = (tile, columns)
    count = 2 * len(pairs)
    half = rows // 2

    def kernel(*refs):
        total = None
        for at in range(0, count, 2):
            product = lax.dot_general(
                refs[at][...], refs[at + 1][...], dims, preferred_element_type=F32
            )
            total = product if total is None else total + product
        outs = refs[count + len(after) :]
        if pieces:
            outs[0][...] = total[:half].astype(dtype)
            for at in range(pieces):
                first = half + at * (half // pieces)
                outs[1 + at][...] = total[first : first + half // pieces].astype(dtype)
        else:
            outs[0][...] = total.astype(dtype)

    if pieces:
        heights = [half] + [half // pieces] * pieces
        out_specs = [pl.BlockSpec((height, tile), pick) for height in heights]
        out_shape = [jax.ShapeDtypeStruct((height, columns), dtype) for height in heights]
    else:
        out_specs = [pl.BlockSpec(shape, pick)]
        out_shape = [jax.ShapeDtypeStruct((rows, columns), dtype)]
    found = pl.pallas_call(
        kernel,
        grid=(grid,),
        in_specs=[spec for both in specs for spec in both] + [ANYWHERE] * len(after),
        out_specs=out_specs,
        out_shape=out_shape,
        compiler_params=pltpu.CompilerParams(
            dimension_semantics=("arbitrary",), vmem_limit_bytes=VMEM_BYTES
        ),
        name="matmul",
    )(*[array for both in pairs for array in both], *after)
    return found if pieces else found[0]


def project(rows, rim, weights, after=()):
    tile = 256

    def kernel(rows_ref, rim_ref, weights_ref, *refs):
        out, out_rim = refs[-2:]
        out[...] = jnp.dot(rows_ref[...], weights_ref[...], preferred_element_type=F32)

        @pl.when(pl.program_id(0) == 0)
        def _():
            out_rim[...] = jnp.dot(rim_ref[...], weights_ref[...], preferred_element_type=F32)

    columns = weights.shape[1]
    return pl.pallas_call(
        kernel,
        grid=(rows.shape[0] // tile,),
        in_specs=[
            pl.BlockSpec((tile, rows.shape[1]), lambda i: (i, 0)),
            pl.BlockSpec(rim.shape, lambda i: (0, 0)),
            pl.BlockSpec(weights.shape, lambda i: (0, 0)),
        ]
        + [ANYWHERE] * len(after),
        out_specs=[
            pl.BlockSpec((tile, columns), lambda i: (i, 0)),
            pl.BlockSpec((rim.shape[0], columns), lambda i: (0, 0)),
        ],
        out_shape=[
            jax.ShapeDtypeStruct((rows.shape[0], columns), F32),
            jax.ShapeDtypeStruct((rim.shape[0], columns), F32),
        ],
        compiler_params=pltpu.CompilerParams(
            dimension_semantics=("arbitrary",), vmem_limit_bytes=VMEM_BYTES
        ),
        name="project",
    )(rows, rim, weights, *after)


def feed_forward(rows, cotangent, w_ffn, w_down, after=()):
    tile = 256
    model, width = w_down.shape

    def kernel(rows_ref, cotangent_ref, ffn_ref, down_ref, *refs):
        hidden_ref, grad_ref = refs[-2:]
        gate = jnp.dot(rows_ref[...], ffn_ref[:, :width], preferred_element_type=F32)
        up = jnp.dot(rows_ref[...], ffn_ref[:, width:], preferred_element_type=F32)
        grad = jnp.dot(cotangent_ref[...], down_ref[...], preferred_element_type=F32)
        sig = jax.nn.sigmoid(gate)
        active = gate * sig
        hidden_ref[...] = (active * up).astype(BF16)
        grad_ref[:, :width] = (grad * up * sig * (1.0 + gate * (1.0 - sig))).astype(BF16)
        grad_ref[:, width:] = (grad * active).astype(BF16)

    def by_rows(columns):
        return pl.BlockSpec((tile, columns), lambda i: (i, 0))

    def once(array):
        return pl.BlockSpec(array.shape, lambda i: (0, 0), pipeline_mode=pl.Buffered(1))

    return pl.pallas_call(
        kernel,
        grid=(rows.shape[0] // tile,),
        in_specs=[by_rows(model), by_rows(model), once(w_ffn), once(w_down)]
        + [ANYWHERE] * len(after),
        out_specs=[by_rows(width), by_rows(2 * width)],
        out_shape=[
            jax.ShapeDtypeStruct((rows.shape[0], width), BF16),
            jax.ShapeDtypeStruct((rows.shape[0], 2 * width), BF16),
        ],
        compiler_params=pltpu.CompilerParams(
            dimension_semantics=("arbitrary",), vmem_limit_bytes=VMEM_BYTES
        ),
        name="feed_forward",
    )(rows, cotangent, w_ffn, w_down, *after)


class Mix:
    def __init__(self, info, micros, chunks, heads, key_size, value_size):
        self.info, self.micros, self.chunks = info, micros, chunks
        self.heads, self.key_size, self.value_size = heads, key_size, value_size
        self.width = heads * (2 * key_size + value_size)
        self.wide = key_size + value_size
        self.rows = micros * chunks * CHUNK
        self.sizes = dict(heads=heads, key_size=key_size, value_size=value_size)

    def block(self, m, c, info):
        return rank_block(c, info[0, info.shape[1] - 1]) * self.micros + m

    def by_rows(self, columns, turned=False):
        def place(m, c, info):
            return self.block(m, self.chunks - 1 - c if turned else c, info), 0

        return pl.BlockSpec((CHUNK, columns), place)

    def by_chunk(self, rows, columns, turned=False):
        def place(m, c, info):
            return m * self.chunks + (self.chunks - 1 - c if turned else c), 0, 0, 0

        return pl.BlockSpec((1, self.heads, rows, columns), place)

    def by_micro(self, *dims):
        return pl.BlockSpec((1,) + dims, lambda m, c, info: (m,) + (0,) * len(dims))

    def whole(self, *dims):
        return pl.BlockSpec(dims, lambda m, c, info: (0,) * len(dims))

    def like(self, dtype, *dims):
        return jax.ShapeDtypeStruct(dims, dtype)

    def call(self, kernel, arrays, in_specs, outs, scratch, name, after, **more):
        return kernel_call(
            kernel,
            self.info,
            arrays,
            (self.micros, self.chunks),
            in_specs,
            [spec for spec, _ in outs],
            [shape for _, shape in outs],
            scratch,
            name,
            after,
            **self.sizes,
            **more,
        )

    def forward(self, projected, rim, taps, par, after=()):
        h, dk, dv, wide, width = self.heads, self.key_size, self.value_size, self.wide, self.width
        steps = self.micros * self.chunks
        return self.call(
            mix_forward_kernel,
            (projected, rim, taps, par),
            [
                self.by_rows(width + LANES),
                pl.BlockSpec((HALO, width + LANES), lambda m, c, info: (m, 0)),
                self.whole(8, width),
                self.whole(8, LANES),
            ],
            [
                (self.by_rows(h * dv), self.like(F32, self.rows, h * dv)),
                (self.by_rows(h * dk), self.like(BF16, self.rows, h * dk)),
                (self.by_chunk(CHUNK, CHUNK), self.like(BF16, steps, h, CHUNK, CHUNK)),
                (self.by_chunk(dk, wide), self.like(BF16, steps, h, dk, wide)),
                (self.by_micro(h, dk, wide), self.like(F32, self.micros, h, dk, wide)),
            ],
            [pltpu.VMEM((HALO, width), BF16), pltpu.VMEM((h, dk, wide), F32)],
            "mix_forward",
            after,
            seq_count=self.info.shape[1] - 2,
        )

    def backward(
        self, projected, rim, taps, par, grad, inverses, starts, incoming, leaving, after=()
    ):
        h, dk, dv, wide, width = self.heads, self.key_size, self.value_size, self.wide, self.width
        halo_blocks = CHUNK // HALO

        def before(m, c, info):
            earlier = jnp.maximum(self.chunks - 2 - c, 0)
            return (self.block(m, earlier, info) + 1) * halo_blocks - 1, 0

        return self.call(
            mix_backward_kernel,
            (projected, projected, rim, taps, par, grad, inverses, starts, incoming, leaving),
            [
                self.by_rows(width + LANES, True),
                pl.BlockSpec((HALO, width + LANES), before),
                pl.BlockSpec((HALO, width + LANES), lambda m, c, info: (m, 0)),
                self.whole(8, width),
                self.whole(8, LANES),
                self.by_rows(h * dv, True),
                self.by_chunk(CHUNK, CHUNK, True),
                self.by_chunk(dk, wide, True),
                self.by_micro(h, dk, dv),
                self.by_micro(h, dk, dv),
            ],
            [
                (self.by_rows(width + LANES, True), self.like(BF16, self.rows, width + LANES)),
                (self.by_micro(8, width), self.like(F32, self.micros, 8, width)),
                (self.by_micro(HALO, width), self.like(F32, self.micros, HALO, width)),
                (self.whole(8, width), self.like(F32, 8, width)),
                (self.whole(8, LANES), self.like(F32, 8, LANES)),
            ],
            [pltpu.VMEM((8, width), F32), pltpu.VMEM((h, dk, dv), F32)],
            "mix_backward",
            after,
            seq_count=self.info.shape[1] - 2,
        )

    def gate_forward(self, plain, cmap, incoming, gate, gain, after=()):
        h, dk, dv = self.heads, self.key_size, self.value_size
        return self.call(
            gate_forward_kernel,
            (plain, cmap, incoming, gate, gain),
            [
                self.by_rows(h * dv),
                self.by_rows(h * dk),
                self.by_micro(h, dk, dv),
                self.by_rows(h * dv),
                self.whole(8, dv),
            ],
            [
                (self.by_rows(h * dv), self.like(F32, self.rows, h * dv)),
                (self.by_rows(h * dv), self.like(BF16, self.rows, h * dv)),
            ],
            [],
            "gate_forward",
            after,
        )

    def gate_backward(self, grad, mixed, cmap, gate, gain, after=()):
        h, dk, dv = self.heads, self.key_size, self.value_size
        return self.call(
            gate_backward_kernel,
            (grad, mixed, cmap, gate, gain),
            [
                self.by_rows(h * dv),
                self.by_rows(h * dv),
                self.by_rows(h * dk),
                self.by_rows(h * dv),
                self.whole(8, dv),
            ],
            [
                (self.by_rows(h * dv), self.like(BF16, self.rows, h * dv)),
                (self.by_rows(h * dv), self.like(F32, self.rows, h * dv)),
                (self.by_micro(h, dk, dv), self.like(F32, self.micros, h, dk, dv)),
                (self.whole(8, dv), self.like(F32, 8, dv)),
            ],
            [],
            "gate_backward",
            after,
        )


def from_behind(value, axis, steps):
    count = lax.axis_size(axis)
    leading, last = (max(0, -steps), min(count, count - steps))
    return lax.ppermute(value, axis, [(source, source + steps) for source in range(leading, last)])


def swap(value, axis, bit):
    return lax.ppermute(value, axis, [(at, at ^ bit) for at in range(lax.axis_size(axis))])


def rank_block(rank, mine):
    apart = jnp.bitwise_xor(rank, mine)
    return 2 * jnp.bitwise_and(apart, 1) + jnp.right_shift(apart, 1)


def cut_rows(value, count):
    size = value.shape[0] // count
    return [value[at * size : (at + 1) * size] for at in range(count)]


class HeadGather:
    def __init__(self, value):
        self.value = value
        self.across = [swap(part, "head", 2) for part in cut_rows(value, PIECES // 2)]

    def pass_on(self, *after):
        self.pair = stacked([self.value, *self.across], after)
        self.near = [swap(part, "head", 1) for part in cut_rows(self.pair, PIECES)]
        return (self.pair,)

    def rows(self, *after):
        return stacked([self.pair, *self.near], after)


class HeadScatter:
    def __init__(self, mine, *sent):
        self.pieces = max(len(sent), 2)
        self.mine, self.sent = cut_rows(mine, self.pieces), sent
        self.near = [swap(part, "head", 1) for part in sent]

    def pass_on(self, *after):
        half = self.pieces // 2
        self.near = [tie(part, *after) for part in self.near]
        if len(self.near) == 1:
            self.near = cut_rows(self.near[0], 2)
        theirs = [
            (mine.astype(F32) + near.astype(F32)).astype(BF16)
            for mine, near in zip(self.mine[half:], self.near[half:])
        ]
        self.across = [swap(part, "head", 2) for part in theirs]
        return tuple(theirs)

    def total(self, *after):
        parts = zip(self.mine, self.near, self.across)
        return jnp.concatenate(
            [
                mine.astype(F32) + near.astype(F32) + tie(across, *after).astype(F32)
                for mine, near, across in parts
            ],
            axis=0,
        )


class Summed:
    def __init__(self, value, hops):
        self.value, self.hops, self.came = value, list(hops), []

    def step(self, *after):
        if not self.came and after:
            self.value = tie(self.value, *after)
        for came in self.came:
            self.value = self.value + tie(came, *after)
        self.came = []
        if self.hops:
            axis, turns = self.hops.pop(0)
            self.came = [swap(self.value, axis, turn) for turn in turns]
        return (self.value,)

    def total(self):
        while self.came:
            self.step()
        return self.value


def head_hops():
    return [("head", [1 << at]) for at in range((lax.axis_size("head") - 1).bit_length())]


def dp_hops():
    count = lax.axis_size("dp")
    if count <= 8:
        return [("dp", [1]), ("dp", list(range(2, count, 2)))]
    return [("dp", [1 << at]) for at in range((count - 1).bit_length())]


def ring_order():
    count = lax.axis_size("dp")
    return list(range(0, count, 2)) + list(range(count - 1, 0, -2))


def ring_place():
    count, mine = lax.axis_size("dp"), lax.axis_index("dp")
    return jnp.where(mine % 2 == 0, mine // 2, count - 1 - mine // 2)


def ring_steps():
    ring = ring_order()
    ahead = [(ring[at], ring[(at + 1) % len(ring)]) for at in range(len(ring))]
    return ahead, [(after, before) for before, after in ahead]


def reorder_kernel(order_ref, *refs, size, outward):
    count = len(refs) // 2
    for source, target in zip(refs[:count], refs[count:]):
        for at in range(order_ref.shape[0]):
            moved = pl.ds(pl.multiple_of(order_ref[at] * size, size), size)
            here = slice(at * size, (at + 1) * size)
            if outward:
                target[:, moved] = source[:, here]
            else:
                target[:, here] = source[:, moved]


def reorder(arrays, outward, after=()):
    ring = ring_order()
    count, place = len(ring), ring_place()
    size = arrays[0].shape[1] // count
    around = jnp.asarray(ring + ring, jnp.int32)
    order = lax.dynamic_slice(around, (place,), (count,))
    if size % LANES == 0:
        return kernel_call(
            reorder_kernel,
            order,
            arrays,
            (1,),
            [pl.BlockSpec(a.shape, lambda i, info: (0, 0)) for a in arrays],
            [pl.BlockSpec(a.shape, lambda i, info: (0, 0)) for a in arrays],
            [jax.ShapeDtypeStruct(a.shape, a.dtype) for a in arrays],
            [],
            "reorder",
            after,
            size=size,
            outward=outward,
        )
    if outward:
        ranks = jnp.arange(count, dtype=jnp.int32)
        order = jnp.sum(jnp.where(order[None, :] == ranks[:, None], ranks[None, :], 0), axis=1)
    return [
        jnp.take(a.reshape(-1, count, size), order, axis=1).reshape(a.shape) for a in arrays
    ]


class Gather:
    def __init__(self, shard):
        self.ahead, self.back = ring_steps()
        self.left, self.right, self.far = [shard], [shard], None

    def step(self, *after):
        if len(self.left) > 1 or after:
            self.left[-1] = tie(self.left[-1], *after)
            self.right[-1] = self.left[0] if len(self.left) == 1 else tie(self.right[-1], *after)
        sent = self.left[-1], self.right[-1]
        if len(self.left) < len(self.ahead) // 2:
            self.left.append(lax.ppermute(self.left[-1], "dp", self.ahead))
            self.right.append(lax.ppermute(self.right[-1], "dp", self.back))
        else:
            half = self.left[0].shape[0] // 2
            self.far = [
                lax.ppermute(self.left[-1][:half], "dp", self.ahead),
                lax.ppermute(self.right[-1][half:], "dp", self.back),
            ]
        return sent

    def run(self, *after):
        while self.far is None:
            after = self.step(*after)
        return after

    def came(self):
        return self.left[-1], self.right[-1]

    def parts(self):
        return [self.left[0]] + self.right[1:] + self.far + self.left[:0:-1]


def gathered(wanted, after=()):
    rings = []
    for cuts in wanted:
        rings += [ring for ring, _, _ in cuts if ring not in rings]
    arrays, first = [], {}
    for ring in rings:
        first[ring] = len(arrays)
        arrays += ring.parts()
    plan = []
    for cuts in wanted:
        column, items = 0, []
        for ring, low, high in cuts:
            row = 0
            for at, part in enumerate(ring.parts()):
                items.append((first[ring] + at, (0, part.shape[0]), (low, high), row, column))
                row += part.shape[0]
            column += high - low
        plan.append(((row, column), items))
    return assemble(plan, arrays, after)


class Scatter:
    def __init__(self, *pairs, after=()):
        self.ahead, self.back = ring_steps()
        self.pairs, self.count = pairs, len(self.ahead)
        self.size = pairs[0][0].shape[1] // self.count
        self.apart = self.size % LANES == 0
        self.at = middle = self.count // 2
        self.left = self.right = None
        self.blocks = [{} for _ in pairs]
        self.groups = [[middle]]
        if self.count > 4:
            self.groups.append([middle - 1, middle + 1])
        self.groups.append([at for at in range(self.count) if all(at not in g for g in self.groups)])
        if self.apart:
            self.work(0, after=after)
        else:
            for which, pair in enumerate(pairs):
                whole = matmul([pair], TN, BF16, after)
                self.blocks[which] = {at: (whole, at) for at in range(self.count)}

    def work(self, group, only=None, after=()):
        found = []
        for which, pair in enumerate(self.pairs):
            if self.apart and only in (None, which):
                found.append(row_blocks(*pair, self.groups[group], self.count, after))
                for place, at in enumerate(self.groups[group]):
                    self.blocks[which][at] = (found[-1], place)
        return tuple(found) or tuple(after)

    def of(self, at):
        return [blocks[at] for blocks in self.blocks]

    def step(self, *after):
        middle, half = self.count // 2, self.size // 2
        if self.at == middle:
            plan, arrays = [], [grad for grad, _ in self.of(middle)]
            for start in (0, half):
                column, items = 0, []
                for at, (grad, place) in enumerate(self.of(middle)):
                    first, width = place * self.size + start, grad.shape[1]
                    items.append((at, (first, first + half), (0, width), 0, column))
                    column += width
                plan.append(((half, column), items))
            up, down = assemble(plan, arrays, after)
        else:
            up, down = ring_add(
                self.of(self.at),
                self.of(self.count - self.at),
                self.left,
                self.right,
                self.at == middle - 1,
                after,
            )
        self.left = lax.ppermute(up, "dp", self.ahead)
        self.right = lax.ppermute(down, "dp", self.back)
        self.at -= 1
        return up, down

    def came(self):
        return self.left, self.right

    def total(self, *after):
        while self.at > 0:
            after = self.step(*after)
        mine = [
            grad[place * self.size : (place + 1) * self.size] for grad, place in self.of(0)
        ]
        mine = mine[0] if len(mine) == 1 else jnp.concatenate(mine, axis=1)
        left, right = tie(self.left, *after), tie(self.right, *after)
        return mine.astype(F32) + left.astype(F32) + right.astype(F32)


def apply_map(moves, state, turned=False):
    return jnp.einsum(
        "hji,hjv->hiv" if turned else "hij,hjv->hiv",
        moves.astype(BF16),
        state.astype(BF16),
        preferred_element_type=F32,
    )


def own_and_swapped(value, bit):
    sent = jnp.where(bit == 0, value[1], value[0]).astype(BF16)
    theirs = swap(sent, "dp", 1).astype(F32)
    mine = jnp.where(bit == 0, value[0], value[1]).astype(F32)
    return jnp.where(bit == 0, mine, theirs), jnp.where(bit == 0, theirs, mine), sent


def hand_back(first, second, bit):
    mine = jnp.where(bit == 0, first, second).astype(BF16)
    sent = jnp.where(bit == 0, second, first).astype(BF16)
    theirs = swap(sent, "dp", 1)
    return jnp.stack([jnp.where(bit == 0, mine, theirs), jnp.where(bit == 0, theirs, mine)]), sent


class Scan:
    def __init__(self, final, value_size):
        self.bit, self.pairs = lax.axis_index("dp") % 2, lax.axis_size("dp") // 2
        self.cut = value_size
        self.sent = jnp.where(self.bit == 0, final[1], final[0]).astype(BF16)
        self.mine = jnp.where(self.bit == 0, final[0], final[1]).astype(F32)
        self.theirs = swap(self.sent, "dp", 1)

    def ordered(self, *after):
        theirs = tie(self.theirs, *after).astype(F32)
        return (
            jnp.where(self.bit == 0, self.mine, theirs),
            jnp.where(self.bit == 0, theirs, self.mine),
        )

    def shifted(self, value, steps):
        return [from_behind(value, "dp", 2 * sign) for sign in steps]

    def send(self, *after):
        self.first, self.second = self.ordered(*after)
        cut = self.cut
        self.first_map, self.second_map = self.first[..., cut:], self.second[..., cut:]
        pair_map = apply_map(self.second_map, self.first_map)
        self.pair_map = pair_map.astype(BF16)
        pair_sum = apply_map(self.second_map, self.first[..., :cut]) + self.second[..., :cut]
        both = jnp.concatenate([pair_sum, pair_map], axis=-1).astype(BF16)
        self.before = self.shifted(both, range(1, self.pairs))
        return (both,)

    def finish(self, *after):
        state = jnp.zeros(self.first[..., : self.cut].shape, F32)
        for both in self.before[::-1]:
            both = tie(both, *after)
            after = ()
            state = apply_map(both[..., self.cut :], state) + both[..., : self.cut].astype(F32)
        after_first = apply_map(self.first_map, state) + self.first[..., : self.cut]
        return self.hand_back(state, after_first)

    def hand_back(self, first, second):
        mine = jnp.where(self.bit == 0, first, second).astype(BF16)
        sent = jnp.where(self.bit == 0, second, first).astype(BF16)
        theirs = swap(sent, "dp", 1)
        states = [jnp.where(self.bit == 0, *pair) for pair in ((mine, theirs), (theirs, mine))]
        return jnp.stack(states), (sent,)


class ScanBack(Scan):
    def __init__(self, local, ahead):
        self.of = ahead
        super().__init__(local, local.shape[-1])

    def send(self, *after):
        self.first, self.second = self.ordered(*after)
        pair_sum = (apply_map(self.of.first_map, self.second, True) + self.first).astype(BF16)
        both = jnp.concatenate([pair_sum, self.of.pair_map], axis=-1)
        self.behind = self.shifted(both, [-step for step in range(1, self.pairs)])
        return (both,)

    def finish(self, *after):
        state = jnp.zeros(self.first.shape, F32)
        for both in self.behind[::-1]:
            both = tie(both, *after)
            after = ()
            moves = both[..., self.cut :]
            state = apply_map(moves, state, True) + both[..., : self.cut].astype(F32)
        before_second = apply_map(self.of.second_map, state, True) + self.second
        return self.hand_back(before_second, state)


def norm_backward(grad_in, normed_rows, scale):
    return scale * (grad_in - normed_rows * jnp.mean(grad_in * normed_rows, axis=-1, keepdims=True))


def body(
    tokens,
    out_grad,
    seq_lengths,
    attn_norm,
    query_proj,
    key_proj,
    value_proj,
    gate_proj,
    decay_proj,
    beta_proj,
    conv_query,
    conv_key,
    conv_value,
    log_rate,
    step_bias,
    head_norm,
    out_proj,
    ffn_norm,
    ffn_gate,
    ffn_up,
    ffn_down,
):
    head_rank, ranks = lax.axis_index("head"), lax.axis_size("head")
    heads = decay_proj.shape[1]
    qk_width = query_proj.shape[1]
    v_width = value_proj.shape[1]
    key_size = qk_width // heads
    value_size = v_width // heads
    ffn_width = ffn_gate.shape[1]
    conv_width = 2 * qk_width + v_width
    micros, part_rows, model = tokens.shape
    assert part_rows == CHUNK and micros == 2 and ranks == 4

    decay_pad = jnp.zeros((decay_proj.shape[0], LANES - 2 * heads), decay_proj.dtype)
    conv_ring = Gather(
        jnp.concatenate(
            [query_proj, key_proj, value_proj, decay_proj, beta_proj, decay_pad], axis=1
        )
    )
    gate_ring = Gather(jnp.concatenate([gate_proj, out_proj.T], axis=1))
    ffn_ring = Gather(jnp.concatenate([ffn_gate, ffn_up, ffn_down.T], axis=1))

    def of_mine(whole, width):
        return lax.dynamic_slice_in_dim(whole, head_rank * width, width, whole.ndim - 1)

    taps = jnp.concatenate(
        [of_mine(conv_query, qk_width), of_mine(conv_key, qk_width), of_mine(conv_value, v_width)],
        axis=1,
    )
    taps = jnp.pad(taps, ((0, 8 - KCONV), (0, 0)))
    par = jnp.pad(
        jnp.stack([-jnp.exp(of_mine(log_rate, heads)), of_mine(step_bias, heads)]),
        ((0, 6), (0, LANES - heads)),
    )
    gain = jnp.broadcast_to(head_norm, (8, value_size))

    def flat(value):
        return value.reshape(-1, value.shape[-1])

    def ranked(value):
        return value.reshape(ranks, micros, part_rows, value.shape[-1])

    conv_ring.step()
    turned, cotangent, attn_gain, ffn_gain = reorder(
        [
            flat(tokens),
            flat(out_grad),
            jnp.broadcast_to(attn_norm, (8, model)),
            jnp.broadcast_to(ffn_norm, (8, model)),
        ],
        False,
    )
    attn_gain, ffn_gain = attn_gain[0], ffn_gain[0]
    residual = turned.astype(F32)
    scale_one = lax.rsqrt(jnp.mean(residual * residual, axis=-1, keepdims=True) + EPSILON)
    normed_one = residual * scale_one
    normed_rows = HeadGather((normed_one * attn_gain).astype(BF16))
    conv_ring.step()
    (pair,) = normed_rows.pass_on(*conv_ring.came(), gate_ring.left[0], ffn_ring.left[0])
    conv_ring.step()
    normed_all = normed_rows.rows(*conv_ring.came())
    last_chunk = rank_block(ranks - 1, head_rank)
    last_rows = lax.dynamic_slice(
        ranked(normed_all), (last_chunk, 0, part_rows - HALO, 0), (1, micros, HALO, model)
    )
    conv_ring.run()
    rim_rows = from_behind(reorder([flat(last_rows)], True)[0], "dp", 1)
    rim_rows = reorder([rim_rows], False)[0]
    first_row = lax.axis_index("dp") * ranks * part_rows
    ends = jnp.cumsum(seq_lengths, axis=1)
    info = jnp.concatenate(
        [
            ends - seq_lengths,
            jnp.full((micros, 1), first_row, jnp.int32),
            jnp.full((micros, 1), head_rank, jnp.int32),
        ],
        axis=1,
    ).astype(jnp.int32)
    mix = Mix(info, micros, ranks, heads, key_size, value_size)
    now = gate_ring.step(rim_rows, *conv_ring.far)
    (w_conv,) = gathered([[(conv_ring, 0, conv_width + LANES)]], now)
    projected, rim = project(normed_all, rim_rows, w_conv)
    now = gate_ring.step(rim)
    now = ffn_ring.step(*now)

    plain, carried_map, inverses, starts, final = mix.forward(projected, rim, taps, par, now)
    scan = Scan(final, value_size)
    now = scan.send(scan.sent, *gate_ring.came(), *ffn_ring.came())
    cotangent_rows = HeadGather(tie(cotangent, *now))
    now = gate_ring.step(*now, *scan.before)
    now = cotangent_rows.pass_on(*now)
    incoming, now = scan.finish(*now)
    cotangent_all = cotangent_rows.rows(*now)
    now = gate_ring.run(*now)
    now = ffn_ring.step(incoming, *gate_ring.far, cotangent_all)
    w_gate, w_out = gathered(
        [[(gate_ring, 0, v_width)], [(gate_ring, v_width, 2 * v_width)]], now
    )
    gate_lin = matmul([(normed_all, w_gate)], NN, F32)
    mixed, gated = mix.gate_forward(plain, carried_map, incoming, gate_lin, gain)

    mix_sum = HeadScatter(*matmul([(gated, w_out)], NT, BF16, pieces=PIECES))
    now = ffn_ring.step(*mix_sum.sent)
    now = mix_sum.pass_on(*now)
    after_mix = residual + mix_sum.total(*now)
    scale_two = lax.rsqrt(jnp.mean(after_mix * after_mix, axis=-1, keepdims=True) + EPSILON)
    normed_two = after_mix * scale_two
    ffn_rows = HeadGather((normed_two * ffn_gain).astype(BF16))
    now = ffn_ring.run(ffn_rows.across[0])
    now = ffn_rows.pass_on(*now)
    ffn_all = ffn_rows.rows(*now)
    w_ffn, w_down = gathered(
        [[(ffn_ring, 0, 2 * ffn_width)], [(ffn_ring, 2 * ffn_width, 3 * ffn_width)]], (ffn_all,)
    )

    hidden, gate_up_grad = feed_forward(ffn_all, cotangent_all, w_ffn, w_down)
    ffn_in_sum = HeadScatter(*matmul([(gate_up_grad, w_ffn)], NT, BF16, pieces=PIECES))
    ffn_sums = Scatter(
        (ffn_all, gate_up_grad), (cotangent_all, hidden), after=ffn_in_sum.sent
    )
    now = ffn_sums.step()
    now = ffn_in_sum.pass_on(*now)
    now = ffn_sums.work(1, after=now)
    now = ffn_sums.step(*now)
    ffn_in_grad = ffn_in_sum.total(*now)
    grad_norm_two = jnp.sum(ffn_in_grad * normed_two, axis=0)
    after_mix_grad = cotangent.astype(F32) + norm_backward(
        ffn_in_grad * ffn_gain, normed_two, scale_two
    )
    branch_rows = HeadGather(after_mix_grad.astype(BF16))
    now = ffn_sums.work(2, after=(branch_rows.value,))
    now = branch_rows.pass_on(*now)
    branch_grad = branch_rows.rows(*now)
    now = (branch_grad,)

    gated_grad = matmul([(branch_grad, w_out)], NN, F32, now)
    gate_grad, mixed_grad, local_grad, grad_head_norm = mix.gate_backward(
        gated_grad, mixed, carried_map, gate_lin, gain, ffn_sums.came()
    )

    back = ScanBack(local_grad, scan)
    gate_sums = Scatter(
        (normed_all, gate_grad), (branch_grad, gated), after=(back.sent, *ffn_sums.came())
    )
    now = gate_sums.work(1, after=(back.sent,)) + gate_sums.work(2, 1, (back.sent,))
    now = back.send(*now)
    now = gate_sums.work(2, 0, now)
    now = gate_sums.step(*now, back.behind[-1])
    ffn_part = matmul([(hidden, w_down)], NT, BF16, now, pieces=PIECES)
    leaving, now = back.finish(ffn_part[0])
    now = ffn_sums.step(leaving, *gate_sums.came())
    now = gate_sums.step(*now)
    conv_grad, rim_grad, tail, taps_grad, par_grad = mix.backward(
        projected, rim, taps, par, mixed_grad, inverses, starts, incoming, leaving, now
    )
    back_rim = from_behind(rim_grad, "dp", -1)
    small = jnp.concatenate(
        [
            taps_grad[:KCONV].reshape(-1),
            jnp.pad(par_grad[0, :heads], (0, LANES - heads)),
            jnp.pad(par_grad[1, :heads], (0, LANES - heads)),
            grad_head_norm[0],
        ]
    ).reshape(-1, LANES)
    ffn_sum = HeadScatter(ffn_part[0], *[tie(part, rim_grad) for part in ffn_part[1:]])
    now = ffn_sums.step(back_rim, *gate_sums.came())
    now = ffn_sum.pass_on(*now)
    tail = tie(tail, back_rim)
    tail = jnp.concatenate([tail[:, :8], tail[:, 8:] + back_rim], axis=1).astype(BF16)
    conv_grad = lax.dynamic_update_slice(
        ranked(conv_grad), tail[None], (last_chunk, 0, part_rows - HALO, 0)
    ).reshape(-1, conv_width + LANES)

    conv_sums = Scatter((normed_all, conv_grad), after=now)
    now = conv_sums.step()
    now = conv_sums.work(1, after=now) + conv_sums.work(2, after=now)
    normed_part = matmul(
        [(conv_grad, w_conv), (gate_grad, w_gate)], NT, BF16, now, pieces=PIECES
    )
    normed_sum = HeadScatter(*normed_part)
    now = gate_sums.step(*normed_sum.sent, *ffn_sums.came(), *conv_sums.came())
    now = normed_sum.pass_on(*now)
    now = conv_sums.step(*now, *gate_sums.came())
    now = gate_sums.step(*now)
    now = conv_sums.step(*now)
    normed_grad = normed_sum.total(*now)
    now = conv_sums.step(*now, *gate_sums.came())
    grad_norm_one = jnp.sum(normed_grad * normed_one, axis=0)
    norm_grads = jnp.pad(jnp.stack([grad_norm_one, grad_norm_two]), ((0, 6), (0, 0)))
    (norm_grads,) = reorder([norm_grads], True, now)
    norm_sum = Summed(norm_grads[:2].reshape(-1, LANES), head_hops())
    norm_sum.step()
    norm_sum.step()
    input_grad = after_mix_grad + norm_backward(normed_grad * attn_gain, normed_one, scale_one)
    block_out = (after_mix + ffn_sum.total(*now)).astype(BF16)
    small_sum = Summed(jnp.concatenate([small, norm_sum.total()], axis=0), dp_hops())
    small_sum.step(*now)
    small_sum.step()
    block_out, input_grad = reorder([block_out, input_grad], True, now)
    block_out, input_grad = block_out.reshape(tokens.shape), input_grad.reshape(tokens.shape)
    shard_ffn = ffn_sums.total(*now)
    shard_gate = gate_sums.total(*now)
    shard_conv = conv_sums.total()
    small, norm_grads = small_sum.total()[: small.shape[0]], small_sum.total()[small.shape[0] :]
    norm_grads = norm_grads.reshape(2, model)

    across = jnp.stack([small, swap(small, "head", 2)])
    near = swap(across, "head", 1)
    small = jnp.stack([across[0], near[0], across[1], near[1]])
    small = jnp.stack([small[jnp.bitwise_xor(at, head_rank)] for at in range(ranks)])
    tap_rows = KCONV * conv_width // LANES
    taps_all = small[:, :tap_rows].reshape(ranks, KCONV, conv_width).transpose(1, 0, 2)

    def joined(low, high):
        return taps_all[:, :, low:high].reshape(KCONV, -1)

    rest = jnp.sum(small[:, tap_rows + 2 :], axis=0).reshape(-1)
    return (
        block_out,
        input_grad,
        norm_grads[0],
        shard_conv[:, :qk_width],
        shard_conv[:, qk_width : 2 * qk_width],
        shard_conv[:, 2 * qk_width : conv_width],
        shard_gate[:, :v_width],
        shard_conv[:, conv_width : conv_width + heads],
        shard_conv[:, conv_width + heads : conv_width + 2 * heads],
        joined(0, qk_width),
        joined(qk_width, 2 * qk_width),
        joined(2 * qk_width, conv_width),
        small[:, tap_rows, :heads].reshape(-1),
        small[:, tap_rows + 1, :heads].reshape(-1),
        rest[:value_size],
        shard_gate[:, v_width:].T,
        norm_grads[1],
        shard_ffn[:, :ffn_width],
        shard_ffn[:, ffn_width : 2 * ffn_width],
        shard_ffn[:, 2 * ffn_width :].T,
    )


def solution(mesh):
    rows, plane, turned, whole = P(None, ("dp", "head"), None), P("dp", "head"), P("head", "dp"), P()
    in_specs = (rows, rows, whole, whole) + (plane,) * 6 + (whole,) * 6
    in_specs += (turned, whole, plane, plane, turned)
    out_specs = (rows, rows, whole) + (plane,) * 6 + (whole,) * 6
    out_specs += (turned, whole, plane, plane, turned)
    return jax.shard_map(body, mesh=mesh, in_specs=in_specs, out_specs=out_specs, check_vma=False)
```

```python
from functools import partial

import jax
import jax.numpy as jnp
from jax import lax
from jax.experimental import pallas as pl
from jax.experimental.pallas import tpu as pltpu
from jax.sharding import PartitionSpec as P

CHUNK = 128
KCONV = 4
LANES = 128
HALO = 16

EPSILON = 1e-06
HEAD_FLOOR = 0.01
F32 = jnp.float32
BF16 = jnp.bfloat16
NN = (((1,), (0,)), ((), ()))
NT = (((1,), (1,)), ((), ()))
TN = (((0,), (0,)), ((), ()))


def mm(left, right, dims=NN):
    return lax.dot_general(
        left.astype(BF16), right.astype(BF16), dims, preferred_element_type=F32
    )


def split(value):
    high = value.astype(BF16)
    return high, (value - high.astype(F32)).astype(BF16)


def mm3(left, right, dims=NN):
    left_high, left_low = split(left)
    right_high, right_low = split(right)
    return mm(left_high, right_high, dims) + (
        mm(left_high, right_low, dims) + mm(left_low, right_high, dims)
    )


def chunk_places(info_ref, micro, chunk, seq_count):
    first = info_ref[micro, seq_count] + chunk * CHUNK
    starts = [info_ref[micro, at] for at in range(seq_count)]
    rows = first + lax.broadcasted_iota(jnp.int32, (CHUNK, 1), 0)
    lanes = first + lax.broadcasted_iota(jnp.int32, (1, CHUNK), 1)
    seg_col = jnp.zeros((CHUNK, 1), jnp.int32)
    seg_row = jnp.zeros((1, CHUNK), jnp.int32)
    begun = jnp.zeros((CHUNK, 1), jnp.int32)
    seg_before = jnp.int32(0)
    seg_last = jnp.int32(0)
    for start in starts:
        seg_col = seg_col + jnp.where(rows >= start, 1, 0)
        seg_row = seg_row + jnp.where(lanes >= start, 1, 0)
        begun = jnp.maximum(begun, jnp.where(rows >= start, start, 0))
        seg_before = seg_before + jnp.where(first - 1 >= start, 1, 0)
        seg_last = seg_last + jnp.where(first + CHUNK - 1 >= start, 1, 0)
    offset = rows - begun
    row_ids = lax.broadcasted_iota(jnp.int32, (CHUNK, CHUNK), 0)
    col_ids = lax.broadcasted_iota(jnp.int32, (CHUNK, CHUNK), 1)
    same = seg_col == seg_row
    return dict(
        row_ids=row_ids,
        col_ids=col_ids,
        inclusive=jnp.logical_and(row_ids >= col_ids, same),
        strictly=jnp.logical_and(row_ids > col_ids, same),
        untouched=jnp.where(seg_col == seg_before, 1.0, 0.0).astype(F32),
        with_last=jnp.where(seg_col == seg_last, 1.0, 0.0).astype(F32),
        lags=[jnp.where(offset >= lag, 1.0, 0.0).astype(F32) for lag in range(1, KCONV)],
    )


def decay_parts(g_col, places):
    row_ids, col_ids = places["row_ids"], places["col_ids"]
    cum_row = jnp.sum(jnp.where(row_ids <= col_ids, g_col, 0.0), axis=0, keepdims=True)
    cum_col = jnp.sum(jnp.where(row_ids == col_ids, cum_row, 0.0), axis=1, keepdims=True)
    spread = jnp.where(places["inclusive"], cum_col - cum_row, 0.0)
    pair = jnp.where(places["inclusive"], jnp.exp(spread), 0.0)
    carry = jnp.exp(cum_col) * places["untouched"]
    cum_last = cum_col[CHUNK - 1 :, :]
    to_last = jnp.exp(jnp.minimum(cum_last - cum_col, 0.0)) * places["with_last"]
    return pair, carry, to_last, carry[CHUNK - 1 :, :]


def conv_rows(extended, taps, lags):
    total = taps[KCONV - 1 :, :] * extended[HALO:]
    for lag in range(1, KCONV):
        shifted = extended[HALO - lag : HALO - lag + CHUNK]
        total = total + taps[KCONV - 1 - lag : KCONV - lag, :] * shifted * lags[lag - 1]
    return total


def head_columns(head, heads, key_size, value_size):
    return (
        (head * key_size, key_size),
        ((heads + head) * key_size, key_size),
        (2 * heads * key_size + head * value_size, value_size),
    )


def unit_rows(active):
    return active * lax.rsqrt(jnp.sum(active * active, axis=1, keepdims=True) + EPSILON)


def softplus(value):
    return jnp.maximum(value, 0.0) + jnp.log1p(jnp.exp(-jnp.abs(value)))


def unit_lower_inverses(systems, places):
    row_ids, col_ids = places["row_ids"], places["col_ids"]
    eye = jnp.where(row_ids == col_ids, 1.0, 0.0).astype(F32)
    pairs = jnp.right_shift(row_ids, 1) == jnp.right_shift(col_ids, 1)
    found = [eye - jnp.where(pairs, system, 0.0) for system in systems]
    level = 1
    while (1 << level) < CHUNK:
        row_block = jnp.right_shift(row_ids, level)
        col_block = jnp.right_shift(col_ids, level)
        lower = jnp.logical_and(
            jnp.right_shift(row_block, 1) == jnp.right_shift(col_block, 1), row_block > col_block
        )
        inner = [
            INVERSE_MM(jnp.where(lower, system, 0.0), inverse)
            for system, inverse in zip(systems, found)
        ]
        found = [
            inverse - INVERSE_MM(inverse, middle) for inverse, middle in zip(found, inner)
        ]
        level += 1
    return found


INVERSE_MM = mm3


def mix_forward_kernel(
    info_ref,
    x_ref,
    rim_ref,
    taps_ref,
    par_ref,
    out_ref,
    cmap_ref,
    inv_ref,
    start_ref,
    final_ref,
    halo,
    state,
    *,
    heads,
    key_size,
    value_size,
    seq_count,
):
    micro, chunk = pl.program_id(0), pl.program_id(1)
    span = range(heads)

    width = halo.shape[1]

    @pl.when(chunk == 0)
    def _():
        halo[...] = rim_ref[:, :width].astype(BF16)
        row_ids = lax.broadcasted_iota(jnp.int32, (key_size, key_size), 0)
        col_ids = lax.broadcasted_iota(jnp.int32, (key_size, key_size), 1)
        eye = jnp.where(row_ids == col_ids, 1.0, 0.0).astype(F32)
        for head in span:
            state[head] = jnp.concatenate([jnp.zeros((key_size, value_size), F32), eye], axis=1)

    places = chunk_places(info_ref, micro, chunk, seq_count)
    dec = x_ref[:, width:]
    beta_all = jax.nn.sigmoid(dec)
    g_all = par_ref[0:1, :] * softplus(dec + par_ref[1:2, :])
    scale = key_size**-0.5

    queries, keys, values = [], [], []
    for head in span:
        rows = []
        for begin, size in head_columns(head, heads, key_size, value_size):
            cut = slice(begin, begin + size)
            extended = jnp.concatenate(
                [halo[:, cut].astype(F32), x_ref[:, cut].astype(BF16).astype(F32)], axis=0
            )
            summed = conv_rows(extended, taps_ref[0:KCONV, cut], places["lags"])
            rows.append(summed * jax.nn.sigmoid(summed))
        queries.append(unit_rows(rows[0]) * scale)
        keys.append(unit_rows(rows[1]))
        values.append(rows[2])
    halo[...] = x_ref[CHUNK - HALO :, :width].astype(BF16)

    betas = [beta_all[:, heads + head : heads + head + 1] for head in span]
    decays = [decay_parts(g_all[:, head : head + 1], places) for head in span]
    grams = [mm(keys[head], keys[head], NT) for head in span]
    systems = [
        jnp.where(places["strictly"], betas[head] * decays[head][0] * grams[head], 0.0)
        for head in span
    ]
    inverses = unit_lower_inverses(systems, places)
    attends = [mm(queries[head], keys[head], NT) * decays[head][0] for head in span]
    solved = [
        mm(
            inverses[head],
            jnp.concatenate(
                [betas[head] * values[head], betas[head] * decays[head][1] * keys[head]], axis=1
            ),
        )
        for head in span
    ]
    starts = [state[head] for head in span]
    written = [
        jnp.concatenate(
            [solved[head][:, :value_size], jnp.zeros((CHUNK, key_size), F32)], axis=1
        )
        - mm(solved[head][:, value_size:], starts[head])
        for head in span
    ]
    outs = [
        decays[head][1] * mm(queries[head], starts[head]) + mm(attends[head], written[head])
        for head in span
    ]
    for head in span:
        _, _, to_last, carry_last = decays[head]
        inv_ref[0, head] = inverses[head].astype(BF16)
        start_ref[0, head] = starts[head].astype(BF16)
        out_ref[:, head * value_size : (head + 1) * value_size] = outs[head][:, :value_size]
        cmap_ref[:, head * key_size : (head + 1) * key_size] = outs[head][:, value_size:].astype(
            BF16
        )
        state[head] = carry_last * starts[head] + mm(to_last * keys[head], written[head], TN)

    @pl.when(chunk == pl.num_programs(1) - 1)
    def _():
        final_ref[0] = state[...]


def mix_backward_kernel(
    info_ref,
    x_ref,
    before_ref,
    rim_ref,
    taps_ref,
    par_ref,
    grad_ref,
    inv_ref,
    start_ref,
    incoming_ref,
    leaving_ref,
    dx_ref,
    rim_grad_ref,
    tail_ref,
    dtaps_ref,
    dpar_ref,
    carry,
    dstate,
    *,
    heads,
    key_size,
    value_size,
    seq_count,
):
    micro, step = pl.program_id(0), pl.program_id(1)
    chunk = pl.num_programs(1) - 1 - step
    span = range(heads)
    width = carry.shape[1]

    @pl.when(step == 0)
    def _():
        carry[...] = jnp.zeros_like(carry)
        dstate[...] = leaving_ref[0].astype(F32)

    @pl.when(jnp.logical_and(micro == 0, step == 0))
    def _():
        dtaps_ref[...] = jnp.zeros_like(dtaps_ref)
        dpar_ref[...] = jnp.zeros_like(dpar_ref)

    places = chunk_places(info_ref, micro, chunk, seq_count)
    row_ids, col_ids = places["row_ids"], places["col_ids"]
    lags = places["lags"]
    dec = x_ref[:, width:]
    beta_all = jax.nn.sigmoid(dec)
    shifted_dec = dec + par_ref[1:2, :]
    g_all = par_ref[0:1, :] * softplus(shifted_dec)
    scale = key_size**-0.5
    opening = jnp.where(chunk == 0, rim_ref[:, :width], before_ref[:, :width])
    opening = opening.astype(BF16).astype(F32)

    def extended_rows(cut):
        return jnp.concatenate(
            [opening[:, cut], x_ref[:, cut].astype(BF16).astype(F32)], axis=0
        )

    sums, norms, unit = [], [], []
    for head in span:
        mine = [
            conv_rows(
                extended_rows(slice(begin, begin + size)),
                taps_ref[0:KCONV, begin : begin + size],
                lags,
            )
            for begin, size in head_columns(head, heads, key_size, value_size)
        ]
        active = [value * jax.nn.sigmoid(value) for value in mine]
        inverse_norms = [
            lax.rsqrt(jnp.sum(value * value, axis=1, keepdims=True) + EPSILON)
            for value in active[:2]
        ]
        sums.append(mine)
        norms.append(inverse_norms)
        unit.append([active[0] * inverse_norms[0], active[1] * inverse_norms[1], active[2]])
    keys = [unit[head][1] for head in span]
    key_low = [keys[head].astype(BF16) for head in span]
    query_low = [(unit[head][0] * scale).astype(BF16) for head in span]
    betas = [beta_all[:, heads + head : heads + head + 1] for head in span]
    decays = [decay_parts(g_all[:, head : head + 1], places) for head in span]
    grams = [mm(key_low[head], key_low[head], NT) for head in span]
    products = [mm(query_low[head], key_low[head], NT) for head in span]
    attends = [(products[head] * decays[head][0]).astype(BF16) for head in span]
    starts = []
    for head in span:
        saved = start_ref[0, head]
        starts.append(
            saved[:, :value_size].astype(F32)
            + mm(saved[:, value_size:], incoming_ref[0, head])
        )
    start_low = [starts[head].astype(BF16) for head in span]
    key_state = [mm(key_low[head], start_low[head]) for head in span]
    query_state = [mm(query_low[head], start_low[head]) for head in span]
    grads = [grad_ref[:, head * value_size : (head + 1) * value_size] for head in span]
    grad_low = [grads[head].astype(BF16) for head in span]
    residues = [unit[head][2] - decays[head][1] * key_state[head] for head in span]
    inverses = [inv_ref[0, head] for head in span]
    written = [mm(inverses[head], betas[head] * residues[head]).astype(BF16) for head in span]
    ahead = [dstate[head] for head in span]
    ahead_low = [ahead[head].astype(BF16) for head in span]
    key_last = [(decays[head][2] * keys[head]).astype(BF16) for head in span]
    dwritten = [
        mm(attends[head], grad_low[head], TN) + mm(key_last[head], ahead_low[head])
        for head in span
    ]
    dresidue = [mm(inverses[head], dwritten[head], TN) for head in span]
    dresidue_low = [dresidue[head].astype(BF16) for head in span]
    dattend = [
        jnp.where(places["inclusive"], mm(grad_low[head], written[head], NT), 0.0)
        for head in span
    ]
    dsystem = [
        jnp.where(places["strictly"], -mm(dresidue_low[head], written[head], NT), 0.0)
        for head in span
    ]
    dproducts = [(dattend[head] * decays[head][0]).astype(BF16) for head in span]
    dcarried = [decays[head][1] * grads[head] for head in span]
    dcarried_low = [dcarried[head].astype(BF16) for head in span]
    dkey_state = [-(betas[head] * decays[head][1]) * dresidue[head] for head in span]
    dkey_state_low = [dkey_state[head].astype(BF16) for head in span]
    dkey_last = [mm(written[head], ahead_low[head], NT) for head in span]
    dgram = [dsystem[head] * betas[head] * decays[head][0] for head in span]
    dgram_low = [dgram[head].astype(BF16) for head in span]
    dquery = [
        mm(dcarried_low[head], start_low[head], NT) + mm(dproducts[head], key_low[head])
        for head in span
    ]
    dkey = [
        mm(dproducts[head], query_low[head], TN)
        + decays[head][2] * dkey_last[head]
        + mm(dkey_state_low[head], start_low[head], NT)
        + mm(dgram_low[head], key_low[head])
        + mm(dgram_low[head], key_low[head], TN)
        for head in span
    ]
    lane_ids = lax.broadcasted_iota(jnp.int32, (CHUNK, LANES), 1)
    ddec = jnp.zeros((CHUNK, LANES), F32)
    dg_all = jnp.zeros((CHUNK, LANES), F32)
    for head in span:
        pair, carried, to_last, carry_last = decays[head]
        coupled = dsystem[head] * grams[head]
        dpair = (dattend[head] * products[head] + coupled * betas[head]) * pair
        dbeta = jnp.sum(coupled * pair, axis=1, keepdims=True) + jnp.sum(
            dresidue[head] * residues[head], axis=1, keepdims=True
        )
        dcarry = jnp.sum(
            grads[head] * query_state[head] - betas[head] * dresidue[head] * key_state[head],
            axis=1,
            keepdims=True,
        )
        dcarry_last = jnp.sum(
            jnp.sum(ahead[head] * starts[head], axis=1, keepdims=True), axis=0, keepdims=True
        )
        dto_last = jnp.sum(dkey_last[head] * keys[head], axis=1, keepdims=True) * to_last
        is_last = lax.broadcasted_iota(jnp.int32, (CHUNK, 1), 0) == CHUNK - 1
        dcum_col = (
            jnp.sum(dpair, axis=1, keepdims=True)
            + dcarry * carried
            - dto_last
            + jnp.where(
                is_last,
                dcarry_last * carry_last + jnp.sum(dto_last, axis=0, keepdims=True),
                0.0,
            )
        )
        dcum_row = jnp.sum(
            jnp.where(row_ids == col_ids, dcum_col, 0.0) - dpair, axis=0, keepdims=True
        )
        dg = jnp.sum(jnp.where(col_ids >= row_ids, dcum_row, 0.0), axis=1, keepdims=True)
        beta = betas[head]
        dg_all = jnp.where(lane_ids == head, dg, dg_all)
        ddec = jnp.where(lane_ids == heads + head, dbeta * beta * (1.0 - beta), ddec)
        dstate[head] = (
            carry_last * ahead[head]
            + mm(query_low[head], dcarried_low[head], TN)
            + mm(key_low[head], dkey_state_low[head], TN)
        )
    dstep = dg_all * par_ref[0:1, :] * jax.nn.sigmoid(shifted_dec)
    ddec = ddec + dstep
    dx_ref[:, width:] = ddec.astype(BF16)
    dpar_ref[0:1, :] += jnp.sum(dg_all * g_all, axis=0, keepdims=True)
    dpar_ref[1:2, :] += jnp.sum(dstep, axis=0, keepdims=True)

    for head in span:
        dunit = [dquery[head] * scale, dkey[head]]
        dactive = [
            norms[head][at]
            * (
                dunit[at]
                - unit[head][at] * jnp.sum(dunit[at] * unit[head][at], axis=1, keepdims=True)
            )
            for at in range(2)
        ]
        dactive.append(betas[head] * dresidue[head])
        for at, (begin, size) in enumerate(head_columns(head, heads, key_size, value_size)):
            cut = slice(begin, begin + size)
            sig = jax.nn.sigmoid(sums[head][at])
            dsum = dactive[at] * sig * (1.0 + sums[head][at] * (1.0 - sig))
            extended = extended_rows(cut)
            taps = taps_ref[0:KCONV, cut]
            zeros = jnp.zeros((8, size), F32)
            dtaps_ref[KCONV - 1 : KCONV, cut] += jnp.sum(
                dsum * extended[HALO:], axis=0, keepdims=True
            )
            total = jnp.concatenate([zeros, taps[KCONV - 1 :, :] * dsum], axis=0)
            for lag in range(1, KCONV):
                masked = dsum * lags[lag - 1]
                at_tap = KCONV - 1 - lag
                dtaps_ref[at_tap : at_tap + 1, cut] += jnp.sum(
                    masked * extended[HALO - lag : HALO - lag + CHUNK], axis=0, keepdims=True
                )
                padded = jnp.concatenate(
                    [zeros, taps[at_tap : at_tap + 1, :] * masked, zeros], axis=0
                )
                total = total + padded[lag : lag + 8 + CHUNK]
            body_rows = jnp.concatenate(
                [total[8:CHUNK], total[CHUNK:] + carry[:, cut]], axis=0
            )
            dx_ref[:, cut] = body_rows.astype(BF16)
            carry[:, cut] = total[:8]

            @pl.when(step == 0)
            def _():
                tail_ref[0, :, cut] = body_rows[CHUNK - HALO :]

    @pl.when(chunk == 0)
    def _():
        rim_grad_ref[0] = carry[...]


def gate_forward_kernel(
    info_ref, plain_ref, cmap_ref, incoming_ref, gate_ref, gain_ref, mixed_ref, gated_ref, *, heads, key_size, value_size
):
    for head in range(heads):
        cut = slice(head * value_size, (head + 1) * value_size)
        mixed = plain_ref[:, cut] + mm(
            cmap_ref[:, head * key_size : (head + 1) * key_size], incoming_ref[0, head]
        )
        mixed_ref[:, cut] = mixed
        normed = mixed * lax.rsqrt(
            jnp.mean(mixed * mixed, axis=1, keepdims=True) + HEAD_FLOOR
        )
        gate = gate_ref[:, cut]
        gated_ref[:, cut] = (normed * gain_ref[0:1, :] * gate * jax.nn.sigmoid(gate)).astype(BF16)


def gate_backward_kernel(
    info_ref,
    grad_ref,
    mixed_ref,
    cmap_ref,
    gate_ref,
    gain_ref,
    dgate_ref,
    dmixed_ref,
    dlocal_ref,
    dgain_ref,
    *,
    heads,
    key_size,
    value_size,
):
    micro, step = pl.program_id(0), pl.program_id(1)

    @pl.when(step == 0)
    def _():
        dlocal_ref[...] = jnp.zeros_like(dlocal_ref)

    @pl.when(jnp.logical_and(micro == 0, step == 0))
    def _():
        dgain_ref[...] = jnp.zeros_like(dgain_ref)

    gain = gain_ref[0:1, :]
    for head in range(heads):
        cut = slice(head * value_size, (head + 1) * value_size)
        mixed = mixed_ref[:, cut]
        scale = lax.rsqrt(jnp.mean(mixed * mixed, axis=1, keepdims=True) + HEAD_FLOOR)
        normed = mixed * scale
        gate = gate_ref[:, cut]
        sig = jax.nn.sigmoid(gate)
        active = gate * sig
        grad = grad_ref[:, cut]
        by_norm = grad * normed
        dgain_ref[0:1, :] += jnp.sum(by_norm * active, axis=0, keepdims=True)
        dgate_ref[:, cut] = (by_norm * gain * sig * (1.0 + gate * (1.0 - sig))).astype(BF16)
        dnormed = grad * gain * active
        dmixed = scale * (dnormed - normed * jnp.mean(dnormed * normed, axis=1, keepdims=True))
        dmixed_ref[:, cut] = dmixed
        dlocal_ref[0, head] += mm(
            cmap_ref[:, head * key_size : (head + 1) * key_size], dmixed, TN
        )


VMEM_BYTES = 48 * 1024 * 1024
PIECES = 4


def kernel_call(
    kernel, info, arrays, grid, in_specs, out_specs, out_shape, scratch, name, after=(), **sizes
):
    count = 1 + len(arrays)

    def body(*refs):
        kernel(*refs[:count], *refs[count + len(after) :], **sizes)

    return pl.pallas_call(
        body,
        grid_spec=pltpu.PrefetchScalarGridSpec(
            num_scalar_prefetch=1,
            grid=grid,
            in_specs=list(in_specs) + [pl.BlockSpec(memory_space=pl.ANY)] * len(after),
            out_specs=out_specs,
            scratch_shapes=scratch,
        ),
        out_shape=out_shape,
        compiler_params=pltpu.CompilerParams(
            dimension_semantics=("arbitrary",) * len(grid), vmem_limit_bytes=VMEM_BYTES
        ),
        name=name,
    )(info, *arrays, *after)


def tie(value, *earlier):
    if not earlier:
        return value
    return pl.pallas_call(
        lambda *refs: None,
        out_shape=jax.ShapeDtypeStruct(value.shape, value.dtype),
        in_specs=[pl.BlockSpec(memory_space=pl.ANY)] * (1 + len(earlier)),
        out_specs=pl.BlockSpec(memory_space=pl.ANY),
        input_output_aliases={0: 0},
        name="tie",
    )(value, *earlier)


ANYWHERE = pl.BlockSpec(memory_space=pl.ANY)


def assemble(plan, arrays, after=()):
    count = len(arrays)
    steps = [(out, *part) for out, (_, parts) in enumerate(plan) for part in parts]

    def kernel(*refs):
        targets = refs[count + len(after) :][: len(plan)]
        held = refs[count + len(after) + len(plan) : -2]
        into, back = refs[-2:]

        def place(buffers, out, rows, columns, row, column):
            return buffers[out].at[
                row : row + rows[1] - rows[0], column : column + columns[1] - columns[0]
            ]

        loads, stores = [], []
        for at, (out, which, rows, columns, row, column) in enumerate(steps):
            source = refs[which].at[rows[0] : rows[1], columns[0] : columns[1]]
            target = place(held, out, rows, columns, row, column)
            loads.append(pltpu.make_async_copy(source, target, into.at[at]))
            loads[-1].start()
        for at, (out, _, rows, columns, row, column) in enumerate(steps):
            loads[at].wait()
            source = place(held, out, rows, columns, row, column)
            target = place(targets, out, rows, columns, row, column)
            stores.append(pltpu.make_async_copy(source, target, back.at[at]))
            stores[-1].start()
        for store in stores:
            store.wait()

    return pl.pallas_call(
        kernel,
        out_shape=[jax.ShapeDtypeStruct(shape, arrays[0].dtype) for shape, _ in plan],
        in_specs=[ANYWHERE] * (count + len(after)),
        out_specs=[ANYWHERE] * len(plan),
        scratch_shapes=[pltpu.VMEM(shape, arrays[0].dtype) for shape, _ in plan]
        + [pltpu.SemaphoreType.DMA((len(steps),))] * 2,
        compiler_params=pltpu.CompilerParams(vmem_limit_bytes=VMEM_BYTES),
        name="assemble",
    )(*arrays, *after)


def stacked(arrays, after=()):
    rows, parts = 0, []
    for at, array in enumerate(arrays):
        parts.append((at, (0, array.shape[0]), (0, array.shape[1]), rows, 0))
        rows += array.shape[0]
    return assemble([((rows, arrays[0].shape[1]), parts)], arrays, after)[0]


def ring_add(ups, downs, left, right, partly, after=()):
    count = len(ups)
    total = sum(grad.shape[1] for grad, _ in ups)
    tile = left.shape[0] if partly else left.shape[0] // 2

    def kernel(*refs):
        mine_up, mine_down = refs[:count], refs[count : 2 * count]
        came_up, came_down = refs[2 * count : 2 * count + 2]
        out_up, out_down = refs[-2:]
        step = pl.program_id(0)
        column = 0
        for up, down in zip(mine_up, mine_down):
            cut = slice(column, column + up.shape[1])
            column += up.shape[1]
            for mine, came, out, when in ((up, came_up, out_up, 0), (down, came_down, out_down, 1)):

                def add(mine=mine, came=came, out=out, cut=cut):
                    out[:, cut] = (mine[...].astype(F32) + came[:, cut].astype(F32)).astype(BF16)

                def keep(mine=mine, out=out, cut=cut):
                    out[:, cut] = mine[...]

                if partly:
                    pl.when(step == when)(add)
                    pl.when(step != when)(keep)
                else:
                    add()

    def of_block(grad, at):
        return pl.BlockSpec((tile, grad.shape[1]), lambda i: (2 * at + i, 0))

    came = pl.BlockSpec((tile, total), lambda i: (0 if partly else i, 0))
    out = pl.BlockSpec((tile, total), lambda i: (i, 0))
    shape = jax.ShapeDtypeStruct((2 * tile, total), BF16)
    return pl.pallas_call(
        kernel,
        grid=(2,),
        out_shape=[shape, shape],
        in_specs=[of_block(*block) for block in ups]
        + [of_block(*block) for block in downs]
        + [came, came]
        + [ANYWHERE] * len(after),
        out_specs=[out, out],
        compiler_params=pltpu.CompilerParams(
            dimension_semantics=("arbitrary",), vmem_limit_bytes=VMEM_BYTES
        ),
        name="ring_add",
    )(*[grad for grad, _ in ups], *[grad for grad, _ in downs], left, right, *after)


def row_blocks(left, right, blocks, count, after=()):
    size = left.shape[1] // count

    def kernel(left_ref, right_ref, *refs):
        refs[-1][...] = lax.dot_general(
            left_ref[...], right_ref[...], TN, preferred_element_type=F32
        ).astype(BF16)

    def block(i):
        found = blocks[0]
        for at, wanted in enumerate(blocks[1:], 1):
            found = jnp.where(i >= at, wanted, found)
        return 0, found

    return pl.pallas_call(
        kernel,
        grid=(len(blocks),),
        in_specs=[
            pl.BlockSpec((left.shape[0], size), block),
            pl.BlockSpec(right.shape, lambda i: (0, 0)),
        ]
        + [ANYWHERE] * len(after),
        out_specs=pl.BlockSpec((size, right.shape[1]), lambda i: (i, 0)),
        out_shape=jax.ShapeDtypeStruct((len(blocks) * size, right.shape[1]), BF16),
        compiler_params=pltpu.CompilerParams(
            dimension_semantics=("arbitrary",), vmem_limit_bytes=VMEM_BYTES
        ),
        name="row_blocks",
    )(left, right, *after)


def matmul(pairs, dims, dtype, after=(), pieces=0):
    if dims == NT:
        rows, columns = pairs[0][0].shape[0], pairs[0][1].shape[0]
        tile = 512 if columns % 512 == 0 else columns
        grid, pick = columns // tile, lambda i: (0, i)
        specs = [
            (pl.BlockSpec(left.shape, lambda i: (0, 0)),
             pl.BlockSpec((tile, right.shape[1]), lambda i: (i, 0)))
            for left, right in pairs
        ]
        shape = (rows, tile)
    else:
        over = 1 if dims == TN else 0
        rows, columns = pairs[0][0].shape[over], pairs[0][1].shape[1]
        tile = 256
        grid, pick = rows // tile, lambda i: (i, 0)
        specs = [
            (pl.BlockSpec((left.shape[0], tile), lambda i: (0, i)) if dims == TN
             else pl.BlockSpec((tile, left.shape[1]), lambda i: (i, 0)),
             pl.BlockSpec(right.shape, lambda i: (0, 0)))
            for left, right in pairs
        ]
        shape = (tile, columns)
    count = 2 * len(pairs)
    half = rows // 2

    def kernel(*refs):
        total = None
        for at in range(0, count, 2):
            product = lax.dot_general(
                refs[at][...], refs[at + 1][...], dims, preferred_element_type=F32
            )
            total = product if total is None else total + product
        outs = refs[count + len(after) :]
        if pieces:
            outs[0][...] = total[:half].astype(dtype)
            for at in range(pieces):
                first = half + at * (half // pieces)
                outs[1 + at][...] = total[first : first + half // pieces].astype(dtype)
        else:
            outs[0][...] = total.astype(dtype)

    if pieces:
        heights = [half] + [half // pieces] * pieces
        out_specs = [pl.BlockSpec((height, tile), pick) for height in heights]
        out_shape = [jax.ShapeDtypeStruct((height, columns), dtype) for height in heights]
    else:
        out_specs = [pl.BlockSpec(shape, pick)]
        out_shape = [jax.ShapeDtypeStruct((rows, columns), dtype)]
    found = pl.pallas_call(
        kernel,
        grid=(grid,),
        in_specs=[spec for both in specs for spec in both] + [ANYWHERE] * len(after),
        out_specs=out_specs,
        out_shape=out_shape,
        compiler_params=pltpu.CompilerParams(
            dimension_semantics=("arbitrary",), vmem_limit_bytes=VMEM_BYTES
        ),
        name="matmul",
    )(*[array for both in pairs for array in both], *after)
    return found if pieces else found[0]


def weighted(body, parts, cuts, operands, specs, out_specs, out_shape, steps, name, after=()):
    count, given, kept = len(parts), len(operands), len(cuts)
    rows, columns = sum(part.shape[0] for part in parts), parts[0].shape[1]

    def kernel(*refs):
        sources, mine = refs[:count], refs[count : count + given]
        rest = refs[count + given + len(after) :]
        held, into, back = rest[-3:]
        stores = [
            pltpu.make_async_copy(held.at[:, low:high], rest[at], back.at[at])
            for at, (low, high) in enumerate(cuts)
        ]

        @pl.when(pl.program_id(0) == 0)
        def _():
            loads, row = [], 0
            for at, source in enumerate(sources):
                target = held.at[row : row + source.shape[0]]
                loads.append(pltpu.make_async_copy(source, target, into.at[at]))
                loads[-1].start()
                row += source.shape[0]
            for load in loads:
                load.wait()
            for store in stores:
                store.start()

        body(held, mine, rest[kept:-3])

        @pl.when(pl.program_id(0) == steps - 1)
        def _():
            for store in stores:
                store.wait()

    dtype = parts[0].dtype
    weights = [jax.ShapeDtypeStruct((rows, high - low), dtype) for low, high in cuts]
    found = pl.pallas_call(
        kernel,
        grid=(steps,),
        in_specs=[ANYWHERE] * count + specs + [ANYWHERE] * len(after),
        out_specs=[ANYWHERE] * kept + out_specs,
        out_shape=weights + out_shape,
        scratch_shapes=[
            pltpu.VMEM((rows, columns), dtype),
            pltpu.SemaphoreType.DMA((count,)),
            pltpu.SemaphoreType.DMA((kept,)),
        ],
        compiler_params=pltpu.CompilerParams(
            dimension_semantics=("arbitrary",), vmem_limit_bytes=VMEM_BYTES
        ),
        name=name,
    )(*parts, *operands, *after)
    return found[:kept], found[kept:]


ROW_TILE = 256


def tiles_of(columns):
    return pl.BlockSpec((ROW_TILE, columns), lambda i: (i, 0))


def project(rows, rim, parts, after=()):
    columns = parts[0].shape[1]

    def body(held, given, outs):
        rows_ref, rim_ref = given
        outs[0][...] = jnp.dot(rows_ref[...], held[...], preferred_element_type=F32)

        @pl.when(pl.program_id(0) == 0)
        def _():
            outs[1][...] = jnp.dot(rim_ref[...], held[...], preferred_element_type=F32)

    (weights,), (projected, rim_projected) = weighted(
        body,
        parts,
        [(0, columns)],
        (rows, rim),
        [tiles_of(rows.shape[1]), pl.BlockSpec(rim.shape, lambda i: (0, 0))],
        [tiles_of(columns), pl.BlockSpec((rim.shape[0], columns), lambda i: (0, 0))],
        [
            jax.ShapeDtypeStruct((rows.shape[0], columns), F32),
            jax.ShapeDtypeStruct((rim.shape[0], columns), F32),
        ],
        rows.shape[0] // ROW_TILE,
        "project",
        after,
    )
    return projected, rim_projected, weights


def gate_project(rows, parts, width, after=()):
    def body(held, given, outs):
        outs[0][...] = jnp.dot(given[0][...], held[:, :width], preferred_element_type=F32)

    (first, second), (found,) = weighted(
        body,
        parts,
        [(0, width), (width, parts[0].shape[1])],
        (rows,),
        [tiles_of(rows.shape[1])],
        [tiles_of(width)],
        [jax.ShapeDtypeStruct((rows.shape[0], width), F32)],
        rows.shape[0] // ROW_TILE,
        "gate_project",
        after,
    )
    return found, first, second


def feed_forward(rows, cotangent, parts, after=()):
    width = parts[0].shape[1] // 3

    def body(held, given, outs):
        rows_ref, cotangent_ref = given
        hidden_ref, grad_ref = outs
        gate = jnp.dot(rows_ref[...], held[:, :width], preferred_element_type=F32)
        up = jnp.dot(rows_ref[...], held[:, width : 2 * width], preferred_element_type=F32)
        grad = jnp.dot(cotangent_ref[...], held[:, 2 * width :], preferred_element_type=F32)
        sig = jax.nn.sigmoid(gate)
        active = gate * sig
        hidden_ref[...] = (active * up).astype(BF16)
        grad_ref[:, :width] = (grad * up * sig * (1.0 + gate * (1.0 - sig))).astype(BF16)
        grad_ref[:, width:] = (grad * active).astype(BF16)

    model = rows.shape[1]
    (w_ffn, w_down), (hidden, grad) = weighted(
        body,
        parts,
        [(0, 2 * width), (2 * width, 3 * width)],
        (rows, cotangent),
        [tiles_of(model), tiles_of(model)],
        [tiles_of(width), tiles_of(2 * width)],
        [
            jax.ShapeDtypeStruct((rows.shape[0], width), BF16),
            jax.ShapeDtypeStruct((rows.shape[0], 2 * width), BF16),
        ],
        rows.shape[0] // ROW_TILE,
        "feed_forward",
        after,
    )
    return hidden, grad, w_ffn, w_down


class Mix:
    def __init__(self, info, micros, chunks, heads, key_size, value_size):
        self.info, self.micros, self.chunks = info, micros, chunks
        self.heads, self.key_size, self.value_size = heads, key_size, value_size
        self.width = heads * (2 * key_size + value_size)
        self.wide = key_size + value_size
        self.rows = micros * chunks * CHUNK
        self.sizes = dict(heads=heads, key_size=key_size, value_size=value_size)

    def block(self, m, c, info):
        return rank_block(c, info[0, info.shape[1] - 1]) * self.micros + m

    def by_rows(self, columns, turned=False):
        def place(m, c, info):
            return self.block(m, self.chunks - 1 - c if turned else c, info), 0

        return pl.BlockSpec((CHUNK, columns), place)

    def by_chunk(self, rows, columns, turned=False):
        def place(m, c, info):
            return m * self.chunks + (self.chunks - 1 - c if turned else c), 0, 0, 0

        return pl.BlockSpec((1, self.heads, rows, columns), place)

    def by_micro(self, *dims):
        return pl.BlockSpec((1,) + dims, lambda m, c, info: (m,) + (0,) * len(dims))

    def whole(self, *dims):
        return pl.BlockSpec(dims, lambda m, c, info: (0,) * len(dims))

    def like(self, dtype, *dims):
        return jax.ShapeDtypeStruct(dims, dtype)

    def call(self, kernel, arrays, in_specs, outs, scratch, name, after, **more):
        return kernel_call(
            kernel,
            self.info,
            arrays,
            (self.micros, self.chunks),
            in_specs,
            [spec for spec, _ in outs],
            [shape for _, shape in outs],
            scratch,
            name,
            after,
            **self.sizes,
            **more,
        )

    def forward(self, projected, rim, taps, par, after=()):
        h, dk, dv, wide, width = self.heads, self.key_size, self.value_size, self.wide, self.width
        steps = self.micros * self.chunks
        return self.call(
            mix_forward_kernel,
            (projected, rim, taps, par),
            [
                self.by_rows(width + LANES),
                pl.BlockSpec((HALO, width + LANES), lambda m, c, info: (m, 0)),
                self.whole(8, width),
                self.whole(8, LANES),
            ],
            [
                (self.by_rows(h * dv), self.like(F32, self.rows, h * dv)),
                (self.by_rows(h * dk), self.like(BF16, self.rows, h * dk)),
                (self.by_chunk(CHUNK, CHUNK), self.like(BF16, steps, h, CHUNK, CHUNK)),
                (self.by_chunk(dk, wide), self.like(BF16, steps, h, dk, wide)),
                (self.by_micro(h, dk, wide), self.like(F32, self.micros, h, dk, wide)),
            ],
            [pltpu.VMEM((HALO, width), BF16), pltpu.VMEM((h, dk, wide), F32)],
            "mix_forward",
            after,
            seq_count=self.info.shape[1] - 2,
        )

    def backward(
        self, projected, rim, taps, par, grad, inverses, starts, incoming, leaving, after=()
    ):
        h, dk, dv, wide, width = self.heads, self.key_size, self.value_size, self.wide, self.width
        halo_blocks = CHUNK // HALO

        def before(m, c, info):
            earlier = jnp.maximum(self.chunks - 2 - c, 0)
            return (self.block(m, earlier, info) + 1) * halo_blocks - 1, 0

        return self.call(
            mix_backward_kernel,
            (projected, projected, rim, taps, par, grad, inverses, starts, incoming, leaving),
            [
                self.by_rows(width + LANES, True),
                pl.BlockSpec((HALO, width + LANES), before),
                pl.BlockSpec((HALO, width + LANES), lambda m, c, info: (m, 0)),
                self.whole(8, width),
                self.whole(8, LANES),
                self.by_rows(h * dv, True),
                self.by_chunk(CHUNK, CHUNK, True),
                self.by_chunk(dk, wide, True),
                self.by_micro(h, dk, dv),
                self.by_micro(h, dk, dv),
            ],
            [
                (self.by_rows(width + LANES, True), self.like(BF16, self.rows, width + LANES)),
                (self.by_micro(8, width), self.like(F32, self.micros, 8, width)),
                (self.by_micro(HALO, width), self.like(F32, self.micros, HALO, width)),
                (self.whole(8, width), self.like(F32, 8, width)),
                (self.whole(8, LANES), self.like(F32, 8, LANES)),
            ],
            [pltpu.VMEM((8, width), F32), pltpu.VMEM((h, dk, dv), F32)],
            "mix_backward",
            after,
            seq_count=self.info.shape[1] - 2,
        )

    def gate_forward(self, plain, cmap, incoming, gate, gain, after=()):
        h, dk, dv = self.heads, self.key_size, self.value_size
        return self.call(
            gate_forward_kernel,
            (plain, cmap, incoming, gate, gain),
            [
                self.by_rows(h * dv),
                self.by_rows(h * dk),
                self.by_micro(h, dk, dv),
                self.by_rows(h * dv),
                self.whole(8, dv),
            ],
            [
                (self.by_rows(h * dv), self.like(F32, self.rows, h * dv)),
                (self.by_rows(h * dv), self.like(BF16, self.rows, h * dv)),
            ],
            [],
            "gate_forward",
            after,
        )

    def gate_backward(self, grad, mixed, cmap, gate, gain, after=()):
        h, dk, dv = self.heads, self.key_size, self.value_size
        return self.call(
            gate_backward_kernel,
            (grad, mixed, cmap, gate, gain),
            [
                self.by_rows(h * dv),
                self.by_rows(h * dv),
                self.by_rows(h * dk),
                self.by_rows(h * dv),
                self.whole(8, dv),
            ],
            [
                (self.by_rows(h * dv), self.like(BF16, self.rows, h * dv)),
                (self.by_rows(h * dv), self.like(F32, self.rows, h * dv)),
                (self.by_micro(h, dk, dv), self.like(F32, self.micros, h, dk, dv)),
                (self.whole(8, dv), self.like(F32, 8, dv)),
            ],
            [],
            "gate_backward",
            after,
        )


def from_behind(value, axis, steps):
    count = lax.axis_size(axis)
    leading, last = (max(0, -steps), min(count, count - steps))
    return lax.ppermute(value, axis, [(source, source + steps) for source in range(leading, last)])


def swap(value, axis, bit):
    return lax.ppermute(value, axis, [(at, at ^ bit) for at in range(lax.axis_size(axis))])


def rank_block(rank, mine):
    apart = jnp.bitwise_xor(rank, mine)
    return 2 * jnp.bitwise_and(apart, 1) + jnp.right_shift(apart, 1)


def cut_rows(value, count):
    size = value.shape[0] // count
    return [value[at * size : (at + 1) * size] for at in range(count)]


class HeadGather:
    def __init__(self, value):
        self.value = value
        self.across = [swap(part, "head", 2) for part in cut_rows(value, PIECES // 2)]

    def pass_on(self, *after):
        self.pair = stacked([self.value, *self.across], after)
        self.near = [swap(part, "head", 1) for part in cut_rows(self.pair, PIECES)]
        return (self.pair,)

    def rows(self, *after):
        return stacked([self.pair, *self.near], after)


class HeadScatter:
    def __init__(self, mine, *sent):
        self.pieces = max(len(sent), 2)
        self.mine, self.sent = cut_rows(mine, self.pieces), sent
        self.near = [swap(part, "head", 1) for part in sent]

    def pass_on(self, *after):
        half = self.pieces // 2
        self.near = [tie(part, *after) for part in self.near]
        if len(self.near) == 1:
            self.near = cut_rows(self.near[0], 2)
        theirs = [
            (mine.astype(F32) + near.astype(F32)).astype(BF16)
            for mine, near in zip(self.mine[half:], self.near[half:])
        ]
        self.across = [swap(part, "head", 2) for part in theirs]
        return tuple(theirs)

    def total(self, *after):
        parts = zip(self.mine, self.near, self.across)
        return jnp.concatenate(
            [
                mine.astype(F32) + near.astype(F32) + tie(across, *after).astype(F32)
                for mine, near, across in parts
            ],
            axis=0,
        )


class Summed:
    def __init__(self, value, hops):
        self.value, self.hops, self.came = value, list(hops), []

    def step(self, *after):
        if not self.came and after:
            self.value = tie(self.value, *after)
        for came in self.came:
            self.value = self.value + tie(came, *after)
        self.came = []
        if self.hops:
            axis, turns = self.hops.pop(0)
            self.came = [swap(self.value, axis, turn) for turn in turns]
        return (self.value,)

    def total(self):
        while self.came:
            self.step()
        return self.value


def head_hops():
    return [("head", [1 << at]) for at in range((lax.axis_size("head") - 1).bit_length())]


def dp_hops():
    count = lax.axis_size("dp")
    if count <= 8:
        return [("dp", [1]), ("dp", list(range(2, count, 2)))]
    return [("dp", [1 << at]) for at in range((count - 1).bit_length())]


def ring_order():
    count = lax.axis_size("dp")
    return list(range(0, count, 2)) + list(range(count - 1, 0, -2))


def ring_place():
    count, mine = lax.axis_size("dp"), lax.axis_index("dp")
    return jnp.where(mine % 2 == 0, mine // 2, count - 1 - mine // 2)


def ring_steps():
    ring = ring_order()
    ahead = [(ring[at], ring[(at + 1) % len(ring)]) for at in range(len(ring))]
    return ahead, [(after, before) for before, after in ahead]


def reorder_kernel(order_ref, *refs, size, outward):
    count = len(refs) // 2
    for source, target in zip(refs[:count], refs[count:]):
        for at in range(order_ref.shape[0]):
            moved = pl.ds(pl.multiple_of(order_ref[at] * size, size), size)
            here = slice(at * size, (at + 1) * size)
            if outward:
                target[:, moved] = source[:, here]
            else:
                target[:, here] = source[:, moved]


def reorder(arrays, outward, after=()):
    ring = ring_order()
    count, place = len(ring), ring_place()
    size = arrays[0].shape[1] // count
    around = jnp.asarray(ring + ring, jnp.int32)
    order = lax.dynamic_slice(around, (place,), (count,))
    if size % LANES == 0:
        return kernel_call(
            reorder_kernel,
            order,
            arrays,
            (1,),
            [pl.BlockSpec(a.shape, lambda i, info: (0, 0)) for a in arrays],
            [pl.BlockSpec(a.shape, lambda i, info: (0, 0)) for a in arrays],
            [jax.ShapeDtypeStruct(a.shape, a.dtype) for a in arrays],
            [],
            "reorder",
            after,
            size=size,
            outward=outward,
        )
    if outward:
        ranks = jnp.arange(count, dtype=jnp.int32)
        order = jnp.sum(jnp.where(order[None, :] == ranks[:, None], ranks[None, :], 0), axis=1)
    return [
        jnp.take(a.reshape(-1, count, size), order, axis=1).reshape(a.shape) for a in arrays
    ]


class Gather:
    def __init__(self, shard):
        self.ahead, self.back = ring_steps()
        self.left, self.right, self.far = [shard], [shard], None

    def step(self, *after):
        if len(self.left) > 1 or after:
            self.left[-1] = tie(self.left[-1], *after)
            self.right[-1] = self.left[0] if len(self.left) == 1 else tie(self.right[-1], *after)
        sent = self.left[-1], self.right[-1]
        if len(self.left) < len(self.ahead) // 2:
            self.left.append(lax.ppermute(self.left[-1], "dp", self.ahead))
            self.right.append(lax.ppermute(self.right[-1], "dp", self.back))
        else:
            half = self.left[0].shape[0] // 2
            self.far = [
                lax.ppermute(self.left[-1][:half], "dp", self.ahead),
                lax.ppermute(self.right[-1][half:], "dp", self.back),
            ]
        return sent

    def run(self, *after):
        while self.far is None:
            after = self.step(*after)
        return after

    def came(self):
        return self.left[-1], self.right[-1]

    def parts(self):
        return [self.left[0]] + self.right[1:] + self.far + self.left[:0:-1]


class Scatter:
    def __init__(self, *pairs, after=()):
        self.ahead, self.back = ring_steps()
        self.pairs, self.count = pairs, len(self.ahead)
        self.size = pairs[0][0].shape[1] // self.count
        self.apart = self.size % LANES == 0
        self.at = middle = self.count // 2
        self.left = self.right = None
        self.blocks = [{} for _ in pairs]
        self.groups = [[middle]]
        if self.count > 4:
            self.groups.append([middle - 1, middle + 1])
        self.groups.append([at for at in range(self.count) if all(at not in g for g in self.groups)])
        if self.apart:
            self.work(0, after=after)
        else:
            for which, pair in enumerate(pairs):
                whole = matmul([pair], TN, BF16, after)
                self.blocks[which] = {at: (whole, at) for at in range(self.count)}

    def work(self, group, only=None, after=()):
        found = []
        for which, pair in enumerate(self.pairs):
            if self.apart and only in (None, which):
                found.append(row_blocks(*pair, self.groups[group], self.count, after))
                for place, at in enumerate(self.groups[group]):
                    self.blocks[which][at] = (found[-1], place)
        return tuple(found) or tuple(after)

    def of(self, at):
        return [blocks[at] for blocks in self.blocks]

    def step(self, *after):
        middle, half = self.count // 2, self.size // 2
        if self.at == middle:
            plan, arrays = [], [grad for grad, _ in self.of(middle)]
            for start in (0, half):
                column, items = 0, []
                for at, (grad, place) in enumerate(self.of(middle)):
                    first, width = place * self.size + start, grad.shape[1]
                    items.append((at, (first, first + half), (0, width), 0, column))
                    column += width
                plan.append(((half, column), items))
            up, down = assemble(plan, arrays, after)
        else:
            up, down = ring_add(
                self.of(self.at),
                self.of(self.count - self.at),
                self.left,
                self.right,
                self.at == middle - 1,
                after,
            )
        self.left = lax.ppermute(up, "dp", self.ahead)
        self.right = lax.ppermute(down, "dp", self.back)
        self.at -= 1
        return up, down

    def came(self):
        return self.left, self.right

    def total(self, *after):
        while self.at > 0:
            after = self.step(*after)
        mine = [
            grad[place * self.size : (place + 1) * self.size] for grad, place in self.of(0)
        ]
        mine = mine[0] if len(mine) == 1 else jnp.concatenate(mine, axis=1)
        left, right = tie(self.left, *after), tie(self.right, *after)
        return mine.astype(F32) + left.astype(F32) + right.astype(F32)


def apply_map(moves, state, turned=False):
    return jnp.einsum(
        "hji,hjv->hiv" if turned else "hij,hjv->hiv",
        moves.astype(BF16),
        state.astype(BF16),
        preferred_element_type=F32,
    )


def own_and_swapped(value, bit):
    sent = jnp.where(bit == 0, value[1], value[0]).astype(BF16)
    theirs = swap(sent, "dp", 1).astype(F32)
    mine = jnp.where(bit == 0, value[0], value[1]).astype(F32)
    return jnp.where(bit == 0, mine, theirs), jnp.where(bit == 0, theirs, mine), sent


def hand_back(first, second, bit):
    mine = jnp.where(bit == 0, first, second).astype(BF16)
    sent = jnp.where(bit == 0, second, first).astype(BF16)
    theirs = swap(sent, "dp", 1)
    return jnp.stack([jnp.where(bit == 0, mine, theirs), jnp.where(bit == 0, theirs, mine)]), sent


class Scan:
    def __init__(self, final, value_size):
        self.bit, self.pairs = lax.axis_index("dp") % 2, lax.axis_size("dp") // 2
        self.cut = value_size
        self.sent = jnp.where(self.bit == 0, final[1], final[0]).astype(BF16)
        self.mine = jnp.where(self.bit == 0, final[0], final[1]).astype(F32)
        self.theirs = swap(self.sent, "dp", 1)

    def ordered(self, *after):
        theirs = tie(self.theirs, *after).astype(F32)
        return (
            jnp.where(self.bit == 0, self.mine, theirs),
            jnp.where(self.bit == 0, theirs, self.mine),
        )

    def shifted(self, value, steps):
        return [from_behind(value, "dp", 2 * sign) for sign in steps]

    def send(self, *after):
        self.first, self.second = self.ordered(*after)
        cut = self.cut
        self.first_map, self.second_map = self.first[..., cut:], self.second[..., cut:]
        pair_map = apply_map(self.second_map, self.first_map)
        self.pair_map = pair_map.astype(BF16)
        pair_sum = apply_map(self.second_map, self.first[..., :cut]) + self.second[..., :cut]
        both = jnp.concatenate([pair_sum, pair_map], axis=-1).astype(BF16)
        self.before = self.shifted(both, range(1, self.pairs))
        return (both,)

    def finish(self, *after):
        state = jnp.zeros(self.first[..., : self.cut].shape, F32)
        for both in self.before[::-1]:
            both = tie(both, *after)
            after = ()
            state = apply_map(both[..., self.cut :], state) + both[..., : self.cut].astype(F32)
        after_first = apply_map(self.first_map, state) + self.first[..., : self.cut]
        return self.hand_back(state, after_first)

    def hand_back(self, first, second):
        mine = jnp.where(self.bit == 0, first, second).astype(BF16)
        sent = jnp.where(self.bit == 0, second, first).astype(BF16)
        theirs = swap(sent, "dp", 1)
        states = [jnp.where(self.bit == 0, *pair) for pair in ((mine, theirs), (theirs, mine))]
        return jnp.stack(states), (sent,)


class ScanBack(Scan):
    def __init__(self, local, ahead):
        self.of = ahead
        super().__init__(local, local.shape[-1])

    def send(self, *after):
        self.first, self.second = self.ordered(*after)
        pair_sum = (apply_map(self.of.first_map, self.second, True) + self.first).astype(BF16)
        both = jnp.concatenate([pair_sum, self.of.pair_map], axis=-1)
        self.behind = self.shifted(both, [-step for step in range(1, self.pairs)])
        return (both,)

    def finish(self, *after):
        state = jnp.zeros(self.first.shape, F32)
        for both in self.behind[::-1]:
            both = tie(both, *after)
            after = ()
            moves = both[..., self.cut :]
            state = apply_map(moves, state, True) + both[..., : self.cut].astype(F32)
        before_second = apply_map(self.of.second_map, state, True) + self.second
        return self.hand_back(before_second, state)


def norm_backward(grad_in, normed_rows, scale):
    return scale * (grad_in - normed_rows * jnp.mean(grad_in * normed_rows, axis=-1, keepdims=True))


def body(
    tokens,
    out_grad,
    seq_lengths,
    attn_norm,
    query_proj,
    key_proj,
    value_proj,
    gate_proj,
    decay_proj,
    beta_proj,
    conv_query,
    conv_key,
    conv_value,
    log_rate,
    step_bias,
    head_norm,
    out_proj,
    ffn_norm,
    ffn_gate,
    ffn_up,
    ffn_down,
):
    head_rank, ranks = lax.axis_index("head"), lax.axis_size("head")
    heads = decay_proj.shape[1]
    qk_width = query_proj.shape[1]
    v_width = value_proj.shape[1]
    key_size = qk_width // heads
    value_size = v_width // heads
    ffn_width = ffn_gate.shape[1]
    conv_width = 2 * qk_width + v_width
    micros, part_rows, model = tokens.shape
    assert part_rows == CHUNK and micros == 2 and ranks == 4

    decay_pad = jnp.zeros((decay_proj.shape[0], LANES - 2 * heads), decay_proj.dtype)
    conv_ring = Gather(
        jnp.concatenate(
            [query_proj, key_proj, value_proj, decay_proj, beta_proj, decay_pad], axis=1
        )
    )
    gate_ring = Gather(jnp.concatenate([gate_proj, out_proj.T], axis=1))
    ffn_ring = Gather(jnp.concatenate([ffn_gate, ffn_up, ffn_down.T], axis=1))

    def of_mine(whole, width):
        return lax.dynamic_slice_in_dim(whole, head_rank * width, width, whole.ndim - 1)

    taps = jnp.concatenate(
        [of_mine(conv_query, qk_width), of_mine(conv_key, qk_width), of_mine(conv_value, v_width)],
        axis=1,
    )
    taps = jnp.pad(taps, ((0, 8 - KCONV), (0, 0)))
    par = jnp.pad(
        jnp.stack([-jnp.exp(of_mine(log_rate, heads)), of_mine(step_bias, heads)]),
        ((0, 6), (0, LANES - heads)),
    )
    gain = jnp.broadcast_to(head_norm, (8, value_size))

    def flat(value):
        return value.reshape(-1, value.shape[-1])

    def ranked(value):
        return value.reshape(ranks, micros, part_rows, value.shape[-1])

    conv_ring.step()
    turned, cotangent, attn_gain, ffn_gain = reorder(
        [
            flat(tokens),
            flat(out_grad),
            jnp.broadcast_to(attn_norm, (8, model)),
            jnp.broadcast_to(ffn_norm, (8, model)),
        ],
        False,
    )
    attn_gain, ffn_gain = attn_gain[0], ffn_gain[0]
    residual = turned.astype(F32)
    scale_one = lax.rsqrt(jnp.mean(residual * residual, axis=-1, keepdims=True) + EPSILON)
    normed_one = residual * scale_one
    normed_rows = HeadGather((normed_one * attn_gain).astype(BF16))
    conv_ring.step()
    (pair,) = normed_rows.pass_on(*conv_ring.came(), gate_ring.left[0], ffn_ring.left[0])
    conv_ring.step()
    normed_all = normed_rows.rows(*conv_ring.came())
    last_chunk = rank_block(ranks - 1, head_rank)
    last_rows = lax.dynamic_slice(
        ranked(normed_all), (last_chunk, 0, part_rows - HALO, 0), (1, micros, HALO, model)
    )
    conv_ring.run()
    rim_rows = from_behind(reorder([flat(last_rows)], True)[0], "dp", 1)
    rim_rows = reorder([rim_rows], False)[0]
    first_row = lax.axis_index("dp") * ranks * part_rows
    ends = jnp.cumsum(seq_lengths, axis=1)
    info = jnp.concatenate(
        [
            ends - seq_lengths,
            jnp.full((micros, 1), first_row, jnp.int32),
            jnp.full((micros, 1), head_rank, jnp.int32),
        ],
        axis=1,
    ).astype(jnp.int32)
    mix = Mix(info, micros, ranks, heads, key_size, value_size)
    now = gate_ring.step(rim_rows, *conv_ring.far)
    projected, rim, w_conv = project(normed_all, rim_rows, conv_ring.parts(), now)
    now = gate_ring.step(rim)
    now = ffn_ring.step(*now)

    plain, carried_map, inverses, starts, final = mix.forward(projected, rim, taps, par, now)
    scan = Scan(final, value_size)
    now = scan.send(scan.sent, *gate_ring.came(), *ffn_ring.came())
    cotangent_rows = HeadGather(tie(cotangent, *now))
    now = gate_ring.step(*now, *scan.before)
    now = cotangent_rows.pass_on(*now)
    incoming, now = scan.finish(*now)
    cotangent_all = cotangent_rows.rows(*now)
    now = gate_ring.run(*now)
    now = ffn_ring.step(incoming, *gate_ring.far, cotangent_all)
    gate_lin, w_gate, w_out = gate_project(normed_all, gate_ring.parts(), v_width, now)
    mixed, gated = mix.gate_forward(plain, carried_map, incoming, gate_lin, gain)

    mix_sum = HeadScatter(*matmul([(gated, w_out)], NT, BF16, pieces=PIECES))
    now = ffn_ring.step(*mix_sum.sent)
    now = mix_sum.pass_on(*now)
    after_mix = residual + mix_sum.total(*now)
    scale_two = lax.rsqrt(jnp.mean(after_mix * after_mix, axis=-1, keepdims=True) + EPSILON)
    normed_two = after_mix * scale_two
    ffn_rows = HeadGather((normed_two * ffn_gain).astype(BF16))
    now = ffn_ring.run(ffn_rows.across[0])
    now = ffn_rows.pass_on(*now)
    ffn_all = ffn_rows.rows(*now)

    hidden, gate_up_grad, w_ffn, w_down = feed_forward(ffn_all, cotangent_all, ffn_ring.parts())
    ffn_in_sum = HeadScatter(*matmul([(gate_up_grad, w_ffn)], NT, BF16, pieces=PIECES))
    ffn_sums = Scatter(
        (ffn_all, gate_up_grad), (cotangent_all, hidden), after=ffn_in_sum.sent
    )
    now = ffn_sums.step()
    now = ffn_in_sum.pass_on(*now)
    now = ffn_sums.work(1, after=now)
    now = ffn_sums.step(*now)
    ffn_in_grad = ffn_in_sum.total(*now)
    grad_norm_two = jnp.sum(ffn_in_grad * normed_two, axis=0)
    after_mix_grad = cotangent.astype(F32) + norm_backward(
        ffn_in_grad * ffn_gain, normed_two, scale_two
    )
    branch_rows = HeadGather(after_mix_grad.astype(BF16))
    now = ffn_sums.work(2, after=(branch_rows.value,))
    now = branch_rows.pass_on(*now)
    branch_grad = branch_rows.rows(*now)
    now = (branch_grad,)

    gated_grad = matmul([(branch_grad, w_out)], NN, F32, now)
    gate_grad, mixed_grad, local_grad, grad_head_norm = mix.gate_backward(
        gated_grad, mixed, carried_map, gate_lin, gain, ffn_sums.came()
    )

    back = ScanBack(local_grad, scan)
    gate_sums = Scatter(
        (normed_all, gate_grad), (branch_grad, gated), after=(back.sent, *ffn_sums.came())
    )
    now = gate_sums.work(1, after=(back.sent,)) + gate_sums.work(2, 1, (back.sent,))
    now = back.send(*now)
    now = gate_sums.work(2, 0, now)
    now = gate_sums.step(*now, back.behind[-1])
    ffn_part = matmul([(hidden, w_down)], NT, BF16, now, pieces=PIECES)
    leaving, now = back.finish(ffn_part[0])
    now = ffn_sums.step(leaving, *gate_sums.came())
    now = gate_sums.step(*now)
    conv_grad, rim_grad, tail, taps_grad, par_grad = mix.backward(
        projected, rim, taps, par, mixed_grad, inverses, starts, incoming, leaving, now
    )
    back_rim = from_behind(rim_grad, "dp", -1)
    small = jnp.concatenate(
        [
            taps_grad[:KCONV].reshape(-1),
            jnp.pad(par_grad[0, :heads], (0, LANES - heads)),
            jnp.pad(par_grad[1, :heads], (0, LANES - heads)),
            grad_head_norm[0],
        ]
    ).reshape(-1, LANES)
    ffn_sum = HeadScatter(ffn_part[0], *[tie(part, rim_grad) for part in ffn_part[1:]])
    now = ffn_sums.step(back_rim, *gate_sums.came())
    now = ffn_sum.pass_on(*now)
    tail = tie(tail, back_rim)
    tail = jnp.concatenate([tail[:, :8], tail[:, 8:] + back_rim], axis=1).astype(BF16)
    conv_grad = lax.dynamic_update_slice(
        ranked(conv_grad), tail[None], (last_chunk, 0, part_rows - HALO, 0)
    ).reshape(-1, conv_width + LANES)

    conv_sums = Scatter((normed_all, conv_grad), after=now)
    now = conv_sums.step()
    now = conv_sums.work(1, after=now) + conv_sums.work(2, after=now)
    normed_part = matmul(
        [(conv_grad, w_conv), (gate_grad, w_gate)], NT, BF16, now, pieces=PIECES
    )
    normed_sum = HeadScatter(*normed_part)
    now = gate_sums.step(*normed_sum.sent, *ffn_sums.came(), *conv_sums.came())
    now = normed_sum.pass_on(*now)
    now = conv_sums.step(*now, *gate_sums.came())
    now = gate_sums.step(*now)
    now = conv_sums.step(*now)
    normed_grad = normed_sum.total(*now)
    now = conv_sums.step(*now, *gate_sums.came())
    grad_norm_one = jnp.sum(normed_grad * normed_one, axis=0)
    norm_grads = jnp.pad(jnp.stack([grad_norm_one, grad_norm_two]), ((0, 6), (0, 0)))
    (norm_grads,) = reorder([norm_grads], True, now)
    norm_sum = Summed(norm_grads[:2].reshape(-1, LANES), head_hops())
    norm_sum.step()
    norm_sum.step()
    input_grad = after_mix_grad + norm_backward(normed_grad * attn_gain, normed_one, scale_one)
    block_out = (after_mix + ffn_sum.total(*now)).astype(BF16)
    small_sum = Summed(jnp.concatenate([small, norm_sum.total()], axis=0), dp_hops())
    small_sum.step(*now)
    small_sum.step()
    block_out, input_grad = reorder([block_out, input_grad], True, now)
    block_out, input_grad = block_out.reshape(tokens.shape), input_grad.reshape(tokens.shape)
    shard_ffn = ffn_sums.total(*now)
    shard_gate = gate_sums.total(*now)
    shard_conv = conv_sums.total()
    small, norm_grads = small_sum.total()[: small.shape[0]], small_sum.total()[small.shape[0] :]
    norm_grads = norm_grads.reshape(2, model)

    across = jnp.stack([small, swap(small, "head", 2)])
    near = swap(across, "head", 1)
    small = jnp.stack([across[0], near[0], across[1], near[1]])
    small = jnp.stack([small[jnp.bitwise_xor(at, head_rank)] for at in range(ranks)])
    tap_rows = KCONV * conv_width // LANES
    taps_all = small[:, :tap_rows].reshape(ranks, KCONV, conv_width).transpose(1, 0, 2)

    def joined(low, high):
        return taps_all[:, :, low:high].reshape(KCONV, -1)

    rest = jnp.sum(small[:, tap_rows + 2 :], axis=0).reshape(-1)
    return (
        block_out,
        input_grad,
        norm_grads[0],
        shard_conv[:, :qk_width],
        shard_conv[:, qk_width : 2 * qk_width],
        shard_conv[:, 2 * qk_width : conv_width],
        shard_gate[:, :v_width],
        shard_conv[:, conv_width : conv_width + heads],
        shard_conv[:, conv_width + heads : conv_width + 2 * heads],
        joined(0, qk_width),
        joined(qk_width, 2 * qk_width),
        joined(2 * qk_width, conv_width),
        small[:, tap_rows, :heads].reshape(-1),
        small[:, tap_rows + 1, :heads].reshape(-1),
        rest[:value_size],
        shard_gate[:, v_width:].T,
        norm_grads[1],
        shard_ffn[:, :ffn_width],
        shard_ffn[:, ffn_width : 2 * ffn_width],
        shard_ffn[:, 2 * ffn_width :].T,
    )


def solution(mesh):
    rows, plane, turned, whole = P(None, ("dp", "head"), None), P("dp", "head"), P("head", "dp"), P()
    in_specs = (rows, rows, whole, whole) + (plane,) * 6 + (whole,) * 6
    in_specs += (turned, whole, plane, plane, turned)
    out_specs = (rows, rows, whole) + (plane,) * 6 + (whole,) * 6
    out_specs += (turned, whole, plane, plane, turned)
    return jax.shard_map(body, mesh=mesh, in_specs=in_specs, out_specs=out_specs, check_vma=False)
```

```python
from functools import partial

import jax
import jax.numpy as jnp
from jax import lax
from jax.experimental import pallas as pl
from jax.experimental.pallas import tpu as pltpu
from jax.sharding import PartitionSpec as P

CHUNK = 128
KCONV = 4
LANES = 128
HALO = 16

EPSILON = 1e-06
HEAD_FLOOR = 0.01
F32 = jnp.float32
BF16 = jnp.bfloat16
NN = (((1,), (0,)), ((), ()))
NT = (((1,), (1,)), ((), ()))
TN = (((0,), (0,)), ((), ()))


def mm(left, right, dims=NN):
    return lax.dot_general(
        left.astype(BF16), right.astype(BF16), dims, preferred_element_type=F32
    )


def split(value):
    high = value.astype(BF16)
    return high, (value - high.astype(F32)).astype(BF16)


def mm3(left, right, dims=NN):
    left_high, left_low = split(left)
    right_high, right_low = split(right)
    return mm(left_high, right_high, dims) + (
        mm(left_high, right_low, dims) + mm(left_low, right_high, dims)
    )


def chunk_places(info_ref, micro, chunk, seq_count):
    first = info_ref[micro, seq_count] + chunk * CHUNK
    starts = [info_ref[micro, at] for at in range(seq_count)]
    rows = first + lax.broadcasted_iota(jnp.int32, (CHUNK, 1), 0)
    lanes = first + lax.broadcasted_iota(jnp.int32, (1, CHUNK), 1)
    seg_col = jnp.zeros((CHUNK, 1), jnp.int32)
    seg_row = jnp.zeros((1, CHUNK), jnp.int32)
    begun = jnp.zeros((CHUNK, 1), jnp.int32)
    seg_before = jnp.int32(0)
    seg_last = jnp.int32(0)
    for start in starts:
        seg_col = seg_col + jnp.where(rows >= start, 1, 0)
        seg_row = seg_row + jnp.where(lanes >= start, 1, 0)
        begun = jnp.maximum(begun, jnp.where(rows >= start, start, 0))
        seg_before = seg_before + jnp.where(first - 1 >= start, 1, 0)
        seg_last = seg_last + jnp.where(first + CHUNK - 1 >= start, 1, 0)
    offset = rows - begun
    row_ids = lax.broadcasted_iota(jnp.int32, (CHUNK, CHUNK), 0)
    col_ids = lax.broadcasted_iota(jnp.int32, (CHUNK, CHUNK), 1)
    same = seg_col == seg_row
    return dict(
        row_ids=row_ids,
        col_ids=col_ids,
        inclusive=jnp.logical_and(row_ids >= col_ids, same),
        strictly=jnp.logical_and(row_ids > col_ids, same),
        untouched=jnp.where(seg_col == seg_before, 1.0, 0.0).astype(F32),
        with_last=jnp.where(seg_col == seg_last, 1.0, 0.0).astype(F32),
        lags=[jnp.where(offset >= lag, 1.0, 0.0).astype(F32) for lag in range(1, KCONV)],
    )


def decay_parts(g_col, places):
    row_ids, col_ids = places["row_ids"], places["col_ids"]
    cum_row = jnp.sum(jnp.where(row_ids <= col_ids, g_col, 0.0), axis=0, keepdims=True)
    cum_col = jnp.sum(jnp.where(row_ids == col_ids, cum_row, 0.0), axis=1, keepdims=True)
    spread = jnp.where(places["inclusive"], cum_col - cum_row, 0.0)
    pair = jnp.where(places["inclusive"], jnp.exp(spread), 0.0)
    carry = jnp.exp(cum_col) * places["untouched"]
    cum_last = cum_col[CHUNK - 1 :, :]
    to_last = jnp.exp(jnp.minimum(cum_last - cum_col, 0.0)) * places["with_last"]
    return pair, carry, to_last, carry[CHUNK - 1 :, :]


def conv_rows(extended, taps, lags):
    total = taps[KCONV - 1 :, :] * extended[HALO:]
    for lag in range(1, KCONV):
        shifted = extended[HALO - lag : HALO - lag + CHUNK]
        total = total + taps[KCONV - 1 - lag : KCONV - lag, :] * shifted * lags[lag - 1]
    return total


def head_columns(head, heads, key_size, value_size):
    return (
        (head * key_size, key_size),
        ((heads + head) * key_size, key_size),
        (2 * heads * key_size + head * value_size, value_size),
    )


def unit_rows(active):
    return active * lax.rsqrt(jnp.sum(active * active, axis=1, keepdims=True) + EPSILON)


def softplus(value):
    return jnp.maximum(value, 0.0) + jnp.log1p(jnp.exp(-jnp.abs(value)))


def unit_lower_inverses(systems, places):
    row_ids, col_ids = places["row_ids"], places["col_ids"]
    eye = jnp.where(row_ids == col_ids, 1.0, 0.0).astype(F32)
    pairs = jnp.right_shift(row_ids, 1) == jnp.right_shift(col_ids, 1)
    found = [eye - jnp.where(pairs, system, 0.0) for system in systems]
    level = 1
    while (1 << level) < CHUNK:
        row_block = jnp.right_shift(row_ids, level)
        col_block = jnp.right_shift(col_ids, level)
        lower = jnp.logical_and(
            jnp.right_shift(row_block, 1) == jnp.right_shift(col_block, 1), row_block > col_block
        )
        inner = [
            INVERSE_MM(jnp.where(lower, system, 0.0), inverse)
            for system, inverse in zip(systems, found)
        ]
        found = [
            inverse - INVERSE_MM(inverse, middle) for inverse, middle in zip(found, inner)
        ]
        level += 1
    return found


INVERSE_MM = mm3


def mix_forward_kernel(
    info_ref,
    x_ref,
    rim_ref,
    taps_ref,
    par_ref,
    out_ref,
    cmap_ref,
    inv_ref,
    start_ref,
    final_ref,
    halo,
    state,
    *,
    heads,
    key_size,
    value_size,
    seq_count,
):
    micro, chunk = pl.program_id(0), pl.program_id(1)
    span = range(heads)

    width = halo.shape[1]

    @pl.when(chunk == 0)
    def _():
        halo[...] = rim_ref[:, :width].astype(BF16)
        row_ids = lax.broadcasted_iota(jnp.int32, (key_size, key_size), 0)
        col_ids = lax.broadcasted_iota(jnp.int32, (key_size, key_size), 1)
        eye = jnp.where(row_ids == col_ids, 1.0, 0.0).astype(F32)
        for head in span:
            state[head] = jnp.concatenate([jnp.zeros((key_size, value_size), F32), eye], axis=1)

    places = chunk_places(info_ref, micro, chunk, seq_count)
    dec = x_ref[:, width:]
    beta_all = jax.nn.sigmoid(dec)
    g_all = par_ref[0:1, :] * softplus(dec + par_ref[1:2, :])
    scale = key_size**-0.5

    queries, keys, values = [], [], []
    for head in span:
        rows = []
        for begin, size in head_columns(head, heads, key_size, value_size):
            cut = slice(begin, begin + size)
            extended = jnp.concatenate(
                [halo[:, cut].astype(F32), x_ref[:, cut].astype(BF16).astype(F32)], axis=0
            )
            summed = conv_rows(extended, taps_ref[0:KCONV, cut], places["lags"])
            rows.append(summed * jax.nn.sigmoid(summed))
        queries.append(unit_rows(rows[0]) * scale)
        keys.append(unit_rows(rows[1]))
        values.append(rows[2])
    halo[...] = x_ref[CHUNK - HALO :, :width].astype(BF16)

    betas = [beta_all[:, heads + head : heads + head + 1] for head in span]
    decays = [decay_parts(g_all[:, head : head + 1], places) for head in span]
    grams = [mm(keys[head], keys[head], NT) for head in span]
    systems = [
        jnp.where(places["strictly"], betas[head] * decays[head][0] * grams[head], 0.0)
        for head in span
    ]
    inverses = unit_lower_inverses(systems, places)
    attends = [mm(queries[head], keys[head], NT) * decays[head][0] for head in span]
    solved = [
        mm(
            inverses[head],
            jnp.concatenate(
                [betas[head] * values[head], betas[head] * decays[head][1] * keys[head]], axis=1
            ),
        )
        for head in span
    ]
    starts = [state[head] for head in span]
    written = [
        jnp.concatenate(
            [solved[head][:, :value_size], jnp.zeros((CHUNK, key_size), F32)], axis=1
        )
        - mm(solved[head][:, value_size:], starts[head])
        for head in span
    ]
    outs = [
        decays[head][1] * mm(queries[head], starts[head]) + mm(attends[head], written[head])
        for head in span
    ]
    for head in span:
        _, _, to_last, carry_last = decays[head]
        inv_ref[0, head] = inverses[head].astype(BF16)
        start_ref[0, head] = starts[head].astype(BF16)
        out_ref[:, head * value_size : (head + 1) * value_size] = outs[head][:, :value_size]
        cmap_ref[:, head * key_size : (head + 1) * key_size] = outs[head][:, value_size:].astype(
            BF16
        )
        state[head] = carry_last * starts[head] + mm(to_last * keys[head], written[head], TN)

    @pl.when(chunk == pl.num_programs(1) - 1)
    def _():
        final_ref[0] = state[...]


def mix_backward_kernel(
    info_ref,
    x_ref,
    before_ref,
    rim_ref,
    taps_ref,
    par_ref,
    grad_ref,
    inv_ref,
    start_ref,
    incoming_ref,
    leaving_ref,
    dx_ref,
    rim_grad_ref,
    tail_ref,
    dtaps_ref,
    dpar_ref,
    carry,
    dstate,
    *,
    heads,
    key_size,
    value_size,
    seq_count,
):
    micro, step = pl.program_id(0), pl.program_id(1)
    chunk = pl.num_programs(1) - 1 - step
    span = range(heads)
    width = carry.shape[1]

    @pl.when(step == 0)
    def _():
        carry[...] = jnp.zeros_like(carry)
        dstate[...] = leaving_ref[0].astype(F32)

    @pl.when(jnp.logical_and(micro == 0, step == 0))
    def _():
        dtaps_ref[...] = jnp.zeros_like(dtaps_ref)
        dpar_ref[...] = jnp.zeros_like(dpar_ref)

    places = chunk_places(info_ref, micro, chunk, seq_count)
    row_ids, col_ids = places["row_ids"], places["col_ids"]
    lags = places["lags"]
    dec = x_ref[:, width:]
    beta_all = jax.nn.sigmoid(dec)
    shifted_dec = dec + par_ref[1:2, :]
    g_all = par_ref[0:1, :] * softplus(shifted_dec)
    scale = key_size**-0.5
    opening = jnp.where(chunk == 0, rim_ref[:, :width], before_ref[:, :width])
    opening = opening.astype(BF16).astype(F32)

    def extended_rows(cut):
        return jnp.concatenate(
            [opening[:, cut], x_ref[:, cut].astype(BF16).astype(F32)], axis=0
        )

    sums, norms, unit = [], [], []
    for head in span:
        mine = [
            conv_rows(
                extended_rows(slice(begin, begin + size)),
                taps_ref[0:KCONV, begin : begin + size],
                lags,
            )
            for begin, size in head_columns(head, heads, key_size, value_size)
        ]
        active = [value * jax.nn.sigmoid(value) for value in mine]
        inverse_norms = [
            lax.rsqrt(jnp.sum(value * value, axis=1, keepdims=True) + EPSILON)
            for value in active[:2]
        ]
        sums.append(mine)
        norms.append(inverse_norms)
        unit.append([active[0] * inverse_norms[0], active[1] * inverse_norms[1], active[2]])
    keys = [unit[head][1] for head in span]
    key_low = [keys[head].astype(BF16) for head in span]
    query_low = [(unit[head][0] * scale).astype(BF16) for head in span]
    betas = [beta_all[:, heads + head : heads + head + 1] for head in span]
    decays = [decay_parts(g_all[:, head : head + 1], places) for head in span]
    grams = [mm(key_low[head], key_low[head], NT) for head in span]
    products = [mm(query_low[head], key_low[head], NT) for head in span]
    attends = [(products[head] * decays[head][0]).astype(BF16) for head in span]
    starts = []
    for head in span:
        saved = start_ref[0, head]
        starts.append(
            saved[:, :value_size].astype(F32)
            + mm(saved[:, value_size:], incoming_ref[0, head])
        )
    start_low = [starts[head].astype(BF16) for head in span]
    key_state = [mm(key_low[head], start_low[head]) for head in span]
    query_state = [mm(query_low[head], start_low[head]) for head in span]
    grads = [grad_ref[:, head * value_size : (head + 1) * value_size] for head in span]
    grad_low = [grads[head].astype(BF16) for head in span]
    residues = [unit[head][2] - decays[head][1] * key_state[head] for head in span]
    inverses = [inv_ref[0, head] for head in span]
    written = [mm(inverses[head], betas[head] * residues[head]).astype(BF16) for head in span]
    ahead = [dstate[head] for head in span]
    ahead_low = [ahead[head].astype(BF16) for head in span]
    key_last = [(decays[head][2] * keys[head]).astype(BF16) for head in span]
    dwritten = [
        mm(attends[head], grad_low[head], TN) + mm(key_last[head], ahead_low[head])
        for head in span
    ]
    dresidue = [mm(inverses[head], dwritten[head], TN) for head in span]
    dresidue_low = [dresidue[head].astype(BF16) for head in span]
    dattend = [
        jnp.where(places["inclusive"], mm(grad_low[head], written[head], NT), 0.0)
        for head in span
    ]
    dsystem = [
        jnp.where(places["strictly"], -mm(dresidue_low[head], written[head], NT), 0.0)
        for head in span
    ]
    dproducts = [(dattend[head] * decays[head][0]).astype(BF16) for head in span]
    dcarried = [decays[head][1] * grads[head] for head in span]
    dcarried_low = [dcarried[head].astype(BF16) for head in span]
    dkey_state = [-(betas[head] * decays[head][1]) * dresidue[head] for head in span]
    dkey_state_low = [dkey_state[head].astype(BF16) for head in span]
    dkey_last = [mm(written[head], ahead_low[head], NT) for head in span]
    dgram = [dsystem[head] * betas[head] * decays[head][0] for head in span]
    dgram_low = [dgram[head].astype(BF16) for head in span]
    dquery = [
        mm(dcarried_low[head], start_low[head], NT) + mm(dproducts[head], key_low[head])
        for head in span
    ]
    dkey = [
        mm(dproducts[head], query_low[head], TN)
        + decays[head][2] * dkey_last[head]
        + mm(dkey_state_low[head], start_low[head], NT)
        + mm(dgram_low[head], key_low[head])
        + mm(dgram_low[head], key_low[head], TN)
        for head in span
    ]
    lane_ids = lax.broadcasted_iota(jnp.int32, (CHUNK, LANES), 1)
    ddec = jnp.zeros((CHUNK, LANES), F32)
    dg_all = jnp.zeros((CHUNK, LANES), F32)
    for head in span:
        pair, carried, to_last, carry_last = decays[head]
        coupled = dsystem[head] * grams[head]
        dpair = (dattend[head] * products[head] + coupled * betas[head]) * pair
        dbeta = jnp.sum(coupled * pair, axis=1, keepdims=True) + jnp.sum(
            dresidue[head] * residues[head], axis=1, keepdims=True
        )
        dcarry = jnp.sum(
            grads[head] * query_state[head] - betas[head] * dresidue[head] * key_state[head],
            axis=1,
            keepdims=True,
        )
        dcarry_last = jnp.sum(
            jnp.sum(ahead[head] * starts[head], axis=1, keepdims=True), axis=0, keepdims=True
        )
        dto_last = jnp.sum(dkey_last[head] * keys[head], axis=1, keepdims=True) * to_last
        is_last = lax.broadcasted_iota(jnp.int32, (CHUNK, 1), 0) == CHUNK - 1
        dcum_col = (
            jnp.sum(dpair, axis=1, keepdims=True)
            + dcarry * carried
            - dto_last
            + jnp.where(
                is_last,
                dcarry_last * carry_last + jnp.sum(dto_last, axis=0, keepdims=True),
                0.0,
            )
        )
        dcum_row = jnp.sum(
            jnp.where(row_ids == col_ids, dcum_col, 0.0) - dpair, axis=0, keepdims=True
        )
        dg = jnp.sum(jnp.where(col_ids >= row_ids, dcum_row, 0.0), axis=1, keepdims=True)
        beta = betas[head]
        dg_all = jnp.where(lane_ids == head, dg, dg_all)
        ddec = jnp.where(lane_ids == heads + head, dbeta * beta * (1.0 - beta), ddec)
        dstate[head] = (
            carry_last * ahead[head]
            + mm(query_low[head], dcarried_low[head], TN)
            + mm(key_low[head], dkey_state_low[head], TN)
        )
    dstep = dg_all * par_ref[0:1, :] * jax.nn.sigmoid(shifted_dec)
    ddec = ddec + dstep
    dx_ref[:, width:] = ddec.astype(BF16)
    dpar_ref[0:1, :] += jnp.sum(dg_all * g_all, axis=0, keepdims=True)
    dpar_ref[1:2, :] += jnp.sum(dstep, axis=0, keepdims=True)

    for head in span:
        dunit = [dquery[head] * scale, dkey[head]]
        dactive = [
            norms[head][at]
            * (
                dunit[at]
                - unit[head][at] * jnp.sum(dunit[at] * unit[head][at], axis=1, keepdims=True)
            )
            for at in range(2)
        ]
        dactive.append(betas[head] * dresidue[head])
        for at, (begin, size) in enumerate(head_columns(head, heads, key_size, value_size)):
            cut = slice(begin, begin + size)
            sig = jax.nn.sigmoid(sums[head][at])
            dsum = dactive[at] * sig * (1.0 + sums[head][at] * (1.0 - sig))
            extended = extended_rows(cut)
            taps = taps_ref[0:KCONV, cut]
            zeros = jnp.zeros((8, size), F32)
            dtaps_ref[KCONV - 1 : KCONV, cut] += jnp.sum(
                dsum * extended[HALO:], axis=0, keepdims=True
            )
            total = jnp.concatenate([zeros, taps[KCONV - 1 :, :] * dsum], axis=0)
            for lag in range(1, KCONV):
                masked = dsum * lags[lag - 1]
                at_tap = KCONV - 1 - lag
                dtaps_ref[at_tap : at_tap + 1, cut] += jnp.sum(
                    masked * extended[HALO - lag : HALO - lag + CHUNK], axis=0, keepdims=True
                )
                padded = jnp.concatenate(
                    [zeros, taps[at_tap : at_tap + 1, :] * masked, zeros], axis=0
                )
                total = total + padded[lag : lag + 8 + CHUNK]
            body_rows = jnp.concatenate(
                [total[8:CHUNK], total[CHUNK:] + carry[:, cut]], axis=0
            )
            dx_ref[:, cut] = body_rows.astype(BF16)
            carry[:, cut] = total[:8]

            @pl.when(step == 0)
            def _():
                tail_ref[0, :, cut] = body_rows[CHUNK - HALO :]

    @pl.when(chunk == 0)
    def _():
        rim_grad_ref[0] = carry[...]


def gate_forward_kernel(
    info_ref, plain_ref, cmap_ref, incoming_ref, gate_ref, gain_ref, mixed_ref, gated_ref, *, heads, key_size, value_size
):
    for head in range(heads):
        cut = slice(head * value_size, (head + 1) * value_size)
        mixed = plain_ref[:, cut] + mm(
            cmap_ref[:, head * key_size : (head + 1) * key_size], incoming_ref[0, head]
        )
        mixed_ref[:, cut] = mixed
        normed = mixed * lax.rsqrt(
            jnp.mean(mixed * mixed, axis=1, keepdims=True) + HEAD_FLOOR
        )
        gate = gate_ref[:, cut]
        gated_ref[:, cut] = (normed * gain_ref[0:1, :] * gate * jax.nn.sigmoid(gate)).astype(BF16)


def gate_backward_kernel(
    info_ref,
    grad_ref,
    mixed_ref,
    cmap_ref,
    gate_ref,
    gain_ref,
    dgate_ref,
    dmixed_ref,
    dlocal_ref,
    dgain_ref,
    *,
    heads,
    key_size,
    value_size,
):
    micro, step = pl.program_id(0), pl.program_id(1)

    @pl.when(step == 0)
    def _():
        dlocal_ref[...] = jnp.zeros_like(dlocal_ref)

    @pl.when(jnp.logical_and(micro == 0, step == 0))
    def _():
        dgain_ref[...] = jnp.zeros_like(dgain_ref)

    gain = gain_ref[0:1, :]
    for head in range(heads):
        cut = slice(head * value_size, (head + 1) * value_size)
        mixed = mixed_ref[:, cut]
        scale = lax.rsqrt(jnp.mean(mixed * mixed, axis=1, keepdims=True) + HEAD_FLOOR)
        normed = mixed * scale
        gate = gate_ref[:, cut]
        sig = jax.nn.sigmoid(gate)
        active = gate * sig
        grad = grad_ref[:, cut]
        by_norm = grad * normed
        dgain_ref[0:1, :] += jnp.sum(by_norm * active, axis=0, keepdims=True)
        dgate_ref[:, cut] = (by_norm * gain * sig * (1.0 + gate * (1.0 - sig))).astype(BF16)
        dnormed = grad * gain * active
        dmixed = scale * (dnormed - normed * jnp.mean(dnormed * normed, axis=1, keepdims=True))
        dmixed_ref[:, cut] = dmixed
        dlocal_ref[0, head] += mm(
            cmap_ref[:, head * key_size : (head + 1) * key_size], dmixed, TN
        )


VMEM_BYTES = 48 * 1024 * 1024
PIECES = 4


def kernel_call(
    kernel, info, arrays, grid, in_specs, out_specs, out_shape, scratch, name, after=(), **sizes
):
    count = 1 + len(arrays)

    def body(*refs):
        kernel(*refs[:count], *refs[count + len(after) :], **sizes)

    return pl.pallas_call(
        body,
        grid_spec=pltpu.PrefetchScalarGridSpec(
            num_scalar_prefetch=1,
            grid=grid,
            in_specs=list(in_specs) + [pl.BlockSpec(memory_space=pl.ANY)] * len(after),
            out_specs=out_specs,
            scratch_shapes=scratch,
        ),
        out_shape=out_shape,
        compiler_params=pltpu.CompilerParams(
            dimension_semantics=("arbitrary",) * len(grid), vmem_limit_bytes=VMEM_BYTES
        ),
        name=name,
    )(info, *arrays, *after)


def tie(value, *earlier):
    if not earlier:
        return value
    return pl.pallas_call(
        lambda *refs: None,
        out_shape=jax.ShapeDtypeStruct(value.shape, value.dtype),
        in_specs=[pl.BlockSpec(memory_space=pl.ANY)] * (1 + len(earlier)),
        out_specs=pl.BlockSpec(memory_space=pl.ANY),
        input_output_aliases={0: 0},
        name="tie",
    )(value, *earlier)


ANYWHERE = pl.BlockSpec(memory_space=pl.ANY)


def assemble(plan, arrays, after=()):
    count = len(arrays)
    steps = [(out, *part) for out, (_, parts) in enumerate(plan) for part in parts]

    def kernel(*refs):
        targets = refs[count + len(after) :][: len(plan)]
        held = refs[count + len(after) + len(plan) : -2]
        into, back = refs[-2:]

        def place(buffers, out, rows, columns, row, column):
            return buffers[out].at[
                row : row + rows[1] - rows[0], column : column + columns[1] - columns[0]
            ]

        loads, stores = [], []
        for at, (out, which, rows, columns, row, column) in enumerate(steps):
            source = refs[which].at[rows[0] : rows[1], columns[0] : columns[1]]
            target = place(held, out, rows, columns, row, column)
            loads.append(pltpu.make_async_copy(source, target, into.at[at]))
            loads[-1].start()
        for at, (out, _, rows, columns, row, column) in enumerate(steps):
            loads[at].wait()
            source = place(held, out, rows, columns, row, column)
            target = place(targets, out, rows, columns, row, column)
            stores.append(pltpu.make_async_copy(source, target, back.at[at]))
            stores[-1].start()
        for store in stores:
            store.wait()

    return pl.pallas_call(
        kernel,
        out_shape=[jax.ShapeDtypeStruct(shape, arrays[0].dtype) for shape, _ in plan],
        in_specs=[ANYWHERE] * (count + len(after)),
        out_specs=[ANYWHERE] * len(plan),
        scratch_shapes=[pltpu.VMEM(shape, arrays[0].dtype) for shape, _ in plan]
        + [pltpu.SemaphoreType.DMA((len(steps),))] * 2,
        compiler_params=pltpu.CompilerParams(vmem_limit_bytes=VMEM_BYTES),
        name="assemble",
    )(*arrays, *after)


def stacked(arrays, after=()):
    rows, parts = 0, []
    for at, array in enumerate(arrays):
        parts.append((at, (0, array.shape[0]), (0, array.shape[1]), rows, 0))
        rows += array.shape[0]
    return assemble([((rows, arrays[0].shape[1]), parts)], arrays, after)[0]


def ring_add(ups, downs, left, right, partly, after=()):
    count = len(ups)
    total = sum(grad.shape[1] for grad, _ in ups)
    tile = left.shape[0] if partly else left.shape[0] // 2

    def kernel(*refs):
        mine_up, mine_down = refs[:count], refs[count : 2 * count]
        came_up, came_down = refs[2 * count : 2 * count + 2]
        out_up, out_down = refs[-2:]
        step = pl.program_id(0)
        column = 0
        for up, down in zip(mine_up, mine_down):
            cut = slice(column, column + up.shape[1])
            column += up.shape[1]
            for mine, came, out, when in ((up, came_up, out_up, 0), (down, came_down, out_down, 1)):

                def add(mine=mine, came=came, out=out, cut=cut):
                    out[:, cut] = (mine[...].astype(F32) + came[:, cut].astype(F32)).astype(BF16)

                def keep(mine=mine, out=out, cut=cut):
                    out[:, cut] = mine[...]

                if partly:
                    pl.when(step == when)(add)
                    pl.when(step != when)(keep)
                else:
                    add()

    def of_block(grad, at):
        return pl.BlockSpec((tile, grad.shape[1]), lambda i: (2 * at + i, 0))

    came = pl.BlockSpec((tile, total), lambda i: (0 if partly else i, 0))
    out = pl.BlockSpec((tile, total), lambda i: (i, 0))
    shape = jax.ShapeDtypeStruct((2 * tile, total), BF16)
    return pl.pallas_call(
        kernel,
        grid=(2,),
        out_shape=[shape, shape],
        in_specs=[of_block(*block) for block in ups]
        + [of_block(*block) for block in downs]
        + [came, came]
        + [ANYWHERE] * len(after),
        out_specs=[out, out],
        compiler_params=pltpu.CompilerParams(
            dimension_semantics=("arbitrary",), vmem_limit_bytes=VMEM_BYTES
        ),
        name="ring_add",
    )(*[grad for grad, _ in ups], *[grad for grad, _ in downs], left, right, *after)


def row_blocks(left, right, blocks, count, after=()):
    size = left.shape[1] // count

    def kernel(left_ref, right_ref, *refs):
        refs[-1][...] = lax.dot_general(
            left_ref[...], right_ref[...], TN, preferred_element_type=F32
        ).astype(BF16)

    def block(i):
        found = blocks[0]
        for at, wanted in enumerate(blocks[1:], 1):
            found = jnp.where(i >= at, wanted, found)
        return 0, found

    return pl.pallas_call(
        kernel,
        grid=(len(blocks),),
        in_specs=[
            pl.BlockSpec((left.shape[0], size), block),
            pl.BlockSpec(right.shape, lambda i: (0, 0)),
        ]
        + [ANYWHERE] * len(after),
        out_specs=pl.BlockSpec((size, right.shape[1]), lambda i: (i, 0)),
        out_shape=jax.ShapeDtypeStruct((len(blocks) * size, right.shape[1]), BF16),
        compiler_params=pltpu.CompilerParams(
            dimension_semantics=("arbitrary",), vmem_limit_bytes=VMEM_BYTES
        ),
        name="row_blocks",
    )(left, right, *after)


def matmul(pairs, dims, dtype, after=(), pieces=0):
    if dims == NT:
        rows, columns = pairs[0][0].shape[0], pairs[0][1].shape[0]
        tile = 512 if columns % 512 == 0 else columns
        grid, pick = columns // tile, lambda i: (0, i)
        specs = [
            (pl.BlockSpec(left.shape, lambda i: (0, 0)),
             pl.BlockSpec((tile, right.shape[1]), lambda i: (i, 0)))
            for left, right in pairs
        ]
        shape = (rows, tile)
    else:
        over = 1 if dims == TN else 0
        rows, columns = pairs[0][0].shape[over], pairs[0][1].shape[1]
        tile = 256
        grid, pick = rows // tile, lambda i: (i, 0)
        specs = [
            (pl.BlockSpec((left.shape[0], tile), lambda i: (0, i)) if dims == TN
             else pl.BlockSpec((tile, left.shape[1]), lambda i: (i, 0)),
             pl.BlockSpec(right.shape, lambda i: (0, 0)))
            for left, right in pairs
        ]
        shape = (tile, columns)
    count = 2 * len(pairs)
    half = rows // 2

    def kernel(*refs):
        total = None
        for at in range(0, count, 2):
            product = lax.dot_general(
                refs[at][...], refs[at + 1][...], dims, preferred_element_type=F32
            )
            total = product if total is None else total + product
        outs = refs[count + len(after) :]
        if pieces:
            outs[0][...] = total[:half].astype(dtype)
            for at in range(pieces):
                first = half + at * (half // pieces)
                outs[1 + at][...] = total[first : first + half // pieces].astype(dtype)
        else:
            outs[0][...] = total.astype(dtype)

    if pieces:
        heights = [half] + [half // pieces] * pieces
        out_specs = [pl.BlockSpec((height, tile), pick) for height in heights]
        out_shape = [jax.ShapeDtypeStruct((height, columns), dtype) for height in heights]
    else:
        out_specs = [pl.BlockSpec(shape, pick)]
        out_shape = [jax.ShapeDtypeStruct((rows, columns), dtype)]
    found = pl.pallas_call(
        kernel,
        grid=(grid,),
        in_specs=[spec for both in specs for spec in both] + [ANYWHERE] * len(after),
        out_specs=out_specs,
        out_shape=out_shape,
        compiler_params=pltpu.CompilerParams(
            dimension_semantics=("arbitrary",), vmem_limit_bytes=VMEM_BYTES
        ),
        name="matmul",
    )(*[array for both in pairs for array in both], *after)
    return found if pieces else found[0]


def weighted(body, parts, cuts, operands, specs, out_specs, out_shape, steps, name, after=()):
    count, given, kept = len(parts), len(operands), len(cuts)
    rows, columns = sum(part.shape[0] for part in parts), parts[0].shape[1]

    def kernel(*refs):
        sources, mine = refs[:count], refs[count : count + given]
        rest = refs[count + given + len(after) :]
        held, into, back = rest[-3:]
        stores = [
            pltpu.make_async_copy(held.at[:, low:high], rest[at], back.at[at])
            for at, (low, high) in enumerate(cuts)
        ]

        @pl.when(pl.program_id(0) == 0)
        def _():
            loads, row = [], 0
            for at, source in enumerate(sources):
                target = held.at[row : row + source.shape[0]]
                loads.append(pltpu.make_async_copy(source, target, into.at[at]))
                loads[-1].start()
                row += source.shape[0]
            for load in loads:
                load.wait()
            for store in stores:
                store.start()

        body(held, mine, rest[kept:-3])

        @pl.when(pl.program_id(0) == steps - 1)
        def _():
            for store in stores:
                store.wait()

    dtype = parts[0].dtype
    weights = [jax.ShapeDtypeStruct((rows, high - low), dtype) for low, high in cuts]
    found = pl.pallas_call(
        kernel,
        grid=(steps,),
        in_specs=[ANYWHERE] * count + specs + [ANYWHERE] * len(after),
        out_specs=[ANYWHERE] * kept + out_specs,
        out_shape=weights + out_shape,
        scratch_shapes=[
            pltpu.VMEM((rows, columns), dtype),
            pltpu.SemaphoreType.DMA((count,)),
            pltpu.SemaphoreType.DMA((kept,)),
        ],
        compiler_params=pltpu.CompilerParams(
            dimension_semantics=("arbitrary",), vmem_limit_bytes=VMEM_BYTES
        ),
        name=name,
    )(*parts, *operands, *after)
    return found[:kept], found[kept:]


ROW_TILE = 256


def tiles_of(columns):
    return pl.BlockSpec((ROW_TILE, columns), lambda i: (i, 0))


def project(rows, rim, parts, after=()):
    columns = parts[0].shape[1]

    def body(held, given, outs):
        rows_ref, rim_ref = given
        outs[0][...] = jnp.dot(rows_ref[...], held[...], preferred_element_type=F32)

        @pl.when(pl.program_id(0) == 0)
        def _():
            outs[1][...] = jnp.dot(rim_ref[...], held[...], preferred_element_type=F32)

    (weights,), (projected, rim_projected) = weighted(
        body,
        parts,
        [(0, columns)],
        (rows, rim),
        [tiles_of(rows.shape[1]), pl.BlockSpec(rim.shape, lambda i: (0, 0))],
        [tiles_of(columns), pl.BlockSpec((rim.shape[0], columns), lambda i: (0, 0))],
        [
            jax.ShapeDtypeStruct((rows.shape[0], columns), F32),
            jax.ShapeDtypeStruct((rim.shape[0], columns), F32),
        ],
        rows.shape[0] // ROW_TILE,
        "project",
        after,
    )
    return projected, rim_projected, weights


def gate_project(rows, parts, width, after=()):
    def body(held, given, outs):
        outs[0][...] = jnp.dot(given[0][...], held[:, :width], preferred_element_type=F32)

    (first, second), (found,) = weighted(
        body,
        parts,
        [(0, width), (width, parts[0].shape[1])],
        (rows,),
        [tiles_of(rows.shape[1])],
        [tiles_of(width)],
        [jax.ShapeDtypeStruct((rows.shape[0], width), F32)],
        rows.shape[0] // ROW_TILE,
        "gate_project",
        after,
    )
    return found, first, second


def feed_forward(rows, cotangent, parts, after=()):
    width = parts[0].shape[1] // 3

    def body(held, given, outs):
        rows_ref, cotangent_ref = given
        hidden_ref, grad_ref = outs
        gate = jnp.dot(rows_ref[...], held[:, :width], preferred_element_type=F32)
        up = jnp.dot(rows_ref[...], held[:, width : 2 * width], preferred_element_type=F32)
        grad = jnp.dot(cotangent_ref[...], held[:, 2 * width :], preferred_element_type=F32)
        sig = jax.nn.sigmoid(gate)
        active = gate * sig
        hidden_ref[...] = (active * up).astype(BF16)
        grad_ref[:, :width] = (grad * up * sig * (1.0 + gate * (1.0 - sig))).astype(BF16)
        grad_ref[:, width:] = (grad * active).astype(BF16)

    model = rows.shape[1]
    (w_ffn, w_down), (hidden, grad) = weighted(
        body,
        parts,
        [(0, 2 * width), (2 * width, 3 * width)],
        (rows, cotangent),
        [tiles_of(model), tiles_of(model)],
        [tiles_of(width), tiles_of(2 * width)],
        [
            jax.ShapeDtypeStruct((rows.shape[0], width), BF16),
            jax.ShapeDtypeStruct((rows.shape[0], 2 * width), BF16),
        ],
        rows.shape[0] // ROW_TILE,
        "feed_forward",
        after,
    )
    return hidden, grad, w_ffn, w_down


class Mix:
    def __init__(self, info, micros, chunks, heads, key_size, value_size):
        self.info, self.micros, self.chunks = info, micros, chunks
        self.heads, self.key_size, self.value_size = heads, key_size, value_size
        self.width = heads * (2 * key_size + value_size)
        self.wide = key_size + value_size
        self.rows = micros * chunks * CHUNK
        self.sizes = dict(heads=heads, key_size=key_size, value_size=value_size)

    def block(self, m, c, info):
        return rank_block(c, info[0, info.shape[1] - 1]) * self.micros + m

    def by_rows(self, columns, turned=False):
        def place(m, c, info):
            return self.block(m, self.chunks - 1 - c if turned else c, info), 0

        return pl.BlockSpec((CHUNK, columns), place)

    def by_chunk(self, rows, columns, turned=False):
        def place(m, c, info):
            return m * self.chunks + (self.chunks - 1 - c if turned else c), 0, 0, 0

        return pl.BlockSpec((1, self.heads, rows, columns), place)

    def by_micro(self, *dims):
        return pl.BlockSpec((1,) + dims, lambda m, c, info: (m,) + (0,) * len(dims))

    def whole(self, *dims):
        return pl.BlockSpec(dims, lambda m, c, info: (0,) * len(dims))

    def like(self, dtype, *dims):
        return jax.ShapeDtypeStruct(dims, dtype)

    def call(self, kernel, arrays, in_specs, outs, scratch, name, after, **more):
        return kernel_call(
            kernel,
            self.info,
            arrays,
            (self.micros, self.chunks),
            in_specs,
            [spec for spec, _ in outs],
            [shape for _, shape in outs],
            scratch,
            name,
            after,
            **self.sizes,
            **more,
        )

    def forward(self, projected, rim, taps, par, after=()):
        h, dk, dv, wide, width = self.heads, self.key_size, self.value_size, self.wide, self.width
        steps = self.micros * self.chunks
        return self.call(
            mix_forward_kernel,
            (projected, rim, taps, par),
            [
                self.by_rows(width + LANES),
                pl.BlockSpec((HALO, width + LANES), lambda m, c, info: (m, 0)),
                self.whole(8, width),
                self.whole(8, LANES),
            ],
            [
                (self.by_rows(h * dv), self.like(F32, self.rows, h * dv)),
                (self.by_rows(h * dk), self.like(BF16, self.rows, h * dk)),
                (self.by_chunk(CHUNK, CHUNK), self.like(BF16, steps, h, CHUNK, CHUNK)),
                (self.by_chunk(dk, wide), self.like(BF16, steps, h, dk, wide)),
                (self.by_micro(h, dk, wide), self.like(F32, self.micros, h, dk, wide)),
            ],
            [pltpu.VMEM((HALO, width), BF16), pltpu.VMEM((h, dk, wide), F32)],
            "mix_forward",
            after,
            seq_count=self.info.shape[1] - 2,
        )

    def backward(
        self, projected, rim, taps, par, grad, inverses, starts, incoming, leaving, after=()
    ):
        h, dk, dv, wide, width = self.heads, self.key_size, self.value_size, self.wide, self.width
        halo_blocks = CHUNK // HALO

        def before(m, c, info):
            earlier = jnp.maximum(self.chunks - 2 - c, 0)
            return (self.block(m, earlier, info) + 1) * halo_blocks - 1, 0

        return self.call(
            mix_backward_kernel,
            (projected, projected, rim, taps, par, grad, inverses, starts, incoming, leaving),
            [
                self.by_rows(width + LANES, True),
                pl.BlockSpec((HALO, width + LANES), before),
                pl.BlockSpec((HALO, width + LANES), lambda m, c, info: (m, 0)),
                self.whole(8, width),
                self.whole(8, LANES),
                self.by_rows(h * dv, True),
                self.by_chunk(CHUNK, CHUNK, True),
                self.by_chunk(dk, wide, True),
                self.by_micro(h, dk, dv),
                self.by_micro(h, dk, dv),
            ],
            [
                (self.by_rows(width + LANES, True), self.like(BF16, self.rows, width + LANES)),
                (self.by_micro(8, width), self.like(F32, self.micros, 8, width)),
                (self.by_micro(HALO, width), self.like(F32, self.micros, HALO, width)),
                (self.whole(8, width), self.like(F32, 8, width)),
                (self.whole(8, LANES), self.like(F32, 8, LANES)),
            ],
            [pltpu.VMEM((8, width), F32), pltpu.VMEM((h, dk, dv), F32)],
            "mix_backward",
            after,
            seq_count=self.info.shape[1] - 2,
        )

    def gate_forward(self, plain, cmap, incoming, gate, gain, after=()):
        h, dk, dv = self.heads, self.key_size, self.value_size
        return self.call(
            gate_forward_kernel,
            (plain, cmap, incoming, gate, gain),
            [
                self.by_rows(h * dv),
                self.by_rows(h * dk),
                self.by_micro(h, dk, dv),
                self.by_rows(h * dv),
                self.whole(8, dv),
            ],
            [
                (self.by_rows(h * dv), self.like(F32, self.rows, h * dv)),
                (self.by_rows(h * dv), self.like(BF16, self.rows, h * dv)),
            ],
            [],
            "gate_forward",
            after,
        )

    def gate_backward(self, grad, mixed, cmap, gate, gain, after=()):
        h, dk, dv = self.heads, self.key_size, self.value_size
        return self.call(
            gate_backward_kernel,
            (grad, mixed, cmap, gate, gain),
            [
                self.by_rows(h * dv),
                self.by_rows(h * dv),
                self.by_rows(h * dk),
                self.by_rows(h * dv),
                self.whole(8, dv),
            ],
            [
                (self.by_rows(h * dv), self.like(BF16, self.rows, h * dv)),
                (self.by_rows(h * dv), self.like(F32, self.rows, h * dv)),
                (self.by_micro(h, dk, dv), self.like(F32, self.micros, h, dk, dv)),
                (self.whole(8, dv), self.like(F32, 8, dv)),
            ],
            [],
            "gate_backward",
            after,
        )


def from_behind(value, axis, steps):
    count = lax.axis_size(axis)
    leading, last = (max(0, -steps), min(count, count - steps))
    return lax.ppermute(value, axis, [(source, source + steps) for source in range(leading, last)])


def swap(value, axis, bit):
    return lax.ppermute(value, axis, [(at, at ^ bit) for at in range(lax.axis_size(axis))])


def rank_block(rank, mine):
    apart = jnp.bitwise_xor(rank, mine)
    return 2 * jnp.bitwise_and(apart, 1) + jnp.right_shift(apart, 1)


def cut_rows(value, count):
    size = value.shape[0] // count
    return [value[at * size : (at + 1) * size] for at in range(count)]


class HeadGather:
    def __init__(self, value):
        self.value = value
        self.across = [swap(part, "head", 2) for part in cut_rows(value, PIECES // 2)]

    def pass_on(self, *after):
        self.pair = stacked([self.value, *self.across], after)
        self.near = [swap(part, "head", 1) for part in cut_rows(self.pair, PIECES)]
        return (self.pair,)

    def rows(self, *after):
        return stacked([self.pair, *self.near], after)


class HeadScatter:
    def __init__(self, mine, *sent):
        self.pieces = max(len(sent), 2)
        self.mine, self.sent = cut_rows(mine, self.pieces), sent
        self.near = [swap(part, "head", 1) for part in sent]

    def pass_on(self, *after):
        half = self.pieces // 2
        self.near = [tie(part, *after) for part in self.near]
        if len(self.near) == 1:
            self.near = cut_rows(self.near[0], 2)
        theirs = [
            (mine.astype(F32) + near.astype(F32)).astype(BF16)
            for mine, near in zip(self.mine[half:], self.near[half:])
        ]
        self.across = [swap(part, "head", 2) for part in theirs]
        return tuple(theirs)

    def total(self, *after):
        parts = zip(self.mine, self.near, self.across)
        return jnp.concatenate(
            [
                mine.astype(F32) + near.astype(F32) + tie(across, *after).astype(F32)
                for mine, near, across in parts
            ],
            axis=0,
        )


class Summed:
    def __init__(self, value, hops):
        self.value, self.hops, self.came = value, list(hops), []

    def step(self, *after):
        if not self.came and after:
            self.value = tie(self.value, *after)
        for came in self.came:
            self.value = self.value + tie(came, *after)
        self.came = []
        if self.hops:
            axis, turns = self.hops.pop(0)
            self.came = [swap(self.value, axis, turn) for turn in turns]
        return (self.value,)

    def total(self):
        while self.came:
            self.step()
        return self.value


def head_hops():
    return [("head", [1 << at]) for at in range((lax.axis_size("head") - 1).bit_length())]


def dp_hops():
    count = lax.axis_size("dp")
    if count <= 8:
        return [("dp", [1]), ("dp", list(range(2, count, 2)))]
    return [("dp", [1 << at]) for at in range((count - 1).bit_length())]


def ring_order():
    count = lax.axis_size("dp")
    return list(range(0, count, 2)) + list(range(count - 1, 0, -2))


def ring_place():
    count, mine = lax.axis_size("dp"), lax.axis_index("dp")
    return jnp.where(mine % 2 == 0, mine // 2, count - 1 - mine // 2)


def ring_steps():
    ring = ring_order()
    ahead = [(ring[at], ring[(at + 1) % len(ring)]) for at in range(len(ring))]
    return ahead, [(after, before) for before, after in ahead]


def reorder_kernel(order_ref, *refs, size, outward):
    count = len(refs) // 2
    for source, target in zip(refs[:count], refs[count:]):
        for at in range(order_ref.shape[0]):
            moved = pl.ds(pl.multiple_of(order_ref[at] * size, size), size)
            here = slice(at * size, (at + 1) * size)
            if outward:
                target[:, moved] = source[:, here]
            else:
                target[:, here] = source[:, moved]


def reorder(arrays, outward, after=()):
    ring = ring_order()
    count, place = len(ring), ring_place()
    size = arrays[0].shape[1] // count
    around = jnp.asarray(ring + ring, jnp.int32)
    order = lax.dynamic_slice(around, (place,), (count,))
    if size % LANES == 0:
        return kernel_call(
            reorder_kernel,
            order,
            arrays,
            (1,),
            [pl.BlockSpec(a.shape, lambda i, info: (0, 0)) for a in arrays],
            [pl.BlockSpec(a.shape, lambda i, info: (0, 0)) for a in arrays],
            [jax.ShapeDtypeStruct(a.shape, a.dtype) for a in arrays],
            [],
            "reorder",
            after,
            size=size,
            outward=outward,
        )
    if outward:
        ranks = jnp.arange(count, dtype=jnp.int32)
        order = jnp.sum(jnp.where(order[None, :] == ranks[:, None], ranks[None, :], 0), axis=1)
    return [
        jnp.take(a.reshape(-1, count, size), order, axis=1).reshape(a.shape) for a in arrays
    ]


class Gather:
    def __init__(self, shard):
        self.ahead, self.back = ring_steps()
        self.left, self.right, self.far = [shard], [shard], None

    def step(self, *after):
        if len(self.left) > 1 or after:
            self.left[-1] = tie(self.left[-1], *after)
            self.right[-1] = self.left[0] if len(self.left) == 1 else tie(self.right[-1], *after)
        sent = self.left[-1], self.right[-1]
        if len(self.left) < len(self.ahead) // 2:
            self.left.append(lax.ppermute(self.left[-1], "dp", self.ahead))
            self.right.append(lax.ppermute(self.right[-1], "dp", self.back))
        else:
            half = self.left[0].shape[0] // 2
            self.far = [
                lax.ppermute(self.left[-1][:half], "dp", self.ahead),
                lax.ppermute(self.right[-1][half:], "dp", self.back),
            ]
        return sent

    def run(self, *after):
        while self.far is None:
            after = self.step(*after)
        return after

    def came(self):
        return self.left[-1], self.right[-1]

    def parts(self):
        return [self.left[0]] + self.right[1:] + self.far + self.left[:0:-1]


class Scatter:
    def __init__(self, *pairs, after=()):
        self.ahead, self.back = ring_steps()
        self.pairs, self.count = pairs, len(self.ahead)
        self.size = pairs[0][0].shape[1] // self.count
        self.apart = self.size % LANES == 0
        self.at = middle = self.count // 2
        self.left = self.right = None
        self.blocks = [{} for _ in pairs]
        self.groups = [[middle]]
        if self.count > 4:
            self.groups.append([middle - 1, middle + 1])
        self.groups.append([at for at in range(self.count) if all(at not in g for g in self.groups)])
        if self.apart:
            self.work(0, after=after)
        else:
            for which, pair in enumerate(pairs):
                whole = matmul([pair], TN, BF16, after)
                self.blocks[which] = {at: (whole, at) for at in range(self.count)}

    def work(self, group, only=None, after=()):
        found = []
        for which, pair in enumerate(self.pairs):
            if self.apart and only in (None, which):
                found.append(row_blocks(*pair, self.groups[group], self.count, after))
                for place, at in enumerate(self.groups[group]):
                    self.blocks[which][at] = (found[-1], place)
        return tuple(found) or tuple(after)

    def of(self, at):
        return [blocks[at] for blocks in self.blocks]

    def step(self, *after):
        middle, half = self.count // 2, self.size // 2
        if self.at == middle:
            plan, arrays = [], [grad for grad, _ in self.of(middle)]
            for start in (0, half):
                column, items = 0, []
                for at, (grad, place) in enumerate(self.of(middle)):
                    first, width = place * self.size + start, grad.shape[1]
                    items.append((at, (first, first + half), (0, width), 0, column))
                    column += width
                plan.append(((half, column), items))
            up, down = assemble(plan, arrays, after)
        else:
            up, down = ring_add(
                self.of(self.at),
                self.of(self.count - self.at),
                self.left,
                self.right,
                self.at == middle - 1,
                after,
            )
        self.left = lax.ppermute(up, "dp", self.ahead)
        self.right = lax.ppermute(down, "dp", self.back)
        self.at -= 1
        return up, down

    def came(self):
        return self.left, self.right

    def total(self, *after):
        while self.at > 0:
            after = self.step(*after)
        mine = [
            grad[place * self.size : (place + 1) * self.size] for grad, place in self.of(0)
        ]
        mine = mine[0] if len(mine) == 1 else jnp.concatenate(mine, axis=1)
        left, right = tie(self.left, *after), tie(self.right, *after)
        return mine.astype(F32) + left.astype(F32) + right.astype(F32)


def apply_map(moves, state, turned=False):
    return jnp.einsum(
        "hji,hjv->hiv" if turned else "hij,hjv->hiv",
        moves.astype(BF16),
        state.astype(BF16),
        preferred_element_type=F32,
    )


def own_and_swapped(value, bit):
    sent = jnp.where(bit == 0, value[1], value[0]).astype(BF16)
    theirs = swap(sent, "dp", 1).astype(F32)
    mine = jnp.where(bit == 0, value[0], value[1]).astype(F32)
    return jnp.where(bit == 0, mine, theirs), jnp.where(bit == 0, theirs, mine), sent


def hand_back(first, second, bit):
    mine = jnp.where(bit == 0, first, second).astype(BF16)
    sent = jnp.where(bit == 0, second, first).astype(BF16)
    theirs = swap(sent, "dp", 1)
    return jnp.stack([jnp.where(bit == 0, mine, theirs), jnp.where(bit == 0, theirs, mine)]), sent


class Scan:
    def __init__(self, final, value_size):
        self.bit, self.pairs = lax.axis_index("dp") % 2, lax.axis_size("dp") // 2
        self.cut = value_size
        self.sent = jnp.where(self.bit == 0, final[1], final[0]).astype(BF16)
        self.mine = jnp.where(self.bit == 0, final[0], final[1]).astype(F32)
        self.theirs = swap(self.sent, "dp", 1)

    def ordered(self, *after):
        theirs = tie(self.theirs, *after).astype(F32)
        return (
            jnp.where(self.bit == 0, self.mine, theirs),
            jnp.where(self.bit == 0, theirs, self.mine),
        )

    def shifted(self, value, steps):
        return [from_behind(value, "dp", 2 * sign) for sign in steps]

    def send(self, *after):
        self.first, self.second = self.ordered(*after)
        cut = self.cut
        self.first_map, self.second_map = self.first[..., cut:], self.second[..., cut:]
        pair_map = apply_map(self.second_map, self.first_map)
        self.pair_map = pair_map.astype(BF16)
        pair_sum = apply_map(self.second_map, self.first[..., :cut]) + self.second[..., :cut]
        both = jnp.concatenate([pair_sum, pair_map], axis=-1).astype(BF16)
        self.before = self.shifted(both, range(1, self.pairs))
        return (both,)

    def finish(self, *after):
        state = jnp.zeros(self.first[..., : self.cut].shape, F32)
        for both in self.before[::-1]:
            both = tie(both, *after)
            after = ()
            state = apply_map(both[..., self.cut :], state) + both[..., : self.cut].astype(F32)
        after_first = apply_map(self.first_map, state) + self.first[..., : self.cut]
        return self.hand_back(state, after_first)

    def hand_back(self, first, second):
        mine = jnp.where(self.bit == 0, first, second).astype(BF16)
        sent = jnp.where(self.bit == 0, second, first).astype(BF16)
        theirs = swap(sent, "dp", 1)
        states = [jnp.where(self.bit == 0, *pair) for pair in ((mine, theirs), (theirs, mine))]
        return jnp.stack(states), (sent,)


class ScanBack(Scan):
    def __init__(self, local, ahead):
        self.of = ahead
        super().__init__(local, local.shape[-1])

    def send(self, *after):
        self.first, self.second = self.ordered(*after)
        pair_sum = (apply_map(self.of.first_map, self.second, True) + self.first).astype(BF16)
        both = jnp.concatenate([pair_sum, self.of.pair_map], axis=-1)
        self.behind = self.shifted(both, [-step for step in range(1, self.pairs)])
        return (both,)

    def finish(self, *after):
        state = jnp.zeros(self.first.shape, F32)
        for both in self.behind[::-1]:
            both = tie(both, *after)
            after = ()
            moves = both[..., self.cut :]
            state = apply_map(moves, state, True) + both[..., : self.cut].astype(F32)
        before_second = apply_map(self.of.second_map, state, True) + self.second
        return self.hand_back(before_second, state)


def norm_backward(grad_in, normed_rows, scale):
    return scale * (grad_in - normed_rows * jnp.mean(grad_in * normed_rows, axis=-1, keepdims=True))


def body(
    tokens,
    out_grad,
    seq_lengths,
    attn_norm,
    query_proj,
    key_proj,
    value_proj,
    gate_proj,
    decay_proj,
    beta_proj,
    conv_query,
    conv_key,
    conv_value,
    log_rate,
    step_bias,
    head_norm,
    out_proj,
    ffn_norm,
    ffn_gate,
    ffn_up,
    ffn_down,
):
    head_rank, ranks = lax.axis_index("head"), lax.axis_size("head")
    heads = decay_proj.shape[1]
    qk_width = query_proj.shape[1]
    v_width = value_proj.shape[1]
    key_size = qk_width // heads
    value_size = v_width // heads
    ffn_width = ffn_gate.shape[1]
    conv_width = 2 * qk_width + v_width
    micros, part_rows, model = tokens.shape
    assert part_rows == CHUNK and micros == 2 and ranks == 4

    decay_pad = jnp.zeros((decay_proj.shape[0], LANES - 2 * heads), decay_proj.dtype)
    conv_ring = Gather(
        jnp.concatenate(
            [query_proj, key_proj, value_proj, decay_proj, beta_proj, decay_pad], axis=1
        )
    )
    gate_ring = Gather(jnp.concatenate([gate_proj, out_proj.T], axis=1))
    ffn_ring = Gather(jnp.concatenate([ffn_gate, ffn_up, ffn_down.T], axis=1))

    def of_mine(whole, width):
        return lax.dynamic_slice_in_dim(whole, head_rank * width, width, whole.ndim - 1)

    taps = jnp.concatenate(
        [of_mine(conv_query, qk_width), of_mine(conv_key, qk_width), of_mine(conv_value, v_width)],
        axis=1,
    )
    taps = jnp.pad(taps, ((0, 8 - KCONV), (0, 0)))
    par = jnp.pad(
        jnp.stack([-jnp.exp(of_mine(log_rate, heads)), of_mine(step_bias, heads)]),
        ((0, 6), (0, LANES - heads)),
    )
    gain = jnp.broadcast_to(head_norm, (8, value_size))

    def flat(value):
        return value.reshape(-1, value.shape[-1])

    def ranked(value):
        return value.reshape(ranks, micros, part_rows, value.shape[-1])

    conv_ring.step()
    turned, cotangent, attn_gain, ffn_gain = reorder(
        [
            flat(tokens),
            flat(out_grad),
            jnp.broadcast_to(attn_norm, (8, model)),
            jnp.broadcast_to(ffn_norm, (8, model)),
        ],
        False,
    )
    attn_gain, ffn_gain = attn_gain[0], ffn_gain[0]
    residual = turned.astype(F32)
    scale_one = lax.rsqrt(jnp.mean(residual * residual, axis=-1, keepdims=True) + EPSILON)
    normed_one = residual * scale_one
    normed_rows = HeadGather((normed_one * attn_gain).astype(BF16))
    conv_ring.step(gate_ring.left[0], ffn_ring.left[0])
    normed_rows.pass_on(*conv_ring.came())
    conv_ring.step()
    normed_all = normed_rows.rows(*conv_ring.came())
    last_chunk = rank_block(ranks - 1, head_rank)
    last_rows = lax.dynamic_slice(
        ranked(normed_all), (last_chunk, 0, part_rows - HALO, 0), (1, micros, HALO, model)
    )
    conv_ring.run()
    rim_rows = from_behind(reorder([flat(last_rows)], True)[0], "dp", 1)
    rim_rows = reorder([rim_rows], False)[0]
    first_row = lax.axis_index("dp") * ranks * part_rows
    ends = jnp.cumsum(seq_lengths, axis=1)
    info = jnp.concatenate(
        [
            ends - seq_lengths,
            jnp.full((micros, 1), first_row, jnp.int32),
            jnp.full((micros, 1), head_rank, jnp.int32),
        ],
        axis=1,
    ).astype(jnp.int32)
    mix = Mix(info, micros, ranks, heads, key_size, value_size)
    now = ffn_ring.step(rim_rows, *conv_ring.far)
    now = gate_ring.step(*now)
    projected, rim, w_conv = project(normed_all, rim_rows, conv_ring.parts(), now)

    plain, carried_map, inverses, starts, final = mix.forward(projected, rim, taps, par, now)
    scan = Scan(final, value_size)
    now = gate_ring.step(scan.sent)
    now = scan.send(*now, *ffn_ring.came())
    cotangent_rows = HeadGather(tie(cotangent, *now))
    now = gate_ring.step(*now, *scan.before)
    now = cotangent_rows.pass_on(*now)
    incoming, now = scan.finish(*now)
    cotangent_all = cotangent_rows.rows(*now)
    now = gate_ring.run(*now)
    now = ffn_ring.step(incoming, *gate_ring.far, cotangent_all)
    gate_lin, w_gate, w_out = gate_project(normed_all, gate_ring.parts(), v_width, now)
    mixed, gated = mix.gate_forward(plain, carried_map, incoming, gate_lin, gain)

    mix_sum = HeadScatter(*matmul([(gated, w_out)], NT, BF16, pieces=PIECES))
    now = ffn_ring.step(*mix_sum.sent)
    now = mix_sum.pass_on(*now)
    after_mix = residual + mix_sum.total(*now)
    scale_two = lax.rsqrt(jnp.mean(after_mix * after_mix, axis=-1, keepdims=True) + EPSILON)
    normed_two = after_mix * scale_two
    ffn_rows = HeadGather((normed_two * ffn_gain).astype(BF16))
    now = ffn_ring.run(ffn_rows.across[0])
    now = ffn_rows.pass_on(*now)
    ffn_all = ffn_rows.rows(*now)

    hidden, gate_up_grad, w_ffn, w_down = feed_forward(ffn_all, cotangent_all, ffn_ring.parts())
    ffn_in_sum = HeadScatter(*matmul([(gate_up_grad, w_ffn)], NT, BF16, pieces=PIECES))
    ffn_sums = Scatter(
        (ffn_all, gate_up_grad), (cotangent_all, hidden), after=ffn_in_sum.sent
    )
    now = ffn_sums.step()
    now = ffn_in_sum.pass_on(*now)
    now = ffn_sums.work(1, after=now)
    now = ffn_sums.step(*now)
    ffn_in_grad = ffn_in_sum.total(*now)
    grad_norm_two = jnp.sum(ffn_in_grad * normed_two, axis=0)
    after_mix_grad = cotangent.astype(F32) + norm_backward(
        ffn_in_grad * ffn_gain, normed_two, scale_two
    )
    branch_rows = HeadGather(after_mix_grad.astype(BF16))
    now = ffn_sums.work(2, after=(branch_rows.value,))
    now = branch_rows.pass_on(*now)
    branch_grad = branch_rows.rows(*now)
    now = (branch_grad,)

    gated_grad = matmul([(branch_grad, w_out)], NN, F32, now)
    gate_grad, mixed_grad, local_grad, grad_head_norm = mix.gate_backward(
        gated_grad, mixed, carried_map, gate_lin, gain, ffn_sums.came()
    )

    back = ScanBack(local_grad, scan)
    gate_sums = Scatter(
        (normed_all, gate_grad), (branch_grad, gated), after=(back.sent, *ffn_sums.came())
    )
    now = gate_sums.work(1, after=(back.sent,)) + gate_sums.work(2, 1, (back.sent,))
    now = back.send(*now)
    now = gate_sums.work(2, 0, now)
    now = gate_sums.step(*now, back.behind[-1])
    ffn_part = matmul([(hidden, w_down)], NT, BF16, now, pieces=PIECES)
    leaving, now = back.finish(ffn_part[0])
    now = ffn_sums.step(leaving, *gate_sums.came())
    now = gate_sums.step(*now)
    conv_grad, rim_grad, tail, taps_grad, par_grad = mix.backward(
        projected, rim, taps, par, mixed_grad, inverses, starts, incoming, leaving, now
    )
    back_rim = from_behind(rim_grad, "dp", -1)
    small = jnp.concatenate(
        [
            taps_grad[:KCONV].reshape(-1),
            jnp.pad(par_grad[0, :heads], (0, LANES - heads)),
            jnp.pad(par_grad[1, :heads], (0, LANES - heads)),
            grad_head_norm[0],
        ]
    ).reshape(-1, LANES)
    ffn_sum = HeadScatter(ffn_part[0], *[tie(part, rim_grad) for part in ffn_part[1:]])
    now = ffn_sums.step(back_rim, *gate_sums.came())
    now = ffn_sum.pass_on(*now)
    tail = tie(tail, back_rim)
    tail = jnp.concatenate([tail[:, :8], tail[:, 8:] + back_rim], axis=1).astype(BF16)
    conv_grad = lax.dynamic_update_slice(
        ranked(conv_grad), tail[None], (last_chunk, 0, part_rows - HALO, 0)
    ).reshape(-1, conv_width + LANES)

    conv_sums = Scatter((normed_all, conv_grad), after=now)
    now = conv_sums.step()
    now = conv_sums.work(1, after=now) + conv_sums.work(2, after=now)
    normed_part = matmul(
        [(conv_grad, w_conv), (gate_grad, w_gate)], NT, BF16, now, pieces=PIECES
    )
    normed_sum = HeadScatter(*normed_part)
    now = gate_sums.step(*normed_sum.sent, *ffn_sums.came(), *conv_sums.came())
    now = normed_sum.pass_on(*now)
    now = conv_sums.step(*now, *gate_sums.came())
    now = gate_sums.step(*now)
    now = conv_sums.step(*now)
    normed_grad = normed_sum.total(*now)
    now = conv_sums.step(*now, *gate_sums.came())
    grad_norm_one = jnp.sum(normed_grad * normed_one, axis=0)
    norm_grads = jnp.pad(jnp.stack([grad_norm_one, grad_norm_two]), ((0, 6), (0, 0)))
    (norm_grads,) = reorder([norm_grads], True, now)
    norm_sum = Summed(norm_grads[:2].reshape(-1, LANES), head_hops())
    norm_sum.step()
    norm_sum.step()
    input_grad = after_mix_grad + norm_backward(normed_grad * attn_gain, normed_one, scale_one)
    block_out = (after_mix + ffn_sum.total(*now)).astype(BF16)
    small_sum = Summed(jnp.concatenate([small, norm_sum.total()], axis=0), dp_hops())
    small_sum.step(*now)
    small_sum.step()
    block_out, input_grad = reorder([block_out, input_grad], True, now)
    block_out, input_grad = block_out.reshape(tokens.shape), input_grad.reshape(tokens.shape)
    shard_ffn = ffn_sums.total(*now)
    shard_gate = gate_sums.total(*now)
    shard_conv = conv_sums.total()
    small, norm_grads = small_sum.total()[: small.shape[0]], small_sum.total()[small.shape[0] :]
    norm_grads = norm_grads.reshape(2, model)

    across = jnp.stack([small, swap(small, "head", 2)])
    near = swap(across, "head", 1)
    small = jnp.stack([across[0], near[0], across[1], near[1]])
    small = jnp.stack([small[jnp.bitwise_xor(at, head_rank)] for at in range(ranks)])
    tap_rows = KCONV * conv_width // LANES
    taps_all = small[:, :tap_rows].reshape(ranks, KCONV, conv_width).transpose(1, 0, 2)

    def joined(low, high):
        return taps_all[:, :, low:high].reshape(KCONV, -1)

    rest = jnp.sum(small[:, tap_rows + 2 :], axis=0).reshape(-1)
    return (
        block_out,
        input_grad,
        norm_grads[0],
        shard_conv[:, :qk_width],
        shard_conv[:, qk_width : 2 * qk_width],
        shard_conv[:, 2 * qk_width : conv_width],
        shard_gate[:, :v_width],
        shard_conv[:, conv_width : conv_width + heads],
        shard_conv[:, conv_width + heads : conv_width + 2 * heads],
        joined(0, qk_width),
        joined(qk_width, 2 * qk_width),
        joined(2 * qk_width, conv_width),
        small[:, tap_rows, :heads].reshape(-1),
        small[:, tap_rows + 1, :heads].reshape(-1),
        rest[:value_size],
        shard_gate[:, v_width:].T,
        norm_grads[1],
        shard_ffn[:, :ffn_width],
        shard_ffn[:, ffn_width : 2 * ffn_width],
        shard_ffn[:, 2 * ffn_width :].T,
    )


def solution(mesh):
    rows, plane, turned, whole = P(None, ("dp", "head"), None), P("dp", "head"), P("head", "dp"), P()
    in_specs = (rows, rows, whole, whole) + (plane,) * 6 + (whole,) * 6
    in_specs += (turned, whole, plane, plane, turned)
    out_specs = (rows, rows, whole) + (plane,) * 6 + (whole,) * 6
    out_specs += (turned, whole, plane, plane, turned)
    return jax.shard_map(body, mesh=mesh, in_specs=in_specs, out_specs=out_specs, check_vma=False)
```
